32 devices in a mesh: exp: 8 (over z, y), seq: 4 (over x, core).
Axes of the slice: x: 2, y: 2, z: 4, core: 2. Of those that a mesh axis runs over, the one named last changes fastest.
Arguments:
- block_input: bfloat16 [2, 8, 512, 1536], P(None, 'exp', 'seq'), may hold values from -6 to 6
- norm_attn: bfloat16 [1536], P(('exp', 'seq')), may hold values from 0.5 to 1.5
- w_query: bfloat16 [1536, 1536], P(('exp', 'seq')), may hold values from -0.15625 to 0.15625
- w_key: bfloat16 [1536, 512], P(('exp', 'seq')), may hold values from -0.15625 to 0.15625
- w_value: bfloat16 [1536, 512], P(('exp', 'seq')), may hold values from -0.15625 to 0.15625
- w_out: bfloat16 [1536, 1536], P(('exp', 'seq')), may hold values from -1.75 to 1.75
- norm_ffn: bfloat16 [1536], P(('exp', 'seq')), may hold values from 0.5 to 1.5
- w_router: bfloat16 [1536, 16], P(('exp', 'seq')), may hold values from -0.078125 to 0.078125
- shared_gate: bfloat16 [1536, 1024], P(('exp', 'seq')), may hold values from -0.15625 to 0.15625
- shared_up: bfloat16 [1536, 1024], P(('exp', 'seq')), may hold values from -0.15625 to 0.15625
- shared_down: bfloat16 [1024, 1536], P(('exp', 'seq')), may hold values from -0.1875 to 0.1875
- expert_gate: bfloat16 [16, 1536, 512], P('exp', 'seq'), may hold values from -0.15625 to 0.15625
- expert_up: bfloat16 [16, 1536, 512], P('exp', 'seq'), may hold values from -0.15625 to 0.15625
- expert_down: bfloat16 [16, 512, 1536], P('exp', 'seq'), may hold values from -0.25 to 0.25
- routes: int32 [2, 8, 512, 6], P(None, 'exp', 'seq'), may hold values from 0 to 15, all different within a row; in each aligned block of 128 rows (0 to 127, 128 to 255, ..., all dimensions but the last counted through in order) at most 72 rows name the same one
- out_grad: bfloat16 [2, 8, 512, 1536], P(None, 'exp', 'seq'), may hold values from -6 to 6
Outputs:
- block_output: bfloat16 [2, 8, 512, 1536], P(None, 'exp', 'seq')
- input_grad: float32 [2, 8, 512, 1536], P(None, 'exp', 'seq')
- norm_attn_grad: float32 [1536], P(('exp', 'seq'))
- w_query_grad: float32 [1536, 1536], P(('exp', 'seq'))
- w_key_grad: float32 [1536, 512], P(('exp', 'seq'))
- w_value_grad: float32 [1536, 512], P(('exp', 'seq'))
- w_out_grad: float32 [1536, 1536], P(('exp', 'seq'))
- norm_ffn_grad: float32 [1536], P(('exp', 'seq'))
- w_router_grad: float32 [1536, 16], P(('exp', 'seq'))
- shared_gate_grad: float32 [1536, 1024], P(('exp', 'seq'))
- shared_up_grad: float32 [1536, 1024], P(('exp', 'seq'))
- shared_down_grad: float32 [1024, 1536], P(('exp', 'seq'))
- expert_gate_grad: float32 [16, 1536, 512], P('exp', 'seq')
- expert_up_grad: float32 [16, 1536, 512], P('exp', 'seq')
- expert_down_grad: float32 [16, 512, 1536], P('exp', 'seq')
The draws below stay inside these ranges and needn't reach their ends.
Inputs may be any that keep to these rules, and one draw needn't show every extreme that they name: `routes`: each row names 6 different experts. In the rows of one device and micro-batch (aligned blocks of 128 rows) no expert is named more than 72 times, and in some blocks one expert exactly 72 times.
All inputs are finite; a program needn't handle non-finite values.
Results may differ from the reference program's by a relative error of at most 0.015.
Values may be sent and summed in bfloat16 or wider, within the bound.
A program may use at most 320 MiB of HBM per device.

```python
import math
import jax
import jax.numpy as jnp
import numpy as np
from jax import lax

D = 1536
HEADS = 12
KV_HEADS = 4
HEAD_DIM = 128
EFF = 512
SHARED_FF = 1024
TOPK = 6
SEQ_TOK = 128
MB = 2
EXPERTS = 16
BATCH = 8
LEN = 512
CAP = 72
N_SEQ = 4


def shard_levels(key, dims, split, low, largest):
    def one(position, shards_of):
        heights = jax.random.uniform(jax.random.fold_in(jax.random.fold_in(key, 6), position), (shards_of,), jnp.float32, low / len(split), largest / len(split))
        return jnp.repeat(jnp.exp(heights), dims[position] // shards_of).reshape((-1,) + (1,) * (len(dims) - position - 1))

    gain = one(*split[0])
    for cut in split[1:]:
        gain = gain * one(*cut)
    return gain


def shared_out(key, own, number, rows, number_of, top, bound, slope):
    order = jax.random.permutation(key, number_of)
    heavy_load, ordinary = load_shares(number_of, rows * top, bound, slope, True), load_shares(number_of, rows * top, bound, slope, False)
    places = jnp.arange(number_of)

    def named(tallies, offset_by):
        used = int((tallies > 0).sum())
        fixed = max(1, used // 4)
        shifted = fixed + (places - fixed + offset_by * (used - fixed)) % max(1, number_of - fixed)
        return jnp.zeros((number_of,), jnp.int32).at[order[jnp.where(places < fixed, places, shifted)]].set(jnp.asarray(tallies, jnp.int32))

    tallies = jnp.where(number % 4 == 0, named(heavy_load, number // 4), named(ordinary, number - number // 4 - 1))
    mixed = jax.random.permutation(jax.random.fold_in(own, 3), number_of)
    source_of, taker = mixed[0:number_of // 2 * 2:2], mixed[1:number_of // 2 * 2:2]
    slack = jnp.minimum(tallies[source_of] - 1, bound - tallies[taker]) // 2
    slack = jnp.where((source_of == order[0]) | (taker == order[0]) | (tallies[taker] == 0), 0, jnp.maximum(slack, 0))
    shifted = jax.random.randint(jax.random.fold_in(own, 4), (number_of // 2,), 0, 1 << 20) % (slack + 1)
    tallies = tallies.at[source_of].add(-shifted).at[taker].add(shifted)
    labels = jnp.searchsorted(jnp.cumsum(tallies), jnp.arange(rows * top), side="right").astype(jnp.int32)
    grid = labels.reshape(top, rows).T
    grid = grid[jax.random.permutation(jax.random.fold_in(own, 1), rows)]
    offset_by = jax.random.randint(jax.random.fold_in(own, 2), (rows, 1), 0, top)
    return jnp.take_along_axis(grid, (jnp.arange(top)[None, :] + offset_by) % top, axis=1)


def load_shares(number_of, total, reach, slope, full):
    loads = [(1 << 20) // math.isqrt(grade ** slope) + 1 for grade in range(1, number_of + 1)]
    largest = reach if full else min(reach, max(-(-total // number_of), total * loads[0] // sum(loads)))
    least = 1 if total - largest >= number_of - 1 else 0
    given, spare = [largest] + [least] * (number_of - 1), total - largest - least * (number_of - 1)
    while spare > 0:
        movable = [i for i in range(1, number_of) if given[i] < largest] or [i for i in range(1, number_of) if given[i] < reach]
        mass, left = sum([loads[i] for i in movable]), spare
        for i in movable:
            addition = min(reach - given[i], max(1, left * loads[i] // mass), spare)
            given[i] = given[i] + addition
            spare = spare - addition
    return np.array(given)


def normal_values(key, extent, deviation, most, cuts=(), kind=jnp.bfloat16):
    gain = shard_levels(key, extent, cuts, -0.22, 0.18) if cuts else 1.0
    values = jax.random.normal(key, extent, jnp.float32) * deviation * gain
    return jnp.minimum(jnp.maximum(values, -most), most).astype(kind)


def setup_inputs(seed: int = 0) -> dict:
    streams_of = jax.random.split(jax.random.key(seed), 17)
    block_input = normal_values(streams_of[0], (MB, BATCH, LEN, D), 1.0, 6.0, ((1, 8), (2, 4)))
    norm_attn = jnp.clip(1.0 + 0.1 * jax.random.normal(streams_of[1], (D,), jnp.float32), 0.5, 1.5).astype(jnp.bfloat16)
    w_query = normal_values(streams_of[2], (D, HEADS * HEAD_DIM), D ** -0.5, 0.15625, ((0, 32),))
    w_key = normal_values(streams_of[3], (D, KV_HEADS * HEAD_DIM), D ** -0.5, 0.15625, ((0, 32),))
    w_value = normal_values(streams_of[4], (D, KV_HEADS * HEAD_DIM), D ** -0.5, 0.15625, ((0, 32),))
    w_out = normal_values(streams_of[5], (HEADS * HEAD_DIM, D), (max(1, 4 * HEADS * HEAD_DIM // LEN)) ** -0.5, 1.75, ((0, 32),))
    norm_ffn = jnp.clip(1.0 + 0.1 * jax.random.normal(streams_of[6], (D,), jnp.float32), 0.5, 1.5).astype(jnp.bfloat16)
    w_router = normal_values(streams_of[7], (D, EXPERTS), (0.5 * D ** -0.5), 0.078125, ((0, 32),))
    shared_gate = normal_values(streams_of[8], (D, SHARED_FF), D ** -0.5, 0.15625, ((0, 32),))
    shared_up = normal_values(streams_of[9], (D, SHARED_FF), D ** -0.5, 0.15625, ((0, 32),))
    shared_down = normal_values(streams_of[10], (SHARED_FF, D), SHARED_FF ** -0.5, 0.1875, ((0, 32),))
    expert_gate = normal_values(streams_of[11], (EXPERTS, D, EFF), D ** -0.5, 0.15625, ((0, 8), (1, 4)))
    expert_up = normal_values(streams_of[12], (EXPERTS, D, EFF), D ** -0.5, 0.15625, ((0, 8), (1, 4)))
    expert_down = normal_values(streams_of[13], (EXPERTS, EFF, D), EFF ** -0.5, 0.25, ((0, 8), (1, 4)))
    routes_keys = jax.random.split(jax.random.fold_in(streams_of[14], 1), MB * BATCH * LEN // SEQ_TOK)
    routes_turns = jax.random.permutation(jax.random.fold_in(streams_of[14], 3), MB * BATCH * LEN // SEQ_TOK)
    routes = jax.vmap(lambda own, number: shared_out(jax.random.fold_in(streams_of[14], 2), own, number, SEQ_TOK, EXPERTS, TOPK, CAP, 1))(routes_keys, routes_turns).reshape((MB, BATCH, LEN, TOPK))
    out_grad = normal_values(streams_of[15], (MB, BATCH, LEN, D), 1.0, 6.0, ((1, 8), (2, 4)))
    return {"block_input": block_input, "norm_attn": norm_attn, "w_query": w_query, "w_key": w_key, "w_value": w_value, "w_out": w_out, "norm_ffn": norm_ffn, "w_router": w_router, "shared_gate": shared_gate, "shared_up": shared_up, "shared_down": shared_down, "expert_gate": expert_gate, "expert_up": expert_up, "expert_down": expert_down, "routes": routes, "out_grad": out_grad}


@jax.custom_vjp
def low(v):
    return lax.optimization_barrier(v.astype(jnp.bfloat16)).astype(jnp.float32)

@jax.custom_vjp
def low_back(v):
    return v

def low_keep(v):
    return (low(v), None)

def low_pass(kept, grad):
    return (grad,)

def back_keep(v):
    return (v, None)

def back_low(kept, grad):
    return (low(grad),)
low.defvjp(low_keep, low_pass)
low_back.defvjp(back_keep, back_low)
NORM_EPSILON = 1e-05

def rms_norm(hidden, norm_gain):
    return hidden * lax.rsqrt(lax.optimization_barrier(jnp.mean(hidden * hidden, axis=-1, keepdims=True)) + NORM_EPSILON) * norm_gain

def product(left_side, right_side):
    return jnp.dot(left_side, right_side, precision=lax.Precision.HIGHEST)

def attention(queries, keys, values):
    seq_length = queries.shape[0]
    block_rows = math.gcd(seq_length, 512)
    score_scale = HEAD_DIM ** (-0.5)
    blocks = queries.reshape(seq_length // block_rows, block_rows, KV_HEADS, HEADS // KV_HEADS, HEAD_DIM)
    starts = jnp.arange(seq_length // block_rows, dtype=jnp.int32) * block_rows
    key_pos = jnp.arange(seq_length, dtype=jnp.int32)

    def one_block(pair):
        query_block, start_row = pair
        scores = jnp.einsum('qkgd,skd->kgqs', query_block, keys, precision=lax.Precision.HIGHEST) * score_scale
        scores = low_back(scores)
        query_pos = start_row + jnp.arange(block_rows, dtype=jnp.int32)
        causal = key_pos[None, :] <= query_pos[:, None]
        scores = jnp.where(causal, scores, -1e+30)
        highest = lax.optimization_barrier(jnp.max(scores, axis=-1, keepdims=True))
        exp_scores = jnp.exp(scores - highest)
        attn_probs = low(exp_scores / lax.optimization_barrier(jnp.sum(exp_scores, axis=-1, keepdims=True)))
        return jnp.einsum('kgqs,skd->qkgd', attn_probs, values, precision=lax.Precision.HIGHEST)
    mixed_rows = lax.map(jax.checkpoint(one_block), (blocks, starts))
    return mixed_rows.reshape(seq_length, HEADS * HEAD_DIM)

def slot_tables(route_rows):
    flat_routes = route_rows.reshape(N_SEQ, SEQ_TOK * TOPK)
    onehot = (flat_routes[:, :, None] == jnp.arange(EXPERTS, dtype=jnp.int32)[None, None, :]).astype(jnp.int32)
    before = jnp.cumsum(onehot, axis=1) - onehot
    slot_rank = lax.optimization_barrier(jnp.sum(before * onehot, axis=2))
    device_block = jnp.arange(N_SEQ, dtype=jnp.int32)[:, None]
    slot_place = ((flat_routes * N_SEQ + device_block) * CAP + slot_rank).reshape(-1).astype(jnp.int32)
    pair_ids = jnp.arange(LEN * TOPK, dtype=jnp.int32)
    slot_owner = jnp.zeros((EXPERTS * N_SEQ * CAP,), jnp.int32).at[slot_place].set(pair_ids // TOPK)
    filled = jnp.zeros((EXPERTS * N_SEQ * CAP,), jnp.int32).at[slot_place].set(1)
    return (slot_place, slot_owner, filled > 0)

def sequence(weights, hidden, route_rows):
    norm_attn, w_query, w_key, w_value, w_out, norm_ffn, w_router, shared_gate, shared_up, shared_down, expert_gate, expert_up, expert_down = weights
    normed_one = low(rms_norm(hidden, norm_attn))
    queries = low(low_back(product(normed_one, w_query)))
    keys = low(low_back(product(normed_one, w_key)))
    values = low(low_back(product(normed_one, w_value)))
    mixed = attention(queries, keys.reshape(LEN, KV_HEADS, HEAD_DIM), values.reshape(LEN, KV_HEADS, HEAD_DIM))
    attended = low(low_back(mixed))
    hidden_mid = hidden + low_back(product(attended, w_out))
    normed_two = low(rms_norm(hidden_mid, norm_ffn))
    logits = low_back(product(normed_two, w_router))
    gate_vals = jax.nn.softmax(jnp.take_along_axis(logits, route_rows, axis=1), axis=-1)
    shared_pre_gate = low_back(product(normed_two, shared_gate))
    shared_pre_up = low_back(product(normed_two, shared_up))
    shared_hidden = low(jax.nn.silu(shared_pre_gate) * shared_pre_up)
    shared_result = low_back(product(shared_hidden, shared_down))
    slot_place, slot_owner, filled = slot_tables(route_rows)
    expert_in = low_back(jnp.where(filled[:, None], normed_two[slot_owner], 0.0))
    expert_in = expert_in.reshape(EXPERTS, N_SEQ * CAP, D)
    pre_gate = low_back(jnp.einsum('erd,edf->erf', expert_in, expert_gate, precision=lax.Precision.HIGHEST))
    pre_up = low_back(jnp.einsum('erd,edf->erf', expert_in, expert_up, precision=lax.Precision.HIGHEST))
    activation = low(jax.nn.silu(pre_gate) * pre_up)
    expert_out = low(low_back(jnp.einsum('erf,efd->erd', activation, expert_down, precision=lax.Precision.HIGHEST)))
    picked = expert_out.reshape(EXPERTS * N_SEQ * CAP, D)[slot_place].reshape(LEN, TOPK, D)
    mixture = lax.optimization_barrier(jnp.sum(gate_vals[:, :, None] * picked, axis=1))
    return hidden_mid + shared_result + mixture

def reference(block_input, norm_attn, w_query, w_key, w_value, w_out, norm_ffn, w_router, shared_gate, shared_up, shared_down, expert_gate, expert_up, expert_down, routes, out_grad):
    params = (norm_attn.astype(jnp.float32), w_query.astype(jnp.float32), w_key.astype(jnp.float32), w_value.astype(jnp.float32), w_out.astype(jnp.float32), norm_ffn.astype(jnp.float32), w_router.astype(jnp.float32), shared_gate.astype(jnp.float32), shared_up.astype(jnp.float32), shared_down.astype(jnp.float32), expert_gate.astype(jnp.float32), expert_up.astype(jnp.float32), expert_down.astype(jnp.float32))
    route_seqs = routes.reshape(MB * BATCH, LEN, TOPK)

    def forward(inputs, *weights):

        def one_sequence(pair):
            return sequence(weights, pair[0], pair[1])
        seq_outputs = lax.map(jax.checkpoint(one_sequence), (inputs.reshape(MB * BATCH, LEN, D), route_seqs))
        return seq_outputs.reshape(MB, BATCH, LEN, D)
    result, pull = jax.vjp(forward, block_input.astype(jnp.float32), *params)
    grads = pull(out_grad.astype(jnp.float32))
    return (result.astype(jnp.bfloat16), grads[0], grads[1], grads[2], grads[3], grads[4], grads[5], grads[6], grads[7], grads[8], grads[9], grads[10], grads[11], grads[12], grads[13])
```

```python
import functools
import itertools
import math

import jax
import jax.numpy as jnp
from jax import lax
from jax.experimental import pallas as pl
from jax.experimental.pallas import tpu as pltpu
from jax.sharding import PartitionSpec as P

MESH = pl.DeviceIdType.MESH
CANON = "abxc"


class Grid:
    def __init__(self, exp_size, seq_size):
        self.size = {"a": exp_size // 2, "b": 2, "x": seq_size // 2, "c": 2}

    def here(self):
        e = lax.axis_index("exp")
        s = lax.axis_index("seq")
        return {"a": lax.div(e, 2), "b": lax.rem(e, 2), "x": lax.div(s, 2), "c": lax.rem(s, 2)}

    def device(self, pos):
        return (pos["a"] * 2 + pos["b"], pos["x"] * 2 + pos["c"])

    def index(self, pos, dims):
        number = 0
        for d in CANON:
            if d in dims:
                number = number * self.size[d] + pos[d]
        return number

    def count(self, dims):
        return math.prod(self.size[d] for d in dims)

    def offsets(self, d):
        n = self.size[d]
        return (0, 1) if n == 2 else tuple(range(-(n - 1), n))

    def move(self, pos, d, off):
        new = dict(pos)
        if off:
            new[d] = 1 - pos[d] if self.size[d] == 2 else pos[d] + off
        return new

    def valid(self, pos, d, off):
        if off == 0 or self.size[d] == 2:
            return None
        return pos[d] + off >= 0 if off < 0 else pos[d] + off < self.size[d]

    def steps(self, d):
        if self.size[d] == 1:
            return ()
        return (1,) if self.size[d] == 2 else (1, -1)


def both(*conds):
    conds = [c for c in conds if c is not None]
    return functools.reduce(jnp.logical_and, conds) if conds else None


def under(cond, body):
    if cond is None:
        body()
    else:
        pl.when(cond)(body)


def greet(grid, me, dims):
    bar = pltpu.get_barrier_semaphore()
    total = 0
    for d in dims:
        for step in grid.steps(d):
            ok = grid.valid(me, d, step)

            def signal(d=d, step=step):
                pl.semaphore_signal(
                    bar, inc=1, device_id=grid.device(grid.move(me, d, step)), device_id_type=MESH
                )

            under(ok, signal)
            total = total + (1 if ok is None else ok.astype(jnp.int32))
    pl.semaphore_wait(bar, total)


def remote(src, dst, ssem, rsem, device):
    return pltpu.make_async_remote_copy(
        src_ref=src, dst_ref=dst, send_sem=ssem, recv_sem=rsem, device_id=device, device_id_type=MESH
    )


def gather_plan(grid, orders):
    dims = orders[0]
    events = []
    for combo in itertools.product(*[grid.offsets(d) for d in dims]):
        off = dict(zip(dims, combo))
        sends = []
        for order in orders:
            last = max([k for k, d in enumerate(order) if off[d]], default=-1)
            mine = []
            if last >= 0 and grid.size[order[last]] > 2:
                mine.append((order[last], 1 if off[order[last]] < 0 else -1))
            for d in order[last + 1 :]:
                mine.extend((d, step) for step in grid.steps(d))
            sends.append(mine)
        events.append((sum(abs(v) for v in combo), off, sends))
    events.sort(key=lambda ev: ev[0])
    return events


def gather_kernel(grid, routes, *refs):
    count = len(routes)
    srcs, dsts = refs[:count], refs[count : 2 * count]
    ssem, rsem, lsem = refs[2 * count :]
    me = grid.here()
    used = "".join(d for d in CANON if any(d in orders[0] for orders in routes))
    greet(grid, me, used)
    merged = []
    for i, orders in enumerate(routes):
        for ev in gather_plan(grid, orders):
            merged.append((ev[0], i, ev[1], ev[2]))
    merged.sort(key=lambda ev: ev[0])
    base, total = [], 0
    for orders in routes:
        base.append(total)
        total += grid.count(orders[0])
    waits = []
    slot = 0
    for hops, i, off, sends in merged:
        dims = routes[i][0]
        pos = me
        conds = []
        for d in dims:
            conds.append(grid.valid(me, d, off[d]))
            pos = grid.move(pos, d, off[d])
        ok = both(*conds)
        idx = grid.index(pos, dims)
        sem = rsem.at[base[i] + idx]
        block = dsts[i].at[idx]
        src = srcs[i] if hops == 0 else block
        plan = []
        for d, step in sorted(set(sends[0]) | set(sends[1])):
            side = None
            if (d, step) not in sends[0]:
                side = me["c"] == 1
            elif (d, step) not in sends[1]:
                side = me["c"] == 0
            cp = remote(src, block, ssem.at[slot], sem, grid.device(grid.move(me, d, step)))
            plan.append((both(grid.valid(me, d, step), side), cp))
            slot += 1

        def arrive(hops=hops, i=i, block=block, sem=sem, plan=plan):
            if hops == 0:
                pltpu.make_async_copy(srcs[i], block, lsem.at[i]).start()
            else:
                remote(block, block, lsem.at[i], sem, grid.device(grid.move(me, used[-1], 1))).wait_recv()
            for cond, cp in plan:
                under(cond, cp.start)

        def finish(hops=hops, i=i, block=block, plan=plan):
            if hops == 0:
                pltpu.make_async_copy(srcs[i], block, lsem.at[i]).wait()
            for cond, cp in plan:
                under(cond, cp.wait_send)

        under(ok, arrive)
        waits.append((ok, finish))
    for ok, finish in waits:
        under(ok, finish)


def count_sends(grid, routes):
    return sum(
        len(set(ev[2][0]) | set(ev[2][1])) for orders in routes for ev in gather_plan(grid, orders)
    )


def gather(grid, arrays, routes, collective_id, name):
    total = sum(grid.count(orders[0]) for orders in routes)
    return pl.pallas_call(
        functools.partial(gather_kernel, grid, routes),
        out_shape=[
            jax.ShapeDtypeStruct((grid.count(orders[0]),) + x.shape, x.dtype)
            for x, orders in zip(arrays, routes)
        ],
        in_specs=[pl.BlockSpec(memory_space=pl.ANY)] * len(arrays),
        out_specs=[pl.BlockSpec(memory_space=pl.ANY)] * len(arrays),
        scratch_shapes=[
            pltpu.SemaphoreType.DMA((count_sends(grid, routes),)),
            pltpu.SemaphoreType.DMA((total,)),
            pltpu.SemaphoreType.DMA((len(arrays),)),
        ],
        compiler_params=pltpu.CompilerParams(collective_id=collective_id, has_side_effects=True),
        name=name,
    )(*arrays)


def scatter_plan(grid, order):
    lead = order[-1]
    span = grid.size[lead]
    events = []
    for stage, d in enumerate(order):
        rest = order[stage:]
        for combo in itertools.product(*[grid.offsets(r) for r in rest]):
            off = dict(zip(rest, combo))
            time = span - 1 - abs(off[lead]) + stage
            first = 0 if off[d] else 1
            events.append((time, stage, first, off))
    events.sort(key=lambda ev: ev[:3])
    return events


def inbox_shape(grid, order, stage):
    d = order[stage]
    n = grid.size[d]
    later = grid.count(order[stage + 1 :])
    return (1 if n == 2 else n + 1) * later


def scatter_kernel(grid, items, *refs):
    count = len(items)
    srcs, outs = refs[:count], refs[count : 2 * count]
    refs = refs[2 * count :]
    accs, inboxes = refs[:count], []
    refs = refs[count:]
    for item in items:
        inboxes.append(refs[: len(item[0])])
        refs = refs[len(item[0]) :]
    lsem, ssem, rsem = refs
    me = grid.here()
    used = "".join(d for d in CANON if any(d in item[0] for item in items))
    greet(grid, me, used)

    def blocks(i, order, stage):
        def of(off):
            pos = me
            for d in order[stage:]:
                pos = grid.move(pos, d, off[d])
            return pos

        return of

    for side in (0, 1):
        plans = []
        for i, item in enumerate(items):
            order = item[side]
            plans += [ev + (i,) for ev in scatter_plan(grid, order)]
        plans.sort(key=lambda ev: ev[:3])
        if all(item[0] == item[1] for item in items):
            if side == 0:
                run_scatter(grid, items, 0, plans, me, srcs, outs, accs, inboxes, lsem, ssem, rsem)
        else:

            def go(side=side, plans=plans):
                run_scatter(grid, items, side, plans, me, srcs, outs, accs, inboxes, lsem, ssem, rsem)

            pl.when(me["c"] == side)(go)


def scatter_bases(grid, items):
    block_base, send_base, inbox_base = [], [], []
    blocks = sends = slots = 0
    for item in items:
        block_base.append(blocks)
        blocks += grid.count(item[0])
        send_base.append(sends)
        sends += grid.count(item[0])
        stages = []
        for stage in range(len(item[0])):
            stages.append(slots)
            slots += max(inbox_shape(grid, item[0], stage), inbox_shape(grid, item[1], stage))
        inbox_base.append(stages)
    return block_base, send_base, inbox_base, (blocks, sends, slots)


def run_scatter(grid, items, side, plans, me, srcs, outs, accs, inboxes, lsem, ssem, rsem):
    block_base, send_base, inbox_base, _ = scatter_bases(grid, items)
    waits = []
    orders = [item[side] for item in items]

    def owner(order, stage, off):
        pos, conds = me, []
        for d in order[stage:]:
            conds.append(grid.valid(me, d, off[d]))
            pos = grid.move(pos, d, off[d])
        return pos, both(*conds)

    for time, stage, first, off, i in plans:
        order = orders[i]
        if stage != 0:
            continue
        pos, ok = owner(order, 0, off)
        idx = grid.index(pos, order)
        if off[order[0]] == 0 or grid.size[order[0]] > 2:
            under(ok, pltpu.make_async_copy(srcs[i].at[idx], accs[i].at[idx], lsem.at[block_base[i] + idx]).start)

    for time, stage, first, off, i in plans:
        order, step_rows = orders[i], items[i][2]
        d = order[stage]
        n = grid.size[d]
        pos, ok = owner(order, stage, off)
        idx = grid.index(pos, order)
        acc, inbox = accs[i], inboxes[i][stage]
        later = order[stage + 1 :]
        rows = acc.shape[1]

        def slot_of(line_slot, later=later, pos=pos, order=order, d=d, n=n):
            tail = grid.index(pos, later)
            return tail if n == 2 else line_slot * grid.count(later) + tail

        def box(line_slot, i=i, stage=stage, inbox=inbox, slot_of=slot_of):
            k = slot_of(line_slot)
            return inbox.at[k], rsem.at[inbox_base[i][stage] + k]

        def take(line_slot, box=box):
            ref, sem = box(line_slot)
            remote(ref, ref, ssem.at[0], sem, grid.device(grid.move(me, "c", 1))).wait_recv()
            return ref

        def add(ref, acc=acc, idx=idx, rows=rows, step_rows=step_rows):
            def body(r, carry):
                at = pl.ds(pl.multiple_of(r * step_rows, step_rows), step_rows)
                acc[idx, at, :] = (
                    acc[idx, at, :].astype(jnp.float32) + ref[at, :].astype(jnp.float32)
                ).astype(acc.dtype)
                return carry

            lax.fori_loop(0, rows // step_rows, body, 0)

        def load(i=i, idx=idx):
            pltpu.make_async_copy(srcs[i].at[idx], accs[i].at[idx], lsem.at[block_base[i] + idx]).wait()

        def send(src, to, line_slot, i=i, idx=idx, box=box, order=order):
            ref, sem = box(line_slot)
            return remote(src, ref, ssem.at[send_base[i] + idx], sem, grid.device(to))

        last = stage == len(order) - 1
        if n == 2:
            if off[d]:
                src = srcs[i].at[idx] if stage == 0 else acc.at[idx]
                cp = send(src, grid.move(me, d, 1), 0)
                under(ok, cp.start)
                waits.append((ok, cp))
            else:

                def merge(stage=stage, load=load, take=take, add=add, last=last, i=i, acc=acc, idx=idx, rows=rows, step_rows=step_rows):
                    if stage == 0:
                        load()
                    ref = take(0)
                    if last:
                        close(outs[i], acc, idx, [ref], rows, step_rows)
                    else:
                        add(ref)

                under(ok, merge)
            continue
        if off[d]:
            back = -1 if off[d] > 0 else 1
            ahead = -back
            has_back = grid.valid(me, d, back)
            nxt = me[d] + ahead
            to_slot = pos[d] if ahead > 0 else jnp.where(pos[d] == nxt, n, pos[d])
            cp = send(acc.at[idx], grid.move(me, d, ahead), to_slot)

            def pass_on(stage=stage, load=load, take=take, add=add, has_back=has_back, pos=pos, d=d, cp=cp):
                if stage == 0:
                    load()
                under(has_back, lambda: add(take(pos[d])))
                cp.start()

            under(ok, pass_on)
            waits.append((ok, cp))
        else:

            def gather_in(stage=stage, load=load, take=take, add=add, last=last, i=i, acc=acc, idx=idx, d=d, n=n, rows=rows, step_rows=step_rows):
                if stage == 0:
                    load()
                low, high = grid.valid(me, d, -1), grid.valid(me, d, 1)
                if not last:
                    pl.when(low)(lambda: add(take(me[d])))
                    pl.when(high)(lambda: add(take(n)))
                    return

                def middle():
                    close(outs[i], acc, idx, [take(me[d]), take(n)], rows, step_rows)

                def bottom():
                    close(outs[i], acc, idx, [take(n)], rows, step_rows)

                def top():
                    close(outs[i], acc, idx, [take(me[d])], rows, step_rows)

                pl.when(jnp.logical_and(low, high))(middle)
                pl.when(me[d] == 0)(bottom)
                pl.when(me[d] == n - 1)(top)

            under(ok, gather_in)
    for ok, cp in waits:
        under(ok, cp.wait_send)


def close(out, acc, idx, parts, rows, step_rows):
    def body(r, carry):
        at = pl.ds(pl.multiple_of(r * step_rows, step_rows), step_rows)
        total = acc[idx, at, :].astype(jnp.float32)
        for part in parts:
            total = total + part[at, :].astype(jnp.float32)
        out[at, :] = total.astype(out.dtype)
        return carry

    lax.fori_loop(0, rows // step_rows, body, 0)


def scatter(grid, arrays, orders, out_types, collective_id, name):
    items = [(o[0], o[1], min(16, x.shape[1])) for x, o in zip(arrays, orders)]
    _, _, _, (blocks, sends, slots) = scatter_bases(grid, items)
    scratch = [pltpu.VMEM(x.shape, x.dtype) for x in arrays]
    block_bytes = [-(-x.shape[1] // 16) * 16 * x.shape[2] * x.dtype.itemsize for x in arrays]
    used = sum(x.shape[0] * b for x, b in zip(arrays, block_bytes))
    used += sum(2 * 4 * b // x.dtype.itemsize for x, b in zip(arrays, block_bytes))
    for x, item, size in zip(arrays, items, block_bytes):
        for stage in range(len(item[0])):
            k = max(inbox_shape(grid, item[0], stage), inbox_shape(grid, item[1], stage))
            scratch.append(pltpu.VMEM((k,) + x.shape[1:], x.dtype))
            used += k * size
    scratch += [
        pltpu.SemaphoreType.DMA((blocks,)),
        pltpu.SemaphoreType.DMA((sends,)),
        pltpu.SemaphoreType.DMA((slots,)),
    ]
    return pl.pallas_call(
        functools.partial(scatter_kernel, grid, items),
        out_shape=[jax.ShapeDtypeStruct(x.shape[1:], t) for x, t in zip(arrays, out_types)],
        in_specs=[pl.BlockSpec(memory_space=pl.ANY)] * len(arrays),
        out_specs=[pl.BlockSpec(memory_space=pltpu.VMEM)] * len(arrays),
        scratch_shapes=scratch,
        compiler_params=pltpu.CompilerParams(
            collective_id=collective_id, has_side_effects=True, vmem_limit_bytes=used + (4 << 20)
        ),
        name=name,
    )(*arrays)


HEADS = 12
KV_HEADS = 4
HEAD_DIM = 128
TOPK = 6
NORM_EPSILON = 1e-05
GROUP = HEADS // KV_HEADS
BF = jnp.bfloat16
F32 = jnp.float32


def matmul(left, right):
    return jnp.dot(left, right, preferred_element_type=F32)


def left_product(left, right):
    return jnp.einsum("sa,sb->ab", left, right, preferred_element_type=F32)


def right_product(left, right):
    return jnp.einsum("sb,ab->sa", left, right, preferred_element_type=F32)


def inverse_rms(hidden):
    return lax.rsqrt(jnp.mean(hidden * hidden, axis=-1, keepdims=True) + NORM_EPSILON)


def norm_back(grad, hidden, inverse, gain):
    scaled = grad * gain
    inner = jnp.mean(scaled * hidden, axis=-1, keepdims=True)
    gain_grad = jnp.sum(grad * (hidden * inverse), axis=0)
    return inverse * scaled - hidden * (inverse * inverse * inverse) * inner, gain_grad


def silu_parts(pre):
    sigmoid = jax.nn.sigmoid(pre)
    return pre * sigmoid, sigmoid * (1.0 + pre * (1.0 - sigmoid))


def stacked(ref):
    return jnp.concatenate(
        [ref[0, :, g * HEAD_DIM : (g + 1) * HEAD_DIM] for g in range(GROUP)], axis=0
    )


def unstacked(ref, value):
    rows = ref.shape[1]
    for g in range(GROUP):
        ref[0, :, g * HEAD_DIM : (g + 1) * HEAD_DIM] = value[g * rows : (g + 1) * rows].astype(
            ref.dtype
        )


def masked_scores(first, query, key, rows):
    scores = lax.dot_general(
        query, key, (((1,), (1,)), ((), ())), preferred_element_type=F32
    ) * (HEAD_DIM**-0.5)
    place = first + lax.rem(lax.broadcasted_iota(jnp.int32, scores.shape, 0), rows)
    seen = lax.broadcasted_iota(jnp.int32, scores.shape, 1) <= place
    return jnp.where(seen, scores, -1e30)


def attend_kernel(first_ref, query_ref, key_ref, value_ref, out_ref):
    rows = query_ref.shape[1]
    length = key_ref.shape[0] * rows
    query = stacked(query_ref)
    key = key_ref[...].reshape(length, HEAD_DIM)
    value = value_ref[...].reshape(length, HEAD_DIM)
    scores = masked_scores(first_ref[0], query, key, rows)
    weights = jnp.exp(scores - jnp.max(scores, axis=-1, keepdims=True))
    probs = (weights / jnp.sum(weights, axis=-1, keepdims=True)).astype(BF)
    unstacked(out_ref, jnp.dot(probs, value, preferred_element_type=F32))


def attend_back_kernel(
    first_ref, query_ref, key_ref, value_ref, grad_ref, query_out, key_out, value_out
):
    rows = query_ref.shape[1]
    length = key_ref.shape[0] * rows
    scale = HEAD_DIM**-0.5
    query, grad = stacked(query_ref), stacked(grad_ref)
    key = key_ref[...].reshape(length, HEAD_DIM)
    value = value_ref[...].reshape(length, HEAD_DIM)
    scores = masked_scores(first_ref[0], query, key, rows)
    weights = jnp.exp(scores - jnp.max(scores, axis=-1, keepdims=True))
    probs = weights / jnp.sum(weights, axis=-1, keepdims=True)
    prob_grad = lax.dot_general(
        grad, value, (((1,), (1,)), ((), ())), preferred_element_type=F32
    )
    delta = jnp.sum(probs * prob_grad, axis=-1, keepdims=True)
    score_grad = (probs * (prob_grad - delta)).astype(BF)
    unstacked(query_out, jnp.dot(score_grad, key, preferred_element_type=F32) * scale)
    down = (((0,), (0,)), ((), ()))
    key_grad = lax.dot_general(score_grad, query, down, preferred_element_type=F32) * scale
    value_grad = lax.dot_general(probs.astype(BF), grad, down, preferred_element_type=F32)
    key_out[...] = key_grad.astype(BF).reshape(key_out.shape)
    value_out[...] = value_grad.astype(BF).reshape(value_out.shape)


def attention_specs(places, rows):
    query = pl.BlockSpec((1, rows, GROUP * HEAD_DIM), lambda m, h: (m, 0, h))
    key = pl.BlockSpec((places, 1, rows, HEAD_DIM), lambda m, h: (0, m, 0, h))
    value = pl.BlockSpec((places, 1, rows, HEAD_DIM), lambda m, h: (0, m, 0, KV_HEADS + h))
    return pl.BlockSpec(memory_space=pltpu.SMEM), query, key, value


def attend(first, qkv, kv_all):
    micro, rows, _ = qkv.shape
    scalar, query, key, value = attention_specs(kv_all.shape[0], rows)
    return pl.pallas_call(
        attend_kernel,
        grid=(micro, KV_HEADS),
        out_shape=jax.ShapeDtypeStruct((micro, rows, HEADS * HEAD_DIM), BF),
        in_specs=[scalar, query, key, value],
        out_specs=query,
        compiler_params=pltpu.CompilerParams(vmem_limit_bytes=40 << 20),
        name="attend",
    )(first, qkv, kv_all, kv_all)


def attend_back(first, qkv, kv_all, grad):
    micro, rows, _ = qkv.shape
    scalar, query, key, value = attention_specs(kv_all.shape[0], rows)
    kv_out = jax.ShapeDtypeStruct((kv_all.shape[0], micro, rows, KV_HEADS * HEAD_DIM), BF)
    return pl.pallas_call(
        attend_back_kernel,
        grid=(micro, KV_HEADS),
        out_shape=[jax.ShapeDtypeStruct((micro, rows, HEADS * HEAD_DIM), BF), kv_out, kv_out],
        in_specs=[scalar, query, key, value, query],
        out_specs=[query, key, key],
        compiler_params=pltpu.CompilerParams(vmem_limit_bytes=56 << 20),
        name="attend_back",
    )(first, qkv, kv_all, kv_all, grad)


def expert_step(inputs, grads, pick, gate, w_gate, w_up, w_down):
    groups, slots, _ = pick.shape
    width = inputs.shape[-1]
    taken = jnp.einsum("nkt,ntd->nkd", pick, inputs, preferred_element_type=F32)
    taken = taken.astype(BF).reshape(groups * slots, width)
    top = jnp.einsum("nkt,ntd->nkd", pick, grads, preferred_element_type=F32)
    top = top.reshape(groups * slots, width)
    gain = jnp.sum(pick.astype(F32) * gate[:, None, :], axis=-1).reshape(groups * slots, 1)
    pre_gate, pre_up = matmul(taken, w_gate), matmul(taken, w_up)
    silu, slope = silu_parts(pre_gate)
    hidden = (silu * pre_up).astype(BF)
    result = matmul(hidden, w_down).astype(BF).astype(F32)
    scaled = (gain * result).astype(BF).reshape(groups, slots, width)
    mixed = jnp.einsum("nkt,nkd->ntd", pick, scaled, preferred_element_type=F32)
    gate_grad = jnp.sum(top * result, axis=-1).reshape(groups, slots, 1)
    gate_grad = jnp.sum(pick.astype(F32) * gate_grad, axis=1)
    out_grad = (gain * top).astype(BF)
    hidden_grad = right_product(out_grad, w_down)
    gate_in = (hidden_grad * pre_up * slope).astype(BF)
    up_in = (hidden_grad * silu).astype(BF)
    back = (right_product(gate_in, w_gate) + right_product(up_in, w_up)).astype(BF)
    back = jnp.einsum(
        "nkt,nkd->ntd", pick, back.reshape(groups, slots, width), preferred_element_type=F32
    )
    terms = (
        left_product(taken, gate_in).astype(BF),
        left_product(taken, up_in).astype(BF),
        left_product(hidden, out_grad).astype(BF),
    )
    return mixed, back, gate_grad, terms


def per_device(
    block_input,
    norm_attn,
    w_query,
    w_key,
    w_value,
    w_out,
    norm_ffn,
    w_router,
    shared_gate,
    shared_up,
    shared_down,
    expert_gate,
    expert_up,
    expert_down,
    routes,
    out_grad,
):
    micro, _, rows, width = block_input.shape
    tokens = micro * rows
    experts = w_router.shape[1]
    held = expert_gate.shape[0]
    exp_size, seq_size = lax.axis_size("exp"), lax.axis_size("seq")
    blocks = exp_size * seq_size
    grid = Grid(exp_size, seq_size)
    slots = min(rows, 8 * ((3 * rows * TOPK // (2 * experts) + 7) // 8))
    query_width = HEADS * HEAD_DIM
    kv_width = KV_HEADS * HEAD_DIM
    qkv_width = query_width + 2 * kv_width
    own_rows = w_query.shape[0]
    shared_part = shared_gate.shape[1] // exp_size
    first_held = lax.axis_index("exp") * held
    first = (lax.axis_index("seq") * rows).astype(jnp.int32).reshape(1)

    small = jnp.concatenate([norm_attn[:, None], norm_ffn[:, None], w_router], axis=1)
    small = jnp.pad(small, ((0, 0), (0, 128 - small.shape[1])))
    route = ("abxc", "axbc" if seq_size == 4 else "abxc")
    qkv_full, out_full, small_full = gather(
        grid,
        [jnp.concatenate([w_query, w_key, w_value], axis=1), w_out, small],
        [route] * 3,
        1,
        "gather_dense",
    )
    qkv_full = qkv_full.reshape(width, qkv_width)
    out_full = out_full.reshape(query_width, width)
    small_full = small_full.reshape(width, 128)
    gain_one = small_full[:, 0].astype(F32)
    gain_two = small_full[:, 1].astype(F32)
    router_full = small_full[:, 2 : 2 + experts]

    grads_all = lax.all_gather(out_grad.reshape(tokens, width), "exp", axis=0)
    gate_full = lax.all_gather(expert_gate, "seq", axis=1, tiled=True)
    up_full = lax.all_gather(expert_up, "seq", axis=1, tiled=True)
    down_full = lax.all_gather(expert_down, "seq", axis=1, tiled=True)
    halves = jnp.concatenate(
        [
            shared_gate.reshape(own_rows, exp_size, shared_part),
            shared_up.reshape(own_rows, exp_size, shared_part),
        ],
        axis=2,
    ).transpose(1, 0, 2)
    halves = lax.all_to_all(halves, "exp", split_axis=0, concat_axis=0, tiled=True)
    shared_in = lax.all_gather(halves, "seq", axis=1).reshape(width, 2 * shared_part)
    shared_out = lax.all_gather(shared_down, "seq", axis=0, tiled=True)

    hidden_in = block_input.reshape(tokens, width).astype(F32)
    inverse_one = inverse_rms(hidden_in)
    normed_one = (hidden_in * inverse_one * gain_one).astype(BF)
    qkv = matmul(normed_one, qkv_full).astype(BF)
    (kv_all,) = gather(grid, [qkv[:, query_width:]], [("xc", "xc")], 2, "gather_kv")
    kv_all = kv_all.reshape(seq_size, micro, rows, 2 * kv_width)
    qkv = qkv.reshape(micro, rows, qkv_width)
    attended = attend(first, qkv, kv_all).reshape(tokens, query_width)
    hidden_mid = hidden_in + matmul(attended, out_full)
    inverse_two = inverse_rms(hidden_mid)
    normed_two = (hidden_mid * inverse_two * gain_two).astype(BF)

    route_rows = routes.reshape(tokens, TOPK)
    named = route_rows[:, :, None] == jnp.arange(experts, dtype=jnp.int32)
    chosen = jnp.any(named, axis=1)
    logits = matmul(normed_two, router_full)
    masked = jnp.where(chosen, logits, -jnp.inf)
    powers = jnp.exp(masked - jnp.max(masked, axis=-1, keepdims=True))
    gates = powers / jnp.sum(powers, axis=-1, keepdims=True)
    member = chosen.reshape(micro, rows, experts).astype(jnp.int32)
    rank = jnp.cumsum(member, axis=1) - member
    slot = jnp.where(member > 0, rank, -1).astype(F32)

    def by_expert(table):
        return table.reshape(micro, rows, experts).transpose(0, 2, 1).reshape(micro * experts, rows)

    inputs_all, gates_all, slot_all = gather(
        grid,
        [normed_two, by_expert(gates), by_expert(slot)],
        [("ab", "ab")] * 3,
        3,
        "gather_tokens",
    )
    groups = exp_size * micro
    inputs = inputs_all.reshape(groups, rows, width)
    tops = grads_all.reshape(groups, rows, width)

    def held_rows(table):
        table = table.reshape(groups, experts, rows)
        return lax.dynamic_slice_in_dim(table, first_held, held, 1)

    held_gates, held_slots = held_rows(gates_all), held_rows(slot_all)
    counter = jnp.arange(slots, dtype=F32)[None, :, None]

    flat, flat_top = inputs.reshape(groups * rows, width), tops.reshape(groups * rows, width)
    pre = matmul(flat, shared_in)
    silu, slope = silu_parts(pre[:, :shared_part])
    pre_up = pre[:, shared_part:]
    hidden = (silu * pre_up).astype(BF)
    mixed = matmul(hidden, shared_out)
    mid_grad = right_product(flat_top, shared_out)
    pre_grad = jnp.concatenate(
        [(mid_grad * pre_up * slope).astype(BF), (mid_grad * silu).astype(BF)], axis=1
    )
    back = right_product(pre_grad, shared_in)
    shared_in_term = left_product(flat, pre_grad).astype(BF)
    shared_out_term = left_product(hidden, flat_top).astype(BF)
    mixed = mixed.reshape(groups, rows, width)
    back = back.reshape(groups, rows, width)

    terms, gate_grads = [], []
    for k in range(held):
        pick = (counter == held_slots[:, k][:, None, :]).astype(BF)
        mixed_k, back_k, gate_grad_k, terms_k = expert_step(
            inputs, tops, pick, held_gates[:, k], gate_full[k], up_full[k], down_full[k]
        )
        mixed, back = mixed + mixed_k, back + back_k
        gate_grads.append(gate_grad_k)
        terms.append(terms_k)
    gate_table = lax.dynamic_update_slice_in_dim(
        jnp.zeros((groups, experts, rows), F32), jnp.stack(gate_grads, axis=1), first_held, 1
    )
    mixture, token_grad, gate_grad = scatter(
        grid,
        [
            mixed.astype(BF).reshape(exp_size, tokens, width),
            back.astype(BF).reshape(exp_size, tokens, width),
            gate_table.reshape(exp_size, micro * experts, rows),
        ],
        [("ba", "ba")] * 3,
        [F32] * 3,
        4,
        "scatter_tokens",
    )
    shares = [
        lax.psum_scatter(
            jnp.stack([terms[k][i] for k in range(held)]), "seq", scatter_dimension=1, tiled=True
        ).astype(F32)
        for i in range(3)
    ]
    shared_down_grad = lax.psum_scatter(
        shared_out_term, "seq", scatter_dimension=0, tiled=True
    ).astype(F32)
    halves = lax.psum_scatter(
        shared_in_term.reshape(exp_size, seq_size, own_rows, 2 * shared_part),
        "seq",
        scatter_dimension=1,
    )
    halves = lax.all_to_all(halves, "exp", split_axis=0, concat_axis=0, tiled=True).astype(F32)
    halves = halves.transpose(1, 0, 2)
    shared_gate_grad = halves[:, :, :shared_part].reshape(own_rows, exp_size * shared_part)
    shared_up_grad = halves[:, :, shared_part:].reshape(own_rows, exp_size * shared_part)

    block_output = (hidden_mid + mixture).astype(BF).reshape(block_input.shape)

    gate_grad = gate_grad.reshape(micro, experts, rows).transpose(0, 2, 1).reshape(tokens, experts)
    logit_grad = gates * (gate_grad - jnp.sum(gates * gate_grad, axis=-1, keepdims=True))
    logit_grad = logit_grad.astype(BF)
    grad_top = out_grad.reshape(tokens, width).astype(F32)
    normed_two_grad = token_grad + right_product(logit_grad, router_full)
    mid_part, norm_two_term = norm_back(normed_two_grad, hidden_mid, inverse_two, gain_two)
    mid_grad = mid_part + grad_top
    attn_grad = mid_grad.astype(BF)
    attended_grad = right_product(attn_grad, out_full).astype(BF)
    query_grad, key_part, value_part = attend_back(
        first, qkv, kv_all, attended_grad.reshape(micro, rows, query_width)
    )
    key_grad, value_grad = scatter(
        grid,
        [
            key_part.reshape(seq_size, tokens, kv_width),
            value_part.reshape(seq_size, tokens, kv_width),
        ],
        [("cx", "cx")] * 2,
        [BF] * 2,
        5,
        "scatter_kv",
    )
    qkv_grad = jnp.concatenate(
        [query_grad.reshape(tokens, query_width), key_grad, value_grad], axis=1
    )
    normed_one_grad = right_product(qkv_grad, qkv_full)
    in_part, norm_one_term = norm_back(normed_one_grad, hidden_in, inverse_one, gain_one)
    input_grad = (in_part + mid_grad).reshape(block_input.shape)
    small_term = jnp.concatenate(
        [norm_one_term[:, None], norm_two_term[:, None], left_product(normed_two, logit_grad)],
        axis=1,
    )
    small_term = jnp.pad(small_term, ((0, 0), (0, 128 - small_term.shape[1])))
    order = ("cxba", "cbxa" if seq_size == 4 else "cxba")
    qkv_share, out_share, small_share = scatter(
        grid,
        [
            left_product(normed_one, qkv_grad).astype(BF).reshape(blocks, own_rows, qkv_width),
            left_product(attended, attn_grad).astype(BF).reshape(blocks, own_rows, width),
            small_term.reshape(blocks, own_rows, 128),
        ],
        [order] * 3,
        [F32] * 3,
        6,
        "scatter_dense",
    )
    return (
        block_output,
        input_grad,
        small_share[:, 0],
        qkv_share[:, :query_width],
        qkv_share[:, query_width : query_width + kv_width],
        qkv_share[:, query_width + kv_width :],
        out_share,
        small_share[:, 1],
        small_share[:, 2 : 2 + experts],
        shared_gate_grad,
        shared_up_grad,
        shared_down_grad,
        shares[0],
        shares[1],
        shares[2],
    )


def solution(mesh):
    tokens = P(None, "exp", "seq", None)
    vector, matrix = P(("exp", "seq")), P(("exp", "seq"), None)
    stack = P("exp", "seq", None)
    weights = (vector,) + (matrix,) * 4 + (vector,) + (matrix,) * 4 + (stack,) * 3
    return jax.shard_map(
        per_device,
        mesh=mesh,
        in_specs=(tokens,) + weights + (tokens, tokens),
        out_specs=(tokens, tokens) + weights,
        check_vma=False,
    )
```

```python
import functools
import itertools
import math

import jax
import jax.numpy as jnp
from jax import lax
from jax.experimental import pallas as pl
from jax.experimental.pallas import tpu as pltpu
from jax.sharding import PartitionSpec as P

MESH = pl.DeviceIdType.MESH
CANON = "abxc"


class Grid:
    def __init__(self, exp_size, seq_size):
        self.size = {"a": exp_size // 2, "b": 2, "x": seq_size // 2, "c": 2}

    def here(self):
        e = lax.axis_index("exp")
        s = lax.axis_index("seq")
        return {"a": lax.div(e, 2), "b": lax.rem(e, 2), "x": lax.div(s, 2), "c": lax.rem(s, 2)}

    def device(self, pos):
        return (pos["a"] * 2 + pos["b"], pos["x"] * 2 + pos["c"])

    def index(self, pos, dims):
        number = 0
        for d in CANON:
            if d in dims:
                number = number * self.size[d] + pos[d]
        return number

    def count(self, dims):
        return math.prod(self.size[d] for d in dims)

    def offsets(self, d):
        n = self.size[d]
        return (0, 1) if n == 2 else tuple(range(-(n - 1), n))

    def move(self, pos, d, off):
        new = dict(pos)
        if off:
            new[d] = 1 - pos[d] if self.size[d] == 2 else pos[d] + off
        return new

    def valid(self, pos, d, off):
        if off == 0 or self.size[d] == 2:
            return None
        return pos[d] + off >= 0 if off < 0 else pos[d] + off < self.size[d]

    def steps(self, d):
        if self.size[d] == 1:
            return ()
        return (1,) if self.size[d] == 2 else (1, -1)


def both(*conds):
    conds = [c for c in conds if c is not None]
    return functools.reduce(jnp.logical_and, conds) if conds else None


def under(cond, body):
    if cond is None:
        body()
    else:
        pl.when(cond)(body)


def greet(grid, me, dims):
    bar = pltpu.get_barrier_semaphore()
    total = 0
    for d in dims:
        for step in grid.steps(d):
            ok = grid.valid(me, d, step)

            def signal(d=d, step=step):
                pl.semaphore_signal(
                    bar, inc=1, device_id=grid.device(grid.move(me, d, step)), device_id_type=MESH
                )

            under(ok, signal)
            total = total + (1 if ok is None else ok.astype(jnp.int32))
    pl.semaphore_wait(bar, total)


def remote(src, dst, ssem, rsem, device):
    return pltpu.make_async_remote_copy(
        src_ref=src, dst_ref=dst, send_sem=ssem, recv_sem=rsem, device_id=device, device_id_type=MESH
    )


def gather_plan(grid, orders):
    dims = orders[0]
    events = []
    for combo in itertools.product(*[grid.offsets(d) for d in dims]):
        off = dict(zip(dims, combo))
        sends = []
        for order in orders:
            last = max([k for k, d in enumerate(order) if off[d]], default=-1)
            mine = []
            if last >= 0 and grid.size[order[last]] > 2:
                mine.append((order[last], 1 if off[order[last]] < 0 else -1))
            for d in order[last + 1 :]:
                mine.extend((d, step) for step in grid.steps(d))
            sends.append(mine)
        events.append((sum(abs(v) for v in combo), off, sends))
    events.sort(key=lambda ev: ev[0])
    return events


def gather_kernel(grid, routes, *refs):
    count = len(routes)
    srcs, dsts = refs[:count], refs[count : 2 * count]
    ssem, rsem, lsem = refs[2 * count :]
    me = grid.here()
    used = "".join(d for d in CANON if any(d in orders[0] for orders in routes))
    greet(grid, me, used)
    merged = []
    for i, orders in enumerate(routes):
        for ev in gather_plan(grid, orders):
            merged.append((ev[0], i, ev[1], ev[2]))
    merged.sort(key=lambda ev: ev[0])
    base, total = [], 0
    for orders in routes:
        base.append(total)
        total += grid.count(orders[0])
    waits = []
    slot = 0
    for hops, i, off, sends in merged:
        dims = routes[i][0]
        pos = me
        conds = []
        for d in dims:
            conds.append(grid.valid(me, d, off[d]))
            pos = grid.move(pos, d, off[d])
        ok = both(*conds)
        idx = grid.index(pos, dims)
        sem = rsem.at[base[i] + idx]
        block = dsts[i].at[idx]
        src = srcs[i] if hops == 0 else block
        plan = []
        for d, step in sorted(set(sends[0]) | set(sends[1])):
            side = None
            if (d, step) not in sends[0]:
                side = me["c"] == 1
            elif (d, step) not in sends[1]:
                side = me["c"] == 0
            cp = remote(src, block, ssem.at[slot], sem, grid.device(grid.move(me, d, step)))
            plan.append((both(grid.valid(me, d, step), side), cp))
            slot += 1

        def arrive(hops=hops, i=i, block=block, sem=sem, plan=plan):
            if hops == 0:
                pltpu.make_async_copy(srcs[i], block, lsem.at[i]).start()
            else:
                remote(block, block, lsem.at[i], sem, grid.device(grid.move(me, used[-1], 1))).wait_recv()
            for cond, cp in plan:
                under(cond, cp.start)

        def finish(hops=hops, i=i, block=block, plan=plan):
            if hops == 0:
                pltpu.make_async_copy(srcs[i], block, lsem.at[i]).wait()
            for cond, cp in plan:
                under(cond, cp.wait_send)

        under(ok, arrive)
        waits.append((ok, finish))
    for ok, finish in waits:
        under(ok, finish)


def count_sends(grid, routes):
    return sum(
        len(set(ev[2][0]) | set(ev[2][1])) for orders in routes for ev in gather_plan(grid, orders)
    )


def gather(grid, arrays, routes, collective_id, name):
    total = sum(grid.count(orders[0]) for orders in routes)
    return pl.pallas_call(
        functools.partial(gather_kernel, grid, routes),
        out_shape=[
            jax.ShapeDtypeStruct((grid.count(orders[0]),) + x.shape, x.dtype)
            for x, orders in zip(arrays, routes)
        ],
        in_specs=[pl.BlockSpec(memory_space=pl.ANY)] * len(arrays),
        out_specs=[pl.BlockSpec(memory_space=pl.ANY)] * len(arrays),
        scratch_shapes=[
            pltpu.SemaphoreType.DMA((count_sends(grid, routes),)),
            pltpu.SemaphoreType.DMA((total,)),
            pltpu.SemaphoreType.DMA((len(arrays),)),
        ],
        compiler_params=pltpu.CompilerParams(collective_id=collective_id, has_side_effects=True),
        name=name,
    )(*arrays)


class Part:
    def __init__(self, orders, blocks, rows, columns, dtype, source, outputs, row=0, ready=None):
        self.orders, self.blocks, self.rows, self.columns = orders, blocks, rows, columns
        self.dtype, self.source, self.outputs, self.row, self.ready = dtype, source, outputs, row, ready
        self.step = min(16, rows)

    def size(self):
        return -(-self.rows // 16) * 16 * self.columns * jnp.dtype(self.dtype).itemsize

    def kept(self, grid):
        half = self.source is not None and grid.size[self.orders[0][0]] == 2
        return self.blocks // 2 if half else self.blocks

    def place(self, grid, pos, order):
        half = self.source is not None and grid.size[order[0]] == 2
        return grid.index(pos, order[1:] if half else order)

    def inbox(self, grid, stage):
        return max(
            (1 if grid.size[o[stage]] == 2 else grid.size[o[stage]] + 1) * grid.count(o[stage + 1 :])
            for o in self.orders
        )


def scatter_plan(grid, part, order):
    lead = order[-1]
    span = grid.size[lead]
    events = []
    for stage, d in enumerate(order):
        rest = order[stage:]
        for combo in itertools.product(*[grid.offsets(r) for r in rest]):
            off = dict(zip(rest, combo))
            time = span - 1 - abs(off[lead]) + stage - (1.5 if d == "c" else 0)
            first = 0 if off[d] else 1
            if part.ready is not None:
                time = part.ready[2 * min(stage, 1) + first]
            elif stage == 0 and grid.size[d] == 2 and off[d]:
                time -= 100
            events.append((time, -stage, first, off))
    events.sort(key=lambda ev: ev[:3])
    return events


class Scatter:
    def __init__(self, grid, parts):
        self.grid, self.parts = grid, parts
        self.base, blocks, sends, slots = [], 0, 0, 0
        for part in parts:
            stages = []
            for stage in range(len(part.orders[0])):
                stages.append(slots)
                slots += part.inbox(grid, stage)
            self.base.append((blocks, sends, stages))
            blocks += part.kept(grid)
            sends += part.blocks
        self.totals = (blocks, sends, slots)

    def scratch(self):
        dma = pltpu.SemaphoreType.DMA
        out = [pltpu.VMEM((p.kept(self.grid), p.rows, p.columns), p.dtype) for p in self.parts]
        for p in self.parts:
            for stage in range(len(p.orders[0])):
                out.append(pltpu.VMEM((p.inbox(self.grid, stage), p.rows, p.columns), p.dtype))
        return out + [dma((n,)) for n in self.totals]

    def bytes(self):
        return sum(
            p.size() * (p.kept(self.grid) + sum(p.inbox(self.grid, k) for k in range(len(p.orders[0]))))
            for p in self.parts
        )

    def bind(self, me, srcs, outs, refs):
        self.me, self.srcs, self.outs = me, srcs, outs
        count = len(self.parts)
        self.accs, refs = refs[:count], refs[count:]
        self.inboxes = []
        for p in self.parts:
            n = len(p.orders[0])
            self.inboxes.append(refs[:n])
            refs = refs[n:]
        self.lsem, self.ssem, self.rsem = refs

    def run(self, fills=()):
        grid, me = self.grid, self.me
        if all(p.orders[0] == p.orders[1] for p in self.parts):
            self.run_side(0, fills)
        else:
            for side in (0, 1):
                pl.when(me["c"] == side)(functools.partial(self.run_side, side, fills))

    def owner(self, order, off):
        pos, conds = self.me, []
        for d in order:
            conds.append(self.grid.valid(self.me, d, off[d]))
            pos = self.grid.move(pos, d, off[d])
        return pos, both(*conds)

    def run_side(self, side, fills):
        grid = self.grid
        todo, self.waits = [], []
        for i, part in enumerate(self.parts):
            order = part.orders[side]
            for time, minus, first, off in scatter_plan(grid, part, order):
                stage = -minus
                todo.append((time, minus, first, functools.partial(self.event, i, order, stage, off)))
                if stage == 0 and part.source is not None:
                    if off[order[0]] == 0 or grid.size[order[0]] > 2:
                        self.fetch(i, order, off)
        for time, fill in fills:
            todo.append((time, -99, 0, fill))
        todo.sort(key=lambda ev: ev[:3])
        for _, _, _, act in todo:
            act()
        for ok, cp in self.waits:
            under(ok, cp.wait_send)

    def load(self, i, pos, order):
        part = self.parts[i]
        idx, at = self.grid.index(pos, order), part.place(self.grid, pos, order)
        return pltpu.make_async_copy(
            self.source(i, idx), self.accs[i].at[at], self.lsem.at[self.base[i][0] + at]
        )

    def source(self, i, idx):
        part = self.parts[i]
        whole = self.srcs[part.source]
        if part.rows == whole.shape[1]:
            return whole.at[idx]
        return whole.at[idx, pl.ds(part.row, part.rows)]

    def fetch(self, i, order, off):
        pos, ok = self.owner(order, off)
        under(ok, self.load(i, pos, order).start)

    def event(self, i, order, stage, off):
        grid, me, part = self.grid, self.me, self.parts[i]
        acc, inbox = self.accs[i], self.inboxes[i][stage]
        _, send_base, inbox_base = self.base[i]
        d = order[stage]
        n = grid.size[d]
        later = order[stage + 1 :]
        pos, ok = self.owner(order[stage:], off)
        idx, at = grid.index(pos, order), part.place(grid, pos, order)
        last = stage == len(order) - 1

        def box(line_slot):
            tail = grid.index(pos, later)
            k = tail if n == 2 else line_slot * grid.count(later) + tail
            return inbox.at[k], self.rsem.at[inbox_base[stage] + k]

        def take(line_slot):
            ref, sem = box(line_slot)
            other = grid.device(grid.move(me, d, 1) if n == 2 else grid.move(me, order[0], 1))
            remote(ref, ref, self.ssem.at[0], sem, other).wait_recv()
            return ref

        def rows(body):
            def step(r, carry):
                body(pl.ds(pl.multiple_of(r * part.step, part.step), part.step))
                return carry

            lax.fori_loop(0, part.rows // part.step, step, 0)

        def add(ref):
            def body(r):
                acc[at, r, :] = (acc[at, r, :].astype(jnp.float32) + ref[r, :].astype(jnp.float32)).astype(
                    acc.dtype
                )

            rows(body)

        def close(refs):
            def body(r):
                total = acc[at, r, :].astype(jnp.float32)
                for ref in refs:
                    total = total + ref[r, :].astype(jnp.float32)
                for out, lead, first, count in part.outputs:
                    target = self.outs[out] if lead is None else self.outs[out].at[lead]
                    to = pl.ds(part.row + r.start, part.step)
                    target[to, :] = total[:, first : first + count].astype(target.dtype)

            rows(body)

        def ready():
            if stage == 0 and part.source is not None:
                self.load(i, pos, order).wait()

        def send(src, step, line_slot):
            ref, sem = box(line_slot)
            to = grid.device(grid.move(me, d, step))
            return remote(src, ref, self.ssem.at[send_base + idx], sem, to)

        if n == 2 and off[d]:
            direct = stage == 0 and part.source is not None
            cp = send(self.source(i, idx) if direct else acc.at[at], 1, 0)
            under(ok, cp.start)
            self.waits.append((ok, cp))
        elif n == 2:

            def merge():
                ready()
                ref = take(0)
                if last:
                    close([ref])
                else:
                    add(ref)

            under(ok, merge)
        elif off[d]:
            back = -1 if off[d] > 0 else 1
            has_back = grid.valid(me, d, back)
            to_slot = pos[d] if back < 0 else jnp.where(pos[d] == me[d] - 1, n, pos[d])
            cp = send(acc.at[at], -back, to_slot)

            def pass_on():
                ready()
                pl.when(has_back)(lambda: add(take(pos[d])))
                cp.start()

            under(ok, pass_on)
            self.waits.append((ok, cp))
        else:

            def collect():
                ready()
                low, high = grid.valid(me, d, -1), grid.valid(me, d, 1)
                if not last:
                    pl.when(low)(lambda: add(take(me[d])))
                    pl.when(high)(lambda: add(take(n)))
                    return
                pl.when(jnp.logical_and(low, high))(lambda: close([take(me[d]), take(n)]))
                pl.when(me[d] == 0)(lambda: close([take(n)]))
                pl.when(me[d] == n - 1)(lambda: close([take(me[d])]))

            under(ok, collect)


def scatter_kernel(grid, plan, count, outs, *refs):
    me = grid.here()
    plan.bind(me, refs[:count], refs[count : count + outs], refs[count + outs :])
    greet(grid, me, "".join(d for d in CANON if any(d in p.orders[0] for p in plan.parts)))
    plan.run()


def scatter(grid, arrays, orders, out_types, collective_id, name):
    parts = [
        Part(o, x.shape[0], x.shape[1], x.shape[2], x.dtype, i, [(i, None, 0, x.shape[2])])
        for i, (x, o) in enumerate(zip(arrays, orders))
    ]
    plan = Scatter(grid, parts)
    outs = sum(4 * p.size() // jnp.dtype(p.dtype).itemsize for p in parts)
    return pl.pallas_call(
        functools.partial(scatter_kernel, grid, plan, len(arrays), len(arrays)),
        out_shape=[jax.ShapeDtypeStruct(x.shape[1:], t) for x, t in zip(arrays, out_types)],
        in_specs=[pl.BlockSpec(memory_space=pl.ANY)] * len(arrays),
        out_specs=[pl.BlockSpec(memory_space=pltpu.VMEM)] * len(arrays),
        scratch_shapes=plan.scratch(),
        compiler_params=pltpu.CompilerParams(
            collective_id=collective_id, has_side_effects=True, vmem_limit_bytes=plan.bytes() + 2 * outs + (4 << 20)
        ),
        name=name,
    )(*arrays)


HEADS = 12
KV_HEADS = 4
HEAD_DIM = 128
TOPK = 6
NORM_EPSILON = 1e-05
GROUP = HEADS // KV_HEADS
BF = jnp.bfloat16
F32 = jnp.float32


def matmul(left, right):
    return jnp.dot(left, right, preferred_element_type=F32)


def left_product(left, right):
    return jnp.einsum("sa,sb->ab", left, right, preferred_element_type=F32)


def right_product(left, right):
    return jnp.einsum("sb,ab->sa", left, right, preferred_element_type=F32)


def inverse_rms(hidden):
    return lax.rsqrt(jnp.mean(hidden * hidden, axis=-1, keepdims=True) + NORM_EPSILON)


def norm_back(grad, hidden, inverse, gain):
    scaled = grad * gain
    inner = jnp.mean(scaled * hidden, axis=-1, keepdims=True)
    gain_grad = jnp.sum(grad * (hidden * inverse), axis=0)
    return inverse * scaled - hidden * (inverse * inverse * inverse) * inner, gain_grad


def silu_parts(pre):
    sigmoid = jax.nn.sigmoid(pre)
    return pre * sigmoid, sigmoid * (1.0 + pre * (1.0 - sigmoid))


def stacked(ref):
    return jnp.concatenate(
        [ref[0, :, g * HEAD_DIM : (g + 1) * HEAD_DIM] for g in range(GROUP)], axis=0
    )


def unstacked(ref, value):
    rows = ref.shape[1]
    for g in range(GROUP):
        ref[0, :, g * HEAD_DIM : (g + 1) * HEAD_DIM] = value[g * rows : (g + 1) * rows].astype(
            ref.dtype
        )


def masked_scores(first, query, key, rows):
    scores = lax.dot_general(
        query, key, (((1,), (1,)), ((), ())), preferred_element_type=F32
    ) * (HEAD_DIM**-0.5)
    place = first + lax.rem(lax.broadcasted_iota(jnp.int32, scores.shape, 0), rows)
    seen = lax.broadcasted_iota(jnp.int32, scores.shape, 1) <= place
    return jnp.where(seen, scores, -1e30)


def attend_kernel(first_ref, query_ref, key_ref, value_ref, out_ref):
    rows = query_ref.shape[1]
    length = key_ref.shape[0] * rows
    query = stacked(query_ref)
    key = key_ref[...].reshape(length, HEAD_DIM)
    value = value_ref[...].reshape(length, HEAD_DIM)
    scores = masked_scores(first_ref[0], query, key, rows)
    weights = jnp.exp(scores - jnp.max(scores, axis=-1, keepdims=True))
    probs = (weights / jnp.sum(weights, axis=-1, keepdims=True)).astype(BF)
    unstacked(out_ref, jnp.dot(probs, value, preferred_element_type=F32))


def attend_back_kernel(
    first_ref, query_ref, key_ref, value_ref, grad_ref, query_out, key_out, value_out
):
    rows = query_ref.shape[1]
    length = key_ref.shape[0] * rows
    scale = HEAD_DIM**-0.5
    query, grad = stacked(query_ref), stacked(grad_ref)
    key = key_ref[...].reshape(length, HEAD_DIM)
    value = value_ref[...].reshape(length, HEAD_DIM)
    scores = masked_scores(first_ref[0], query, key, rows)
    weights = jnp.exp(scores - jnp.max(scores, axis=-1, keepdims=True))
    probs = weights / jnp.sum(weights, axis=-1, keepdims=True)
    prob_grad = lax.dot_general(
        grad, value, (((1,), (1,)), ((), ())), preferred_element_type=F32
    )
    delta = jnp.sum(probs * prob_grad, axis=-1, keepdims=True)
    score_grad = (probs * (prob_grad - delta)).astype(BF)
    unstacked(query_out, jnp.dot(score_grad, key, preferred_element_type=F32) * scale)
    down = (((0,), (0,)), ((), ()))
    key_grad = lax.dot_general(score_grad, query, down, preferred_element_type=F32) * scale
    value_grad = lax.dot_general(probs.astype(BF), grad, down, preferred_element_type=F32)
    key_out[...] = key_grad.astype(BF).reshape(key_out.shape)
    value_out[...] = value_grad.astype(BF).reshape(value_out.shape)


def attention_specs(places, rows):
    query = pl.BlockSpec((1, rows, GROUP * HEAD_DIM), lambda m, h: (m, 0, h))
    key = pl.BlockSpec((places, 1, rows, HEAD_DIM), lambda m, h: (0, m, 0, h))
    value = pl.BlockSpec((places, 1, rows, HEAD_DIM), lambda m, h: (0, m, 0, KV_HEADS + h))
    return pl.BlockSpec(memory_space=pltpu.SMEM), query, key, value


def attend(first, qkv, kv_all):
    micro, rows, _ = qkv.shape
    scalar, query, key, value = attention_specs(kv_all.shape[0], rows)
    return pl.pallas_call(
        attend_kernel,
        grid=(micro, KV_HEADS),
        out_shape=jax.ShapeDtypeStruct((micro, rows, HEADS * HEAD_DIM), BF),
        in_specs=[scalar, query, key, value],
        out_specs=query,
        compiler_params=pltpu.CompilerParams(vmem_limit_bytes=40 << 20),
        name="attend",
    )(first, qkv, kv_all, kv_all)


def attend_back(first, qkv, kv_all, grad):
    micro, rows, _ = qkv.shape
    scalar, query, key, value = attention_specs(kv_all.shape[0], rows)
    kv_out = jax.ShapeDtypeStruct((kv_all.shape[0], micro, rows, KV_HEADS * HEAD_DIM), BF)
    return pl.pallas_call(
        attend_back_kernel,
        grid=(micro, KV_HEADS),
        out_shape=[jax.ShapeDtypeStruct((micro, rows, HEADS * HEAD_DIM), BF), kv_out, kv_out],
        in_specs=[scalar, query, key, value, query],
        out_specs=[query, key, key],
        compiler_params=pltpu.CompilerParams(vmem_limit_bytes=56 << 20),
        name="attend_back",
    )(first, qkv, kv_all, kv_all, grad)


def nearest(n, place, k):
    value = jnp.int32(0)
    for i in range(n):
        for j, t in enumerate(sorted(range(n), key=lambda t: (abs(t - i), t))):
            if t:
                value = jnp.where(jnp.logical_and(place == i, k == j), t, value)
    return value


TILE = 1536


def tiles(total, body, size=TILE):
    def step(t, carry):
        body(pl.ds(pl.multiple_of(t * size, size), size))
        return carry

    lax.fori_loop(0, total // size, step, 0)


def dot_tn(left, right):
    return lax.dot_general(left, right, (((0,), (0,)), ((), ())), preferred_element_type=F32)


def dot_nt(left, right):
    return lax.dot_general(left, right, (((1,), (1,)), ((), ())), preferred_element_type=F32)


def expert_kernel(grid, micro, slots, *refs):
    (x_ref, table_ref, top_ref, gate_ref, up_ref, down_ref, in_ref, out_ref) = refs[:8]
    (x_all, table_all, mixed_ref, back_ref, gates_ref, taken_ref, grad_ref, acts_ref, shid_ref, spre_ref) = refs[8:18]
    (w_in, w_down, s_in, s_out, x_buf, d_buf, t_buf, mixed_out, back_out, taken, grad, acts, shid, spre, picked, turned, top_rows, scaled, rows_back) = refs[18:37]
    (ssem, rsem, osem, wsem, lsem, dsem, msem, esem, ssem2) = refs[37:]
    me = grid.here()
    line, place = grid.size["a"], me["a"]
    held, hidden_width, width = w_down.shape
    rows = table_ref.shape[1]
    tokens = micro * rows
    unit_tokens = 2 * tokens
    half_slots = micro * slots
    unit_slots = 2 * half_slots
    shared_part = s_out.shape[0]
    experts = table_ref.shape[0] // (2 * micro)
    first_held = (me["a"] * 2 + me["b"]) * held
    greet(grid, me, "ab")

    fetches = [
        pltpu.make_async_copy(src, dst, wsem.at[i])
        for i, (src, dst) in enumerate(
            (
                (gate_ref, w_in.at[:, :, pl.ds(0, hidden_width)]),
                (up_ref, w_in.at[:, :, pl.ds(hidden_width, hidden_width)]),
                (down_ref, w_down),
                (in_ref, s_in),
                (out_ref, s_out),
            )
        )
    ]
    own = me["a"] * 2 + me["b"]
    pairs = ((x_ref, x_all), (table_ref, table_all))
    for i, (src, dst) in enumerate(pairs):
        pltpu.make_async_copy(src, dst.at[own], osem.at[i]).start()
    for i, (src, dst) in enumerate(pairs):
        pltpu.make_async_copy(src, dst.at[own], osem.at[i]).wait()

    def sends(a):
        idx = a * 2 + me["b"]
        made = []
        for i, (_, dst) in enumerate(pairs):
            block = dst.at[idx]
            for j, (d, step) in enumerate((("a", 1), ("a", -1), ("b", 1))):
                cond = None
                if d == "a":
                    ahead = a <= place if step > 0 else a >= place
                    cond = jnp.logical_and(ahead, grid.valid(me, d, step))
                to = grid.device(grid.move(me, d, step))
                made.append((cond, remote(block, block, ssem.at[i, a, j], rsem.at[i, idx], to)))
        return made

    def arrived(idx):
        for i, (_, dst) in enumerate(pairs):
            block = dst.at[idx]
            to = grid.device(grid.move(me, "b", 1))
            remote(block, block, osem.at[i], rsem.at[i, idx], to).wait_recv()

    for cond, cp in sends(place):
        under(cond, cp.start)
    for cp in fetches:
        cp.start()

    def top_copy(k):
        a = nearest(line, place, k)
        at = lax.rem(k, 2)
        return pltpu.make_async_copy(top_ref.at[pl.ds(a * 2, 2)], d_buf.at[at], dsem.at[at])

    top_copy(0).start()
    gates_ref[...] = jnp.zeros_like(gates_ref)
    for cp in fetches:
        cp.wait()

    def out_copies(a):
        at = pl.ds(a * 2, 2)
        return (
            pltpu.make_async_copy(mixed_out, mixed_ref.at[at], msem.at[0]),
            pltpu.make_async_copy(back_out, back_ref.at[at], msem.at[1]),
            pltpu.make_async_copy(shid, shid_ref.at[a], msem.at[2]),
            pltpu.make_async_copy(spre, spre_ref.at[a], msem.at[3]),
        )

    def row_copies(e, k):
        return (
            pltpu.make_async_copy(taken.at[e], taken_ref.at[e, k], esem.at[e, 0]),
            pltpu.make_async_copy(grad.at[e], grad_ref.at[e, k], esem.at[e, 1]),
            pltpu.make_async_copy(acts.at[e], acts_ref.at[e, k], esem.at[e, 2]),
        )

    def unit(k, carry):
        a = nearest(line, place, k)
        for step in (1, -1):
            far = place - step * (k + 1)
            ok = far >= 0 if step > 0 else far < line

            def relay(far=far):
                arrived(far * 2 + me["b"])
                for cond, cp in sends(far):
                    under(cond, cp.start)

            pl.when(ok)(relay)
        pl.when(k + 1 < line)(lambda: top_copy(k + 1).start())
        arrived(a * 2 + 1 - me["b"])
        fetch = (
            pltpu.make_async_copy(x_all.at[pl.ds(a * 2, 2)], x_buf, lsem.at[0]),
            pltpu.make_async_copy(table_all.at[pl.ds(a * 2, 2)], t_buf, lsem.at[1]),
        )
        for cp in fetch:
            cp.start()
        for cp in fetch:
            cp.wait()
        top_copy(k).wait()

        def leave():
            for cp in out_copies(a):
                cp.wait()

        pl.when(k > 0)(leave)
        x = x_buf.reshape(unit_tokens, width)
        top = d_buf.at[lax.rem(k, 2)].reshape(unit_tokens, width)

        def shared_rows(at):
            pre = jnp.dot(x[at, :], s_in[...], preferred_element_type=F32)
            silu, slope = silu_parts(pre[:, :shared_part])
            pre_up = pre[:, shared_part:]
            shid[at, :] = (silu * pre_up).astype(BF)
            mid_grad = dot_nt(top[at, :], s_out[...])
            spre[at, :shared_part] = (mid_grad * pre_up * slope).astype(BF)
            spre[at, shared_part:] = (mid_grad * silu).astype(BF)

        tiles(unit_tokens, shared_rows, 256)

        def expert(e, carry):
            def settle():
                for cp in row_copies(e, k):
                    cp.wait()

            pl.when(k > 0)(settle)
            gains = []
            for b in range(2):
                slot, gate = [], []
                for m in range(micro):
                    row = m * experts + first_held + e
                    one = t_buf[b, pl.ds(micro * experts + row, 1), :]
                    slot.append(jnp.where(one >= 0, one + m * slots, -1.0))
                    gate.append(t_buf[b, pl.ds(row, 1), :])
                slot = jnp.concatenate(slot, axis=1).astype(jnp.int32)
                named = lax.broadcasted_iota(jnp.int32, (half_slots, tokens), 0) == slot
                ones = named.astype(F32)
                picked[e, b] = ones.astype(BF)
                turned[e, b] = ones.T.astype(BF)
                gains.append(
                    jnp.sum(ones * jnp.concatenate(gate, axis=1), axis=1, keepdims=True)
                )
            gain = jnp.concatenate(gains, axis=0)

            def pick_rows(at):
                for b in range(2):
                    own = pl.ds(b * half_slots, half_slots)
                    of = pl.ds(b * tokens, tokens)
                    pick = picked[e, b]
                    taken[e, own, at] = jnp.dot(pick, x[of, at], preferred_element_type=F32).astype(BF)
                    got = jnp.dot(pick, top[of, at], preferred_element_type=F32)
                    top_rows[own, at] = got.astype(BF)
                    grad[e, own, at] = (gains[b] * got).astype(BF)

            tiles(width, pick_rows)
            pre = jnp.dot(taken[e], w_in[e], preferred_element_type=F32)
            hidden_grad = dot_nt(grad[e], w_down[e])
            silu, slope = silu_parts(pre[:, :hidden_width])
            pre_up = pre[:, hidden_width:]
            acts[e, :, :hidden_width] = (silu * pre_up).astype(BF)
            acts[e, :, hidden_width : 2 * hidden_width] = (hidden_grad * pre_up * slope).astype(BF)
            acts[e, :, 2 * hidden_width :] = (hidden_grad * silu).astype(BF)

            def leave_rows(t, gate_grad):
                at = pl.ds(pl.multiple_of(t * TILE, TILE), TILE)
                hidden = acts[e, :, :hidden_width]
                result = jnp.dot(hidden, w_down[e, :, at], preferred_element_type=F32)
                result = result.astype(BF).astype(F32)
                scaled[e, :, at] = (gain * result).astype(BF)
                product = top_rows[:, at].astype(F32) * result
                for c in range(0, TILE, 128):
                    gate_grad = gate_grad + product[:, c : c + 128]
                rows_back[e, :, at] = dot_nt(acts[e, :, hidden_width:], w_in[e, at, :]).astype(BF)
                return gate_grad

            gate_grad = lax.fori_loop(
                0, width // TILE, leave_rows, jnp.zeros((unit_slots, 128), F32)
            )
            gate_grad = jnp.sum(gate_grad, axis=1, keepdims=True)
            for b in range(2):
                spread = jnp.sum(
                    picked[e, b].astype(F32) * gate_grad[b * half_slots : (b + 1) * half_slots],
                    axis=0,
                    keepdims=True,
                )
                for m in range(micro):
                    row = m * experts + first_held + e
                    gates_ref[a * 2 + b, pl.ds(row, 1), :] = spread[:, m * rows : (m + 1) * rows]
            for cp in row_copies(e, k):
                cp.start()
            return carry

        lax.fori_loop(0, held, expert, 0)

        def combine(at):
            for b in range(2):
                own = pl.ds(b * half_slots, half_slots)
                of = pl.ds(b * tokens, tokens)
                mixed = jnp.dot(shid[of, :], s_out[:, at], preferred_element_type=F32)
                back = dot_nt(spre[of, :], s_in[at, :])
                for e in range(held):
                    turn = turned[e, b]
                    mixed += jnp.dot(turn, scaled[e, own, at], preferred_element_type=F32)
                    back += jnp.dot(turn, rows_back[e, own, at], preferred_element_type=F32)
                mixed_out[b, :, at] = mixed.astype(BF)
                back_out[b, :, at] = back.astype(BF)

        tiles(width, combine)
        for cp in out_copies(a):
            cp.start()
        return carry

    lax.fori_loop(0, line, unit, 0)
    for cp in out_copies(0):
        cp.wait()
    for e in range(held):
        for cp in row_copies(e, 0):
            cp.wait()
    for a in range(line):
        for cond, cp in sends(a):
            under(cond, cp.wait_send)


def run_experts(grid, micro, slots, x, table, tops, w_gate, w_up, w_down, s_in, s_out, collective_id):
    line = grid.size["a"]
    blocks = 2 * line
    tokens, width = x.shape
    held, _, hidden_width = w_gate.shape
    unit_tokens, unit_slots = 2 * tokens, 2 * micro * slots
    shared_part = s_out.shape[0]
    any_spec, vmem = pl.BlockSpec(memory_space=pl.ANY), pl.BlockSpec(memory_space=pltpu.VMEM)
    shape = jax.ShapeDtypeStruct
    dma = pltpu.SemaphoreType.DMA
    return pl.pallas_call(
        functools.partial(expert_kernel, grid, micro, slots),
        out_shape=[
            shape((blocks, tokens, width), BF),
            shape((blocks,) + table.shape, F32),
            shape((blocks, tokens, width), BF),
            shape((blocks, tokens, width), BF),
            shape((blocks, table.shape[0] // 2, table.shape[1]), F32),
            shape((held, line, unit_slots, width), BF),
            shape((held, line, unit_slots, width), BF),
            shape((held, line, unit_slots, 3 * hidden_width), BF),
            shape((line, unit_tokens, shared_part), BF),
            shape((line, unit_tokens, 2 * shared_part), BF),
        ],
        in_specs=[any_spec] * 8,
        out_specs=[any_spec] * 4 + [vmem] + [any_spec] * 5,
        scratch_shapes=[
            pltpu.VMEM((held, width, 2 * hidden_width), BF),
            pltpu.VMEM(w_down.shape, BF),
            pltpu.VMEM(s_in.shape, BF),
            pltpu.VMEM(s_out.shape, BF),
            pltpu.VMEM((2, tokens, width), BF),
            pltpu.VMEM((2, 2, tokens, width), BF),
            pltpu.VMEM((2,) + table.shape, F32),
            pltpu.VMEM((2, tokens, width), BF),
            pltpu.VMEM((2, tokens, width), BF),
            pltpu.VMEM((held, unit_slots, width), BF),
            pltpu.VMEM((held, unit_slots, width), BF),
            pltpu.VMEM((held, unit_slots, 3 * hidden_width), BF),
            pltpu.VMEM((unit_tokens, shared_part), BF),
            pltpu.VMEM((unit_tokens, 2 * shared_part), BF),
            pltpu.VMEM((held, 2, micro * slots, tokens), BF),
            pltpu.VMEM((held, 2, tokens, micro * slots), BF),
            pltpu.VMEM((unit_slots, width), BF),
            pltpu.VMEM((held, unit_slots, width), BF),
            pltpu.VMEM((held, unit_slots, width), BF),
            dma((2, line, 3)),
            dma((2, blocks)),
            dma((2,)),
            dma((5,)),
            dma((2,)),
            dma((2,)),
            dma((4,)),
            dma((held, 3)),
            dma((1,)),
        ],
        compiler_params=pltpu.CompilerParams(
            collective_id=collective_id, has_side_effects=True, vmem_limit_bytes=56 << 20
        ),
        name="experts",
    )(x, table, tops, w_gate, w_up, w_down, s_in, s_out)


def return_kernel(grid, plan, micro, *refs):
    ins, outs, refs = refs[:8], refs[8:16], refs[16:]
    taken_ref, grad_ref, acts_ref = ins[5:]
    taken, grad, acts, fsem = refs[:4]
    me = grid.here()
    plan.bind(me, ins[:5], outs, refs[4:])
    held = taken_ref.shape[0]
    hidden_width = acts.shape[1] // 3

    def loads(e):
        return [
            pltpu.make_async_copy(src.at[e], dst, fsem.at[j])
            for j, (src, dst) in enumerate(((taken_ref, taken), (acts_ref, acts), (grad_ref, grad)))
        ]

    for cp in loads(0):
        cp.start()
    greet(grid, me, "abxc")

    def product(left, first, right, total, acc):
        block = acc.shape[1]
        chunk = math.lcm(block, 128)

        def step(t, carry):
            at = pl.ds(pl.multiple_of(first + t * chunk, 128), chunk)
            value = dot_tn(left[:, at], right).astype(BF)
            for q in range(chunk // block):
                acc[t * (chunk // block) + q] = value[q * block : (q + 1) * block]
            return carry

        lax.fori_loop(0, total // chunk, step, 0)

    def fill(e):
        for cp in loads(e):
            cp.wait()
        product(taken, 0, acts[:, hidden_width:], taken.shape[1], plan.accs[3 + 2 * e])
        product(acts, 0, grad[...], hidden_width, plan.accs[4 + 2 * e])
        if e + 1 < held:
            for cp in loads(e + 1):
                cp.start()

    plan.run([(-0.9 + 0.2 * e, functools.partial(fill, e)) for e in range(held)])


def return_tokens(grid, micro, mixed, back, gates, shared_in, shared_out, taken, grad, acts, collective_id):
    held, _, width = taken.shape
    hidden_width = acts.shape[2] // 3
    seq = grid.size["x"] * 2
    parts = [
        Part(("ba", "ba"), x.shape[0], x.shape[1], x.shape[2], x.dtype, i, [(i, None, 0, x.shape[2])])
        for i, x in enumerate((mixed, back, gates))
    ]
    for e in range(held):
        ready = (-0.8 + 0.2 * e, -0.65 + e, -0.6 + e, 2.6 + 2 * e)
        rows = width // seq
        ways = [(5, e, 0, hidden_width), (6, e, hidden_width, hidden_width)]
        parts.append(Part(("cx", "cx"), seq, rows, 2 * hidden_width, BF, None, ways, ready=ready))
        rows = hidden_width // seq
        parts.append(Part(("cx", "cx"), seq, rows, width, BF, None, [(7, e, 0, width)], ready=ready))
    for i, x in enumerate((shared_in, shared_out)):
        parts.append(
            Part(("cx", "cx"), seq, x.shape[1], x.shape[2], BF, 3 + i, [(3 + i, None, 0, x.shape[2])])
        )
    plan = Scatter(grid, parts)
    shape = jax.ShapeDtypeStruct
    dma = pltpu.SemaphoreType.DMA
    return pl.pallas_call(
        functools.partial(return_kernel, grid, plan, micro),
        out_shape=[
            shape(mixed.shape[1:], F32),
            shape(back.shape[1:], F32),
            shape(gates.shape[1:], F32),
            shape(shared_in.shape[1:], BF),
            shape(shared_out.shape[1:], F32),
            shape((held, width // seq, hidden_width), F32),
            shape((held, width // seq, hidden_width), F32),
            shape((held, hidden_width // seq, width), F32),
        ],
        in_specs=[pl.BlockSpec(memory_space=pl.ANY)] * 8,
        out_specs=[pl.BlockSpec(memory_space=pltpu.VMEM)] * 8,
        scratch_shapes=[
            pltpu.VMEM(taken.shape[1:], BF),
            pltpu.VMEM(grad.shape[1:], BF),
            pltpu.VMEM(acts.shape[1:], BF),
            dma((3,)),
        ]
        + plan.scratch(),
        compiler_params=pltpu.CompilerParams(
            collective_id=collective_id, has_side_effects=True, vmem_limit_bytes=62 << 20
        ),
        name="return_tokens",
    )(mixed, back, gates, shared_in, shared_out, taken, grad, acts)


def per_device(
    block_input,
    norm_attn,
    w_query,
    w_key,
    w_value,
    w_out,
    norm_ffn,
    w_router,
    shared_gate,
    shared_up,
    shared_down,
    expert_gate,
    expert_up,
    expert_down,
    routes,
    out_grad,
):
    micro, _, rows, width = block_input.shape
    tokens = micro * rows
    experts = w_router.shape[1]
    held = expert_gate.shape[0]
    exp_size, seq_size = lax.axis_size("exp"), lax.axis_size("seq")
    blocks = exp_size * seq_size
    grid = Grid(exp_size, seq_size)
    slots = min(rows, 8 * ((3 * rows * TOPK // (2 * experts) + 7) // 8))
    query_width = HEADS * HEAD_DIM
    kv_width = KV_HEADS * HEAD_DIM
    qkv_width = query_width + 2 * kv_width
    own_rows = w_query.shape[0]
    shared_part = shared_gate.shape[1] // exp_size
    first = (lax.axis_index("seq") * rows).astype(jnp.int32).reshape(1)

    small = jnp.concatenate([norm_attn[:, None], norm_ffn[:, None], w_router], axis=1)
    small = jnp.pad(small, ((0, 0), (0, 128 - small.shape[1])))
    route = ("abxc", "abxc")
    qkv_full, out_full, small_full, grads_all, shared_out = gather(
        grid,
        [
            jnp.concatenate([w_query, w_key, w_value], axis=1),
            w_out,
            small,
            out_grad.reshape(tokens, width),
            shared_down,
        ],
        [route] * 3 + [("ab", "ab"), ("xc", "xc")],
        1,
        "gather_dense",
    )
    shared_out = shared_out.reshape(shared_part, width)
    qkv_full = qkv_full.reshape(width, qkv_width)
    out_full = out_full.reshape(query_width, width)
    small_full = small_full.reshape(width, 128)
    gain_one = small_full[:, 0].astype(F32)
    gain_two = small_full[:, 1].astype(F32)
    router_full = small_full[:, 2 : 2 + experts]

    gate_full = lax.all_gather(expert_gate, "seq", axis=1, tiled=True)
    up_full = lax.all_gather(expert_up, "seq", axis=1, tiled=True)
    down_full = lax.all_gather(expert_down, "seq", axis=1, tiled=True)
    halves = jnp.concatenate(
        [
            shared_gate.reshape(own_rows, exp_size, shared_part),
            shared_up.reshape(own_rows, exp_size, shared_part),
        ],
        axis=2,
    ).transpose(1, 0, 2)
    halves = lax.all_to_all(halves, "exp", split_axis=0, concat_axis=0, tiled=True)
    shared_in = lax.all_gather(halves, "seq", axis=1).reshape(width, 2 * shared_part)

    hidden_in = block_input.reshape(tokens, width).astype(F32)
    inverse_one = inverse_rms(hidden_in)
    normed_one = (hidden_in * inverse_one * gain_one).astype(BF)
    qkv = matmul(normed_one, qkv_full).astype(BF)
    (kv_all,) = gather(grid, [qkv[:, query_width:]], [("xc", "xc")], 2, "gather_kv")
    kv_all = kv_all.reshape(seq_size, micro, rows, 2 * kv_width)
    qkv = qkv.reshape(micro, rows, qkv_width)
    attended = attend(first, qkv, kv_all).reshape(tokens, query_width)
    hidden_mid = hidden_in + matmul(attended, out_full)
    inverse_two = inverse_rms(hidden_mid)
    normed_two = (hidden_mid * inverse_two * gain_two).astype(BF)

    route_rows = routes.reshape(tokens, TOPK)
    named = route_rows[:, :, None] == jnp.arange(experts, dtype=jnp.int32)
    chosen = jnp.any(named, axis=1)
    logits = matmul(normed_two, router_full)
    masked = jnp.where(chosen, logits, -jnp.inf)
    powers = jnp.exp(masked - jnp.max(masked, axis=-1, keepdims=True))
    gates = powers / jnp.sum(powers, axis=-1, keepdims=True)
    member = chosen.reshape(micro, rows, experts).astype(jnp.int32)
    rank = jnp.cumsum(member, axis=1) - member
    slot = jnp.where(member > 0, rank, -1).astype(F32)

    def by_expert(table):
        return table.reshape(micro, rows, experts).transpose(0, 2, 1).reshape(micro * experts, rows)

    table = jnp.concatenate([by_expert(gates), by_expert(slot)], axis=0)
    inputs_all, _, mixed, back, gate_table, taken, taken_grad, acts, shared_hidden, shared_pre = run_experts(
        grid, micro, slots, normed_two, table, grads_all, gate_full, up_full, down_full, shared_in, shared_out, 3
    )
    flat = inputs_all.reshape(exp_size * tokens, width)
    flat_top = grads_all.reshape(exp_size * tokens, width)
    shared_in_term = left_product(flat, shared_pre.reshape(-1, 2 * shared_part)).astype(BF)
    shared_out_term = left_product(shared_hidden.reshape(-1, shared_part), flat_top).astype(BF)
    hidden_width = expert_gate.shape[2]
    taken = taken.reshape(held, -1, width)
    taken_grad = taken_grad.reshape(held, -1, width)
    acts = acts.reshape(held, -1, 3 * hidden_width)
    shared_in_term = shared_in_term.reshape(exp_size, seq_size, own_rows, 2 * shared_part)
    (
        mixture,
        token_grad,
        gate_grad,
        halves,
        shared_down_grad,
        expert_gate_grad,
        expert_up_grad,
        expert_down_grad,
    ) = return_tokens(
        grid,
        micro,
        mixed,
        back,
        gate_table,
        shared_in_term.transpose(1, 0, 2, 3).reshape(seq_size, exp_size * own_rows, 2 * shared_part),
        shared_out_term.reshape(seq_size, shared_part // seq_size, width),
        taken,
        taken_grad,
        acts,
        4,
    )
    halves = halves.reshape(exp_size, own_rows, 2 * shared_part)
    halves = lax.all_to_all(halves, "exp", split_axis=0, concat_axis=0, tiled=True).astype(F32)
    halves = halves.transpose(1, 0, 2)
    shared_gate_grad = halves[:, :, :shared_part].reshape(own_rows, exp_size * shared_part)
    shared_up_grad = halves[:, :, shared_part:].reshape(own_rows, exp_size * shared_part)

    block_output = (hidden_mid + mixture).astype(BF).reshape(block_input.shape)

    gate_grad = gate_grad.reshape(micro, experts, rows).transpose(0, 2, 1).reshape(tokens, experts)
    logit_grad = gates * (gate_grad - jnp.sum(gates * gate_grad, axis=-1, keepdims=True))
    logit_grad = logit_grad.astype(BF)
    grad_top = out_grad.reshape(tokens, width).astype(F32)
    normed_two_grad = token_grad + right_product(logit_grad, router_full)
    mid_part, norm_two_term = norm_back(normed_two_grad, hidden_mid, inverse_two, gain_two)
    mid_grad = mid_part + grad_top
    attn_grad = mid_grad.astype(BF)
    attended_grad = right_product(attn_grad, out_full).astype(BF)
    query_grad, key_part, value_part = attend_back(
        first, qkv, kv_all, attended_grad.reshape(micro, rows, query_width)
    )
    key_grad, value_grad = scatter(
        grid,
        [
            key_part.reshape(seq_size, tokens, kv_width),
            value_part.reshape(seq_size, tokens, kv_width),
        ],
        [("cx", "cx")] * 2,
        [BF] * 2,
        5,
        "scatter_kv",
    )
    qkv_grad = jnp.concatenate(
        [query_grad.reshape(tokens, query_width), key_grad, value_grad], axis=1
    )
    normed_one_grad = right_product(qkv_grad, qkv_full)
    in_part, norm_one_term = norm_back(normed_one_grad, hidden_in, inverse_one, gain_one)
    input_grad = (in_part + mid_grad).reshape(block_input.shape)
    small_term = jnp.concatenate(
        [norm_one_term[:, None], norm_two_term[:, None], left_product(normed_two, logit_grad)],
        axis=1,
    )
    small_term = jnp.pad(small_term, ((0, 0), (0, 128 - small_term.shape[1])))
    order = ("cxba", "cbxa" if seq_size == 4 else "cxba")
    qkv_share, out_share, small_share = scatter(
        grid,
        [
            left_product(normed_one, qkv_grad).astype(BF).reshape(blocks, own_rows, qkv_width),
            left_product(attended, attn_grad).astype(BF).reshape(blocks, own_rows, width),
            small_term.reshape(blocks, own_rows, 128),
        ],
        [order] * 3,
        [F32] * 3,
        6,
        "scatter_dense",
    )
    return (
        block_output,
        input_grad,
        small_share[:, 0],
        qkv_share[:, :query_width],
        qkv_share[:, query_width : query_width + kv_width],
        qkv_share[:, query_width + kv_width :],
        out_share,
        small_share[:, 1],
        small_share[:, 2 : 2 + experts],
        shared_gate_grad,
        shared_up_grad,
        shared_down_grad,
        expert_gate_grad,
        expert_up_grad,
        expert_down_grad,
    )


def solution(mesh):
    tokens = P(None, "exp", "seq", None)
    vector, matrix = P(("exp", "seq")), P(("exp", "seq"), None)
    stack = P("exp", "seq", None)
    weights = (vector,) + (matrix,) * 4 + (vector,) + (matrix,) * 4 + (stack,) * 3
    return jax.shard_map(
        per_device,
        mesh=mesh,
        in_specs=(tokens,) + weights + (tokens, tokens),
        out_specs=(tokens, tokens) + weights,
        check_vma=False,
    )
```

```python
import functools
import itertools
import math

import jax
import jax.numpy as jnp
from jax import lax
from jax.experimental import pallas as pl
from jax.experimental.pallas import tpu as pltpu
from jax.sharding import PartitionSpec as P

MESH = pl.DeviceIdType.MESH
CANON = "abxc"


class Grid:
    def __init__(self, exp_size, seq_size):
        self.size = {"a": exp_size // 2, "b": 2, "x": seq_size // 2, "c": 2}

    def here(self):
        e = lax.axis_index("exp")
        s = lax.axis_index("seq")
        return {"a": lax.div(e, 2), "b": lax.rem(e, 2), "x": lax.div(s, 2), "c": lax.rem(s, 2)}

    def device(self, pos):
        return (pos["a"] * 2 + pos["b"], pos["x"] * 2 + pos["c"])

    def index(self, pos, dims):
        number = 0
        for d in CANON:
            if d in dims:
                number = number * self.size[d] + pos[d]
        return number

    def count(self, dims):
        return math.prod(self.size[d] for d in dims)

    def offsets(self, d):
        n = self.size[d]
        return (0, 1) if n == 2 else tuple(range(-(n - 1), n))

    def move(self, pos, d, off):
        new = dict(pos)
        if off:
            new[d] = 1 - pos[d] if self.size[d] == 2 else pos[d] + off
        return new

    def valid(self, pos, d, off):
        if off == 0 or self.size[d] == 2:
            return None
        return pos[d] + off >= 0 if off < 0 else pos[d] + off < self.size[d]

    def steps(self, d):
        if self.size[d] == 1:
            return ()
        return (1,) if self.size[d] == 2 else (1, -1)


def both(*conds):
    conds = [c for c in conds if c is not None]
    return functools.reduce(jnp.logical_and, conds) if conds else None


def under(cond, body):
    if cond is None:
        body()
    else:
        pl.when(cond)(body)


def greet(grid, me, dims, total=0):
    bar = pltpu.get_barrier_semaphore()
    for d in dims:
        for step in grid.steps(d):
            ok = grid.valid(me, d, step)

            def signal(d=d, step=step):
                pl.semaphore_signal(
                    bar, inc=1, device_id=grid.device(grid.move(me, d, step)), device_id_type=MESH
                )

            under(ok, signal)
            total = total + (1 if ok is None else ok.astype(jnp.int32))
    pl.semaphore_wait(bar, total)


def remote(src, dst, ssem, rsem, device):
    return pltpu.make_async_remote_copy(
        src_ref=src, dst_ref=dst, send_sem=ssem, recv_sem=rsem, device_id=device, device_id_type=MESH
    )


def gather_plan(grid, orders):
    dims = orders[0]
    events = []
    for combo in itertools.product(*[grid.offsets(d) for d in dims]):
        off = dict(zip(dims, combo))
        sends = []
        for order in orders:
            last = max([k for k, d in enumerate(order) if off[d]], default=-1)
            mine = []
            if last >= 0 and grid.size[order[last]] > 2:
                mine.append((order[last], 1 if off[order[last]] < 0 else -1))
            for d in order[last + 1 :]:
                mine.extend((d, step) for step in grid.steps(d))
            sends.append(mine)
        events.append((sum(abs(v) for v in combo), off, sends))
    events.sort(key=lambda ev: ev[0])
    return events


class Item:
    def __init__(self, array, orders, rows=None, late=0, spread=False, start=0):
        self.array, self.orders, self.rows, self.late, self.spread = array, orders, rows, late, spread
        self.start = start

    def blocks(self, grid):
        return grid.count("abxc" if self.spread else self.orders[0])


def gather_kernel(grid, items, count, *refs):
    srcs, dsts = refs[:count], refs[count : 2 * count]
    ssem, rsem, lsem = refs[2 * count :]
    me = grid.here()
    own = me["a"] * 2 + me["b"]
    exp_size, seq_size = grid.count("ab"), grid.count("xc")
    others = [lax.rem(own + j, exp_size) for j in range(1, exp_size)]
    here = (me["x"] * 2 + me["c"]).astype(jnp.int32)
    wide = any(item.spread for item in items)
    used = "".join(d for d in CANON if any(d in item.orders[0] for item in items))
    if wide:
        greet_wide(grid, me)
    else:
        greet(grid, me, used)
    base, total = [], 0
    for item in items:
        base.append(total)
        total += item.blocks(grid)
    waits, slot, merged = [], 0, []
    for i, item in enumerate(items):
        plan = gather_plan(grid, item.orders)
        for j in range(exp_size if item.spread else 1):
            for hops, off, sends in plan:
                time = hops + item.late * (hops > 0) + item.start + (1.5 if j else 0)
                merged.append((time, i, j, hops, off, sends))
        if item.spread:
            src, dst = srcs[item.array], dsts[item.array]
            mine = own * seq_size + here
            for e in others:
                cp = remote(src.at[e], dst.at[mine], ssem.at[slot], rsem.at[base[i] + mine], (e, here))
                cp.start()
                waits.append((None, cp.wait_send))
                slot += 1
    merged.sort(key=lambda ev: ev[:3])
    for time, i, j, hops, off, sends in merged:
        item = items[i]
        dims = item.orders[0]
        pos, conds = me, []
        for d in dims:
            conds.append(grid.valid(me, d, off[d]))
            pos = grid.move(pos, d, off[d])
        ok = both(*conds)
        idx = grid.index(pos, dims)
        if item.spread:
            idx = (own if j == 0 else others[j - 1]) * seq_size + idx
        sem = rsem.at[base[i] + idx]
        block, src = dsts[item.array].at[idx], srcs[item.array]
        if item.spread:
            src = src.at[own]
        if item.rows is not None:
            block, src = block.at[pl.ds(*item.rows)], src.at[pl.ds(*item.rows)]
        first = hops == 0 and j == 0
        if not first:
            src = block
        plan = []
        for d, step in sorted(set(sends[0]) | set(sends[1])):
            side = None
            if (d, step) not in sends[0]:
                side = me["c"] == 1
            elif (d, step) not in sends[1]:
                side = me["c"] == 0
            cp = remote(src, block, ssem.at[slot], sem, grid.device(grid.move(me, d, step)))
            plan.append((both(grid.valid(me, d, step), side), cp))
            slot += 1

        def arrive(first=first, i=i, src=src, block=block, sem=sem, plan=plan):
            if first:
                pltpu.make_async_copy(src, block, lsem.at[i]).start()
            else:
                to = grid.device(grid.move(me, used[-1], 1))
                remote(block, block, lsem.at[i], sem, to).wait_recv()
            for cond, cp in plan:
                under(cond, cp.start)

        def finish(first=first, i=i, src=src, block=block, plan=plan):
            if first:
                pltpu.make_async_copy(src, block, lsem.at[i]).wait()
            for cond, cp in plan:
                under(cond, cp.wait_send)

        under(ok, arrive)
        waits.append((ok, finish))
    for ok, finish in waits:
        under(ok, finish)


def count_sends(grid, item):
    plan = gather_plan(grid, item.orders)
    sends = sum(len(set(ev[2][0]) | set(ev[2][1])) for ev in plan)
    exp_size = grid.count("ab")
    return sends * exp_size + exp_size - 1 if item.spread else sends


def greet_wide(grid, me):
    bar = pltpu.get_barrier_semaphore()
    own = me["a"] * 2 + me["b"]
    exp_size = grid.count("ab")
    for j in range(1, exp_size):
        to = (lax.rem(own + j, exp_size), me["x"] * 2 + me["c"])
        pl.semaphore_signal(bar, inc=1, device_id=to, device_id_type=MESH)
    greet(grid, me, "xc", exp_size - 1)


def gather(grid, arrays, items, collective_id, name, near=()):
    shapes = {}
    for item in items:
        x = arrays[item.array]
        shapes[item.array] = (item.blocks(grid),) + (x.shape[1:] if item.spread else x.shape)
    return pl.pallas_call(
        functools.partial(gather_kernel, grid, items, len(arrays)),
        out_shape=[jax.ShapeDtypeStruct(shapes[i], x.dtype) for i, x in enumerate(arrays)],
        in_specs=[pl.BlockSpec(memory_space=pltpu.VMEM)] * len(arrays),
        out_specs=[
            pl.BlockSpec(memory_space=pltpu.VMEM if i in near else pl.ANY) for i in range(len(arrays))
        ],
        scratch_shapes=[
            pltpu.SemaphoreType.DMA((sum(count_sends(grid, item) for item in items),)),
            pltpu.SemaphoreType.DMA((sum(item.blocks(grid) for item in items),)),
            pltpu.SemaphoreType.DMA((len(items),)),
        ],
        compiler_params=pltpu.CompilerParams(
            collective_id=collective_id, has_side_effects=True, vmem_limit_bytes=32 << 20
        ),
        name=name,
    )(*arrays)


class Part:
    def __init__(self, orders, blocks, rows, columns, dtype, source, outputs, row=0, ready=None):
        self.orders, self.blocks, self.rows, self.columns = orders, blocks, rows, columns
        self.dtype, self.source, self.outputs, self.row, self.ready = dtype, source, outputs, row, ready
        self.step = min(16, rows)

    def size(self):
        return -(-self.rows // 16) * 16 * self.columns * jnp.dtype(self.dtype).itemsize

    def kept(self, grid):
        half = self.source is not None and grid.size[self.orders[0][0]] == 2
        return self.blocks // 2 if half else self.blocks

    def place(self, grid, pos, order):
        half = self.source is not None and grid.size[order[0]] == 2
        return grid.index(pos, order[1:] if half else order)

    def inbox(self, grid, stage):
        return max(
            (1 if grid.size[o[stage]] == 2 else grid.size[o[stage]] + 1) * grid.count(o[stage + 1 :])
            for o in self.orders
        )


def scatter_plan(grid, part, order):
    lead = order[-1]
    span = grid.size[lead]
    events = []
    for stage, d in enumerate(order):
        rest = order[stage:]
        for combo in itertools.product(*[grid.offsets(r) for r in rest]):
            off = dict(zip(rest, combo))
            time = span - 1 - abs(off[lead]) + stage - (1.5 if d == "c" else 0)
            first = 0 if off[d] else 1
            if order == "ab":
                time = -5 - 0.1 * abs(off["a"]) if stage == 0 else (3.5 if first else -4)
            if part.ready is not None:
                time = part.ready[2 * min(stage, 1) + first]
            elif stage == 0 and grid.size[d] == 2 and off[d]:
                time -= 100
            events.append((time, -stage, first, off))
    events.sort(key=lambda ev: ev[:3])
    return events


class Scatter:
    def __init__(self, grid, parts):
        self.grid, self.parts = grid, parts
        self.base, blocks, sends, slots = [], 0, 0, 0
        for part in parts:
            stages = []
            for stage in range(len(part.orders[0])):
                stages.append(slots)
                slots += part.inbox(grid, stage)
            self.base.append((blocks, sends, stages))
            blocks += part.kept(grid)
            sends += part.blocks
        self.totals = (blocks, sends, slots)

    def scratch(self):
        dma = pltpu.SemaphoreType.DMA
        out = [pltpu.VMEM((p.kept(self.grid), p.rows, p.columns), p.dtype) for p in self.parts]
        for p in self.parts:
            for stage in range(len(p.orders[0])):
                out.append(pltpu.VMEM((p.inbox(self.grid, stage), p.rows, p.columns), p.dtype))
        return out + [dma((n,)) for n in self.totals]

    def bytes(self):
        return sum(
            p.size() * (p.kept(self.grid) + sum(p.inbox(self.grid, k) for k in range(len(p.orders[0]))))
            for p in self.parts
        )

    def bind(self, me, srcs, outs, refs):
        self.me, self.srcs, self.outs = me, srcs, outs
        count = len(self.parts)
        self.accs, refs = refs[:count], refs[count:]
        self.inboxes = []
        for p in self.parts:
            n = len(p.orders[0])
            self.inboxes.append(refs[:n])
            refs = refs[n:]
        self.lsem, self.ssem, self.rsem = refs

    def run(self, fills=()):
        grid, me = self.grid, self.me
        if all(p.orders[0] == p.orders[1] for p in self.parts):
            self.run_side(0, fills)
        else:
            for side in (0, 1):
                pl.when(me["c"] == side)(functools.partial(self.run_side, side, fills))

    def owner(self, order, off):
        pos, conds = self.me, []
        for d in order:
            conds.append(self.grid.valid(self.me, d, off[d]))
            pos = self.grid.move(pos, d, off[d])
        return pos, both(*conds)

    def run_side(self, side, fills):
        grid = self.grid
        todo, self.waits = [], []
        for i, part in enumerate(self.parts):
            order = part.orders[side]
            for time, minus, first, off in scatter_plan(grid, part, order):
                stage = -minus
                todo.append((time, minus, first, functools.partial(self.event, i, order, stage, off)))
                if stage == 0 and part.source is not None:
                    if off[order[0]] == 0 or grid.size[order[0]] > 2:
                        self.fetch(i, order, off)
        for time, fill in fills:
            todo.append((time, -99, 0, fill))
        todo.sort(key=lambda ev: ev[:3])
        for _, _, _, act in todo:
            act()
        for ok, cp in self.waits:
            under(ok, cp.wait_send)

    def load(self, i, pos, order):
        part = self.parts[i]
        idx, at = self.grid.index(pos, order), part.place(self.grid, pos, order)
        return pltpu.make_async_copy(
            self.source(i, idx), self.accs[i].at[at], self.lsem.at[self.base[i][0] + at]
        )

    def source(self, i, idx):
        part = self.parts[i]
        whole = self.srcs[part.source]
        if part.rows == whole.shape[1]:
            return whole.at[idx]
        return whole.at[idx, pl.ds(part.row, part.rows)]

    def fetch(self, i, order, off):
        pos, ok = self.owner(order, off)
        under(ok, self.load(i, pos, order).start)

    def event(self, i, order, stage, off):
        grid, me, part = self.grid, self.me, self.parts[i]
        acc, inbox = self.accs[i], self.inboxes[i][stage]
        _, send_base, inbox_base = self.base[i]
        d = order[stage]
        n = grid.size[d]
        later = order[stage + 1 :]
        pos, ok = self.owner(order[stage:], off)
        idx, at = grid.index(pos, order), part.place(grid, pos, order)
        last = stage == len(order) - 1

        def box(line_slot):
            tail = grid.index(pos, later)
            k = tail if n == 2 else line_slot * grid.count(later) + tail
            return inbox.at[k], self.rsem.at[inbox_base[stage] + k]

        def take(line_slot):
            ref, sem = box(line_slot)
            other = grid.device(grid.move(me, d, 1) if n == 2 else grid.move(me, order[0], 1))
            remote(ref, ref, self.ssem.at[0], sem, other).wait_recv()
            return ref

        def rows(body):
            def step(r, carry):
                body(pl.ds(pl.multiple_of(r * part.step, part.step), part.step))
                return carry

            lax.fori_loop(0, part.rows // part.step, step, 0)

        def add(ref):
            def body(r):
                acc[at, r, :] = (acc[at, r, :].astype(jnp.float32) + ref[r, :].astype(jnp.float32)).astype(
                    acc.dtype
                )

            rows(body)

        def close(refs):
            def body(r):
                total = acc[at, r, :].astype(jnp.float32)
                for ref in refs:
                    total = total + ref[r, :].astype(jnp.float32)
                for out, lead, first, count in part.outputs:
                    target = self.outs[out] if lead is None else self.outs[out].at[lead]
                    to = pl.ds(part.row + r.start, part.step)
                    target[to, :] = total[:, first : first + count].astype(target.dtype)

            rows(body)

        def ready():
            if stage == 0 and part.source is not None:
                self.load(i, pos, order).wait()

        def send(src, step, line_slot):
            ref, sem = box(line_slot)
            to = grid.device(grid.move(me, d, step))
            return remote(src, ref, self.ssem.at[send_base + idx], sem, to)

        if n == 2 and off[d]:
            direct = stage == 0 and part.source is not None
            cp = send(self.source(i, idx) if direct else acc.at[at], 1, 0)
            under(ok, cp.start)
            self.waits.append((ok, cp))
        elif n == 2:

            def merge():
                ready()
                ref = take(0)
                if last:
                    close([ref])
                else:
                    add(ref)

            under(ok, merge)
        elif off[d]:
            back = -1 if off[d] > 0 else 1
            has_back = grid.valid(me, d, back)
            to_slot = pos[d] if back < 0 else jnp.where(pos[d] == me[d] - 1, n, pos[d])
            cp = send(acc.at[at], -back, to_slot)

            def pass_on():
                ready()
                pl.when(has_back)(lambda: add(take(pos[d])))
                cp.start()

            under(ok, pass_on)
            self.waits.append((ok, cp))
        else:

            def collect():
                ready()
                low, high = grid.valid(me, d, -1), grid.valid(me, d, 1)
                if not last:
                    pl.when(low)(lambda: add(take(me[d])))
                    pl.when(high)(lambda: add(take(n)))
                    return
                pl.when(jnp.logical_and(low, high))(lambda: close([take(me[d]), take(n)]))
                pl.when(me[d] == 0)(lambda: close([take(n)]))
                pl.when(me[d] == n - 1)(lambda: close([take(me[d])]))

            under(ok, collect)


def scatter_kernel(grid, plan, count, outs, *refs):
    me = grid.here()
    plan.bind(me, refs[:count], refs[count : count + outs], refs[count + outs :])
    greet(grid, me, "".join(d for d in CANON if any(d in p.orders[0] for p in plan.parts)))
    plan.run()


def scatter(grid, arrays, orders, out_types, collective_id, name):
    parts = [
        Part(o, x.shape[0], x.shape[1], x.shape[2], x.dtype, i, [(i, None, 0, x.shape[2])])
        for i, (x, o) in enumerate(zip(arrays, orders))
    ]
    plan = Scatter(grid, parts)
    outs = sum(4 * p.size() // jnp.dtype(p.dtype).itemsize for p in parts)
    return pl.pallas_call(
        functools.partial(scatter_kernel, grid, plan, len(arrays), len(arrays)),
        out_shape=[jax.ShapeDtypeStruct(x.shape[1:], t) for x, t in zip(arrays, out_types)],
        in_specs=[pl.BlockSpec(memory_space=pl.ANY)] * len(arrays),
        out_specs=[pl.BlockSpec(memory_space=pltpu.VMEM)] * len(arrays),
        scratch_shapes=plan.scratch(),
        compiler_params=pltpu.CompilerParams(
            collective_id=collective_id, has_side_effects=True, vmem_limit_bytes=plan.bytes() + 2 * outs + (4 << 20)
        ),
        name=name,
    )(*arrays)


HEADS = 12
KV_HEADS = 4
HEAD_DIM = 128
TOPK = 6
NORM_EPSILON = 1e-05
GROUP = HEADS // KV_HEADS
BF = jnp.bfloat16
F32 = jnp.float32


def matmul(left, right):
    return jnp.dot(left, right, preferred_element_type=F32)


def left_product(left, right):
    return jnp.einsum("sa,sb->ab", left, right, preferred_element_type=F32)


def right_product(left, right):
    return jnp.einsum("sb,ab->sa", left, right, preferred_element_type=F32)


def inverse_rms(hidden):
    return lax.rsqrt(jnp.mean(hidden * hidden, axis=-1, keepdims=True) + NORM_EPSILON)


def norm_back(grad, hidden, inverse, gain):
    scaled = grad * gain
    inner = jnp.mean(scaled * hidden, axis=-1, keepdims=True)
    gain_grad = jnp.sum(grad * (hidden * inverse), axis=0)
    return inverse * scaled - hidden * (inverse * inverse * inverse) * inner, gain_grad


def silu_parts(pre):
    sigmoid = jax.nn.sigmoid(pre)
    return pre * sigmoid, sigmoid * (1.0 + pre * (1.0 - sigmoid))


def stacked(ref):
    return jnp.concatenate(
        [ref[0, :, g * HEAD_DIM : (g + 1) * HEAD_DIM] for g in range(GROUP)], axis=0
    )


def unstacked(ref, value):
    rows = ref.shape[1]
    for g in range(GROUP):
        ref[0, :, g * HEAD_DIM : (g + 1) * HEAD_DIM] = value[g * rows : (g + 1) * rows].astype(
            ref.dtype
        )


def masked_scores(first, query, key, rows):
    scores = lax.dot_general(
        query, key, (((1,), (1,)), ((), ())), preferred_element_type=F32
    ) * (HEAD_DIM**-0.5)
    place = first + lax.rem(lax.broadcasted_iota(jnp.int32, scores.shape, 0), rows)
    seen = lax.broadcasted_iota(jnp.int32, scores.shape, 1) <= place
    return jnp.where(seen, scores, -1e30)


def attend_kernel(first_ref, query_ref, key_ref, value_ref, out_ref):
    rows = query_ref.shape[1]
    length = key_ref.shape[0] * rows
    query = stacked(query_ref)
    key = key_ref[...].reshape(length, HEAD_DIM)
    value = value_ref[...].reshape(length, HEAD_DIM)
    scores = masked_scores(first_ref[0], query, key, rows)
    weights = jnp.exp(scores - jnp.max(scores, axis=-1, keepdims=True))
    probs = (weights / jnp.sum(weights, axis=-1, keepdims=True)).astype(BF)
    unstacked(out_ref, jnp.dot(probs, value, preferred_element_type=F32))


def attend_back_kernel(
    first_ref, query_ref, key_ref, value_ref, grad_ref, query_out, key_out, value_out
):
    rows = query_ref.shape[1]
    length = key_ref.shape[0] * rows
    scale = HEAD_DIM**-0.5
    query, grad = stacked(query_ref), stacked(grad_ref)
    key = key_ref[...].reshape(length, HEAD_DIM)
    value = value_ref[...].reshape(length, HEAD_DIM)
    scores = masked_scores(first_ref[0], query, key, rows)
    weights = jnp.exp(scores - jnp.max(scores, axis=-1, keepdims=True))
    probs = weights / jnp.sum(weights, axis=-1, keepdims=True)
    prob_grad = lax.dot_general(
        grad, value, (((1,), (1,)), ((), ())), preferred_element_type=F32
    )
    delta = jnp.sum(probs * prob_grad, axis=-1, keepdims=True)
    score_grad = (probs * (prob_grad - delta)).astype(BF)
    unstacked(query_out, jnp.dot(score_grad, key, preferred_element_type=F32) * scale)
    down = (((0,), (0,)), ((), ()))
    key_grad = lax.dot_general(score_grad, query, down, preferred_element_type=F32) * scale
    value_grad = lax.dot_general(probs.astype(BF), grad, down, preferred_element_type=F32)
    key_out[...] = key_grad.astype(BF).reshape(key_out.shape)
    value_out[...] = value_grad.astype(BF).reshape(value_out.shape)


def attention_specs(places, rows):
    query = pl.BlockSpec((1, rows, GROUP * HEAD_DIM), lambda m, h: (m, 0, h))
    key = pl.BlockSpec((places, 1, rows, HEAD_DIM), lambda m, h: (0, m, 0, h))
    value = pl.BlockSpec((places, 1, rows, HEAD_DIM), lambda m, h: (0, m, 0, KV_HEADS + h))
    return pl.BlockSpec(memory_space=pltpu.SMEM), query, key, value


def attend(first, qkv, kv_all):
    micro, rows, _ = qkv.shape
    scalar, query, key, value = attention_specs(kv_all.shape[0], rows)
    return pl.pallas_call(
        attend_kernel,
        grid=(micro, KV_HEADS),
        out_shape=jax.ShapeDtypeStruct((micro, rows, HEADS * HEAD_DIM), BF),
        in_specs=[scalar, query, key, value],
        out_specs=query,
        compiler_params=pltpu.CompilerParams(vmem_limit_bytes=40 << 20),
        name="attend",
    )(first, qkv, kv_all, kv_all)


def attend_back(first, qkv, kv_all, grad):
    micro, rows, _ = qkv.shape
    scalar, query, key, value = attention_specs(kv_all.shape[0], rows)
    kv_out = jax.ShapeDtypeStruct((kv_all.shape[0], micro, rows, KV_HEADS * HEAD_DIM), BF)
    return pl.pallas_call(
        attend_back_kernel,
        grid=(micro, KV_HEADS),
        out_shape=[jax.ShapeDtypeStruct((micro, rows, HEADS * HEAD_DIM), BF), kv_out, kv_out],
        in_specs=[scalar, query, key, value, query],
        out_specs=[query, key, key],
        compiler_params=pltpu.CompilerParams(vmem_limit_bytes=56 << 20),
        name="attend_back",
    )(first, qkv, kv_all, kv_all, grad)


def nearest(n, place, k):
    value = jnp.int32(0)
    for i in range(n):
        for j, t in enumerate(sorted(range(n), key=lambda t: (abs(t - i), t))):
            if t:
                value = jnp.where(jnp.logical_and(place == i, k == j), t, value)
    return value


TILE = 1536


def tiles(total, body, size=TILE):
    def step(t, carry):
        body(pl.ds(pl.multiple_of(t * size, size), size))
        return carry

    lax.fori_loop(0, total // size, step, 0)


def dot_tn(left, right):
    return lax.dot_general(left, right, (((0,), (0,)), ((), ())), preferred_element_type=F32)


def dot_nt(left, right):
    return lax.dot_general(left, right, (((1,), (1,)), ((), ())), preferred_element_type=F32)


def expert_kernel(grid, micro, slots, *refs):
    (x_ref, table_ref, top_ref, gate_ref, up_ref, down_ref, in_ref, out_ref) = refs[:8]
    (x_all, table_all, mixed_ref, back_ref, gates_ref, taken_ref, grad_ref, acts_ref, shid_ref, spre_ref) = refs[8:18]
    (w_in, w_down, s_in, s_out, x_buf, d_buf, t_buf, mixed_out, back_out, taken, grad, acts, shid, spre, picked, turned, top_rows, scaled, rows_back) = refs[18:37]
    (ssem, rsem, osem, wsem, lsem, dsem, msem, esem, ssem2) = refs[37:]
    me = grid.here()
    line, place = grid.size["a"], me["a"]
    held, hidden_width, width = w_down.shape
    rows = table_ref.shape[1]
    tokens = micro * rows
    unit_tokens = 2 * tokens
    half_slots = micro * slots
    unit_slots = 2 * half_slots
    shared_part = s_out.shape[0]
    experts = table_ref.shape[0] // (2 * micro)
    first_held = (me["a"] * 2 + me["b"]) * held
    greet(grid, me, "ab")

    moves = [(in_ref, s_in), (out_ref, s_out)]
    for s in range(gate_ref.shape[0]):
        for e in range(held):
            at = pl.ds(s * gate_ref.shape[2], gate_ref.shape[2])
            moves.append((gate_ref.at[s, e], w_in.at[e, at, pl.ds(0, hidden_width)]))
            moves.append((up_ref.at[s, e], w_in.at[e, at, pl.ds(hidden_width, hidden_width)]))
            at = pl.ds(s * down_ref.shape[2], down_ref.shape[2])
            moves.append((down_ref.at[s, e], w_down.at[e, at]))
    fetches = [pltpu.make_async_copy(src, dst, wsem.at[i]) for i, (src, dst) in enumerate(moves)]
    own = me["a"] * 2 + me["b"]
    pairs = ((x_ref, x_all), (table_ref, table_all))
    keeps = [pltpu.make_async_copy(src, dst.at[own], osem.at[i]) for i, (src, dst) in enumerate(pairs)]

    def sends(a, mine=False):
        idx = a * 2 + me["b"]
        made = []
        for i, (src, dst) in enumerate(pairs):
            block = dst.at[idx]
            src = src if mine else block
            for j, (d, step) in enumerate((("a", 1), ("a", -1), ("b", 1))):
                cond = None
                if d == "a":
                    ahead = a <= place if step > 0 else a >= place
                    cond = jnp.logical_and(ahead, grid.valid(me, d, step))
                to = grid.device(grid.move(me, d, step))
                made.append((cond, remote(src, block, ssem.at[i, a, j], rsem.at[i, idx], to)))
        return made

    def arrived(idx):
        for i, (_, dst) in enumerate(pairs):
            block = dst.at[idx]
            to = grid.device(grid.move(me, "b", 1))
            remote(block, block, osem.at[i], rsem.at[i, idx], to).wait_recv()

    for cond, cp in sends(place, True):
        under(cond, cp.start)
    for cp in fetches + keeps:
        cp.start()

    def top_copy(k):
        a = nearest(line, place, k)
        at = lax.rem(k, 2)
        return pltpu.make_async_copy(top_ref.at[pl.ds(a * 2, 2)], d_buf.at[at], dsem.at[at])

    top_copy(0).start()
    gates_ref[...] = jnp.zeros_like(gates_ref)
    for cp in fetches:
        cp.wait()

    def out_copies(a):
        at = pl.ds(a * 2, 2)
        return (
            pltpu.make_async_copy(mixed_out, mixed_ref.at[at], msem.at[0]),
            pltpu.make_async_copy(back_out, back_ref.at[at], msem.at[1]),
            pltpu.make_async_copy(shid, shid_ref.at[a], msem.at[2]),
            pltpu.make_async_copy(spre, spre_ref.at[a], msem.at[3]),
        )

    def row_copies(e, k):
        return (
            pltpu.make_async_copy(taken.at[e], taken_ref.at[e, k], esem.at[e, 0]),
            pltpu.make_async_copy(grad.at[e], grad_ref.at[e, k], esem.at[e, 1]),
            pltpu.make_async_copy(acts.at[e], acts_ref.at[e, k], esem.at[e, 2]),
        )

    def unit(k, carry):
        a = nearest(line, place, k)
        for step in (1, -1):
            far = place - step * (k + 1)
            ok = far >= 0 if step > 0 else far < line

            def relay(far=far):
                arrived(far * 2 + me["b"])
                for cond, cp in sends(far):
                    under(cond, cp.start)

            pl.when(ok)(relay)
        pl.when(k + 1 < line)(lambda: top_copy(k + 1).start())
        arrived(a * 2 + 1 - me["b"])

        def fetch(near, far):
            copies = []
            for j, (b, sources) in enumerate(((me["b"], near), (1 - me["b"], far))):
                for i, (source, buf) in enumerate(zip(sources, (x_buf, t_buf))):
                    copies.append(pltpu.make_async_copy(source, buf.at[b], lsem.at[2 * j + i]))
            for cp in copies:
                cp.start()
            for cp in copies:
                cp.wait()

        other = a * 2 + 1 - me["b"]
        kept = a * 2 + me["b"]
        far = (x_all.at[other], table_all.at[other])
        pl.when(k == 0)(lambda: fetch((x_ref, table_ref), far))
        pl.when(k > 0)(lambda: fetch((x_all.at[kept], table_all.at[kept]), far))
        top_copy(k).wait()

        def leave():
            for cp in out_copies(a):
                cp.wait()

        pl.when(k > 0)(leave)
        x = x_buf.reshape(unit_tokens, width)
        top = d_buf.at[lax.rem(k, 2)].reshape(unit_tokens, width)

        def shared_rows(at):
            pre = jnp.dot(x[at, :], s_in[...], preferred_element_type=F32)
            silu, slope = silu_parts(pre[:, :shared_part])
            pre_up = pre[:, shared_part:]
            shid[at, :] = (silu * pre_up).astype(BF)
            mid_grad = dot_nt(top[at, :], s_out[...])
            spre[at, :shared_part] = (mid_grad * pre_up * slope).astype(BF)
            spre[at, shared_part:] = (mid_grad * silu).astype(BF)

        tiles(unit_tokens, shared_rows, 256)

        def expert(e, carry):
            def settle():
                for cp in row_copies(e, k):
                    cp.wait()

            pl.when(k > 0)(settle)
            gains = []
            for b in range(2):
                slot, gate = [], []
                for m in range(micro):
                    row = m * experts + first_held + e
                    one = t_buf[b, pl.ds(micro * experts + row, 1), :]
                    slot.append(jnp.where(one >= 0, one + m * slots, -1.0))
                    gate.append(t_buf[b, pl.ds(row, 1), :])
                slot = jnp.concatenate(slot, axis=1).astype(jnp.int32)
                named = lax.broadcasted_iota(jnp.int32, (half_slots, tokens), 0) == slot
                ones = named.astype(F32)
                picked[e, b] = ones.astype(BF)
                turned[e, b] = ones.T.astype(BF)
                gains.append(
                    jnp.sum(ones * jnp.concatenate(gate, axis=1), axis=1, keepdims=True)
                )
            gain = jnp.concatenate(gains, axis=0)

            def pick_rows(at):
                for b in range(2):
                    own = pl.ds(b * half_slots, half_slots)
                    of = pl.ds(b * tokens, tokens)
                    pick = picked[e, b]
                    taken[e, own, at] = jnp.dot(pick, x[of, at], preferred_element_type=F32).astype(BF)
                    got = jnp.dot(pick, top[of, at], preferred_element_type=F32)
                    top_rows[own, at] = got.astype(BF)
                    grad[e, own, at] = (gains[b] * got).astype(BF)

            tiles(width, pick_rows)
            pre = jnp.dot(taken[e], w_in[e], preferred_element_type=F32)
            hidden_grad = dot_nt(grad[e], w_down[e])
            silu, slope = silu_parts(pre[:, :hidden_width])
            pre_up = pre[:, hidden_width:]
            acts[e, :, :hidden_width] = (silu * pre_up).astype(BF)
            acts[e, :, hidden_width : 2 * hidden_width] = (hidden_grad * pre_up * slope).astype(BF)
            acts[e, :, 2 * hidden_width :] = (hidden_grad * silu).astype(BF)

            def leave_rows(t, gate_grad):
                at = pl.ds(pl.multiple_of(t * TILE, TILE), TILE)
                hidden = acts[e, :, :hidden_width]
                result = jnp.dot(hidden, w_down[e, :, at], preferred_element_type=F32)
                result = result.astype(BF).astype(F32)
                scaled[e, :, at] = (gain * result).astype(BF)
                product = top_rows[:, at].astype(F32) * result
                for c in range(0, TILE, 128):
                    gate_grad = gate_grad + product[:, c : c + 128]
                rows_back[e, :, at] = dot_nt(acts[e, :, hidden_width:], w_in[e, at, :]).astype(BF)
                return gate_grad

            gate_grad = lax.fori_loop(
                0, width // TILE, leave_rows, jnp.zeros((unit_slots, 128), F32)
            )
            gate_grad = jnp.sum(gate_grad, axis=1, keepdims=True)
            for b in range(2):
                spread = jnp.sum(
                    picked[e, b].astype(F32) * gate_grad[b * half_slots : (b + 1) * half_slots],
                    axis=0,
                    keepdims=True,
                )
                for m in range(micro):
                    row = m * experts + first_held + e
                    gates_ref[a * 2 + b, pl.ds(row, 1), :] = spread[:, m * rows : (m + 1) * rows]
            for cp in row_copies(e, k):
                cp.start()
            return carry

        lax.fori_loop(0, held, expert, 0)

        def combine(at):
            for b in range(2):
                own = pl.ds(b * half_slots, half_slots)
                of = pl.ds(b * tokens, tokens)
                mixed = jnp.dot(shid[of, :], s_out[:, at], preferred_element_type=F32)
                back = dot_nt(spre[of, :], s_in[at, :])
                for e in range(held):
                    turn = turned[e, b]
                    mixed += jnp.dot(turn, scaled[e, own, at], preferred_element_type=F32)
                    back += jnp.dot(turn, rows_back[e, own, at], preferred_element_type=F32)
                mixed_out[b, :, at] = mixed.astype(BF)
                back_out[b, :, at] = back.astype(BF)

        tiles(width, combine)
        for cp in out_copies(a):
            cp.start()
        return carry

    lax.fori_loop(0, line, unit, 0)
    for cp in out_copies(0):
        cp.wait()
    for e in range(held):
        for cp in row_copies(e, 0):
            cp.wait()
    for cp in keeps:
        cp.wait()
    for a in range(line):
        for cond, cp in sends(a):
            under(cond, cp.wait_send)


def run_experts(grid, micro, slots, x, table, tops, w_gate, w_up, w_down, s_in, s_out, collective_id):
    line = grid.size["a"]
    blocks = 2 * line
    tokens, width = x.shape
    seq, held, _, hidden_width = w_gate.shape
    unit_tokens, unit_slots = 2 * tokens, 2 * micro * slots
    shared_part = s_out.shape[0]
    any_spec, vmem = pl.BlockSpec(memory_space=pl.ANY), pl.BlockSpec(memory_space=pltpu.VMEM)
    shape = jax.ShapeDtypeStruct
    dma = pltpu.SemaphoreType.DMA
    return pl.pallas_call(
        functools.partial(expert_kernel, grid, micro, slots),
        out_shape=[
            shape((blocks, tokens, width), BF),
            shape((blocks,) + table.shape, F32),
            shape((blocks, tokens, width), BF),
            shape((blocks, tokens, width), BF),
            shape((blocks, table.shape[0] // 2, table.shape[1]), F32),
            shape((held, line, unit_slots, width), BF),
            shape((held, line, unit_slots, width), BF),
            shape((held, line, unit_slots, 3 * hidden_width), BF),
            shape((line, unit_tokens, shared_part), BF),
            shape((line, unit_tokens, 2 * shared_part), BF),
        ],
        in_specs=[vmem] * 2 + [any_spec] * 6,
        out_specs=[any_spec] * 4 + [vmem] + [any_spec] * 5,
        scratch_shapes=[
            pltpu.VMEM((held, width, 2 * hidden_width), BF),
            pltpu.VMEM((held, hidden_width, width), BF),
            pltpu.VMEM(s_in.shape, BF),
            pltpu.VMEM(s_out.shape, BF),
            pltpu.VMEM((2, tokens, width), BF),
            pltpu.VMEM((2, 2, tokens, width), BF),
            pltpu.VMEM((2,) + table.shape, F32),
            pltpu.VMEM((2, tokens, width), BF),
            pltpu.VMEM((2, tokens, width), BF),
            pltpu.VMEM((held, unit_slots, width), BF),
            pltpu.VMEM((held, unit_slots, width), BF),
            pltpu.VMEM((held, unit_slots, 3 * hidden_width), BF),
            pltpu.VMEM((unit_tokens, shared_part), BF),
            pltpu.VMEM((unit_tokens, 2 * shared_part), BF),
            pltpu.VMEM((held, 2, micro * slots, tokens), BF),
            pltpu.VMEM((held, 2, tokens, micro * slots), BF),
            pltpu.VMEM((unit_slots, width), BF),
            pltpu.VMEM((held, unit_slots, width), BF),
            pltpu.VMEM((held, unit_slots, width), BF),
            dma((2, line, 3)),
            dma((2, blocks)),
            dma((2,)),
            dma((3 * held * seq + 2,)),
            dma((4,)),
            dma((2,)),
            dma((4,)),
            dma((held, 3)),
            dma((1,)),
        ],
        compiler_params=pltpu.CompilerParams(
            collective_id=collective_id, has_side_effects=True, vmem_limit_bytes=56 << 20
        ),
        name="experts",
    )(x, table, tops, w_gate, w_up, w_down, s_in, s_out)


def return_kernel(grid, plan, micro, *refs):
    ins, outs, refs = refs[:8], refs[8:16], refs[16:]
    taken_ref, grad_ref, acts_ref = ins[5:]
    taken, grad, acts, fsem = refs[:4]
    me = grid.here()
    plan.bind(me, ins[:5], outs, refs[4:])
    held = taken_ref.shape[0]
    hidden_width = acts.shape[1] // 3

    def loads(e):
        return [
            pltpu.make_async_copy(src.at[e], dst, fsem.at[j])
            for j, (src, dst) in enumerate(((taken_ref, taken), (acts_ref, acts), (grad_ref, grad)))
        ]

    for cp in loads(0):
        cp.start()
    greet(grid, me, "abxc")

    def product(left, first, right, total, acc):
        block = acc.shape[1]
        chunk = math.lcm(block, 128)

        def step(t, carry):
            at = pl.ds(pl.multiple_of(first + t * chunk, 128), chunk)
            value = dot_tn(left[:, at], right).astype(BF)
            for q in range(chunk // block):
                acc[t * (chunk // block) + q] = value[q * block : (q + 1) * block]
            return carry

        lax.fori_loop(0, total // chunk, step, 0)

    def fill(e):
        for cp in loads(e):
            cp.wait()
        product(taken, 0, acts[:, hidden_width:], taken.shape[1], plan.accs[9 + 2 * e])
        product(acts, 0, grad[...], hidden_width, plan.accs[10 + 2 * e])
        if e + 1 < held:
            for cp in loads(e + 1):
                cp.start()

    plan.run([(0.04 + 1.05 * e, functools.partial(fill, e)) for e in range(held)])


def return_tokens(grid, micro, mixed, back, gates, shared_in, shared_out, taken, grad, acts, collective_id):
    held, _, width = taken.shape
    hidden_width = acts.shape[2] // 3
    seq = grid.size["x"] * 2
    rows = mixed.shape[1]
    cuts = [0] + [16 * (rows * n // 8 // 16) for n in (1, 3, 5)] + [rows]
    parts = []
    for k in (1, 2, 3, 0):
        for i, x in enumerate((mixed, back)):
            way = ("ba", "ba") if k else ("ab", "ab")
            size, whole = cuts[k + 1] - cuts[k], [(i, None, 0, x.shape[2])]
            parts.append(Part(way, x.shape[0], size, x.shape[2], BF, i, whole, row=cuts[k]))
    parts.append(Part(("ba", "ba"), *gates.shape, F32, 2, [(2, None, 0, gates.shape[2])]))
    for e in range(held):
        ready = (0.041 + 1.05 * e, 0.06 + 1.05 * e, 0.07 + 1.05 * e, 2.6 + 2 * e)
        rows = width // seq
        ways = [(5, e, 0, hidden_width), (6, e, hidden_width, hidden_width)]
        parts.append(Part(("cx", "cx"), seq, rows, 2 * hidden_width, BF, None, ways, ready=ready))
        rows = hidden_width // seq
        parts.append(Part(("cx", "cx"), seq, rows, width, BF, None, [(7, e, 0, width)], ready=ready))
    for i, x in enumerate((shared_in, shared_out)):
        parts.append(
            Part(("cx", "cx"), seq, x.shape[1], x.shape[2], BF, 3 + i, [(3 + i, None, 0, x.shape[2])])
        )
    plan = Scatter(grid, parts)
    shape = jax.ShapeDtypeStruct
    dma = pltpu.SemaphoreType.DMA
    return pl.pallas_call(
        functools.partial(return_kernel, grid, plan, micro),
        out_shape=[
            shape(mixed.shape[1:], F32),
            shape(back.shape[1:], F32),
            shape(gates.shape[1:], F32),
            shape(shared_in.shape[1:], BF),
            shape(shared_out.shape[1:], F32),
            shape((held, width // seq, hidden_width), F32),
            shape((held, width // seq, hidden_width), F32),
            shape((held, hidden_width // seq, width), F32),
        ],
        in_specs=[pl.BlockSpec(memory_space=pl.ANY)] * 8,
        out_specs=[pl.BlockSpec(memory_space=pltpu.VMEM)] * 8,
        scratch_shapes=[
            pltpu.VMEM(taken.shape[1:], BF),
            pltpu.VMEM(grad.shape[1:], BF),
            pltpu.VMEM(acts.shape[1:], BF),
            dma((3,)),
        ]
        + plan.scratch(),
        compiler_params=pltpu.CompilerParams(
            collective_id=collective_id, has_side_effects=True, vmem_limit_bytes=62 << 20
        ),
        name="return_tokens",
    )(mixed, back, gates, shared_in, shared_out, taken, grad, acts)


def per_device(
    block_input,
    norm_attn,
    w_query,
    w_key,
    w_value,
    w_out,
    norm_ffn,
    w_router,
    shared_gate,
    shared_up,
    shared_down,
    expert_gate,
    expert_up,
    expert_down,
    routes,
    out_grad,
):
    micro, _, rows, width = block_input.shape
    tokens = micro * rows
    experts = w_router.shape[1]
    held = expert_gate.shape[0]
    exp_size, seq_size = lax.axis_size("exp"), lax.axis_size("seq")
    blocks = exp_size * seq_size
    grid = Grid(exp_size, seq_size)
    slots = min(rows, 8 * ((3 * rows * TOPK // (2 * experts) + 7) // 8))
    query_width = HEADS * HEAD_DIM
    kv_width = KV_HEADS * HEAD_DIM
    qkv_width = query_width + 2 * kv_width
    own_rows = w_query.shape[0]
    shared_part = shared_gate.shape[1] // exp_size
    first = (lax.axis_index("seq") * rows).astype(jnp.int32).reshape(1)

    small = jnp.concatenate([norm_attn[:, None], norm_ffn[:, None], w_router], axis=1)
    small = jnp.pad(small, ((0, 0), (0, 128 - small.shape[1])))
    halves = jnp.concatenate(
        [
            shared_gate.reshape(own_rows, exp_size, shared_part),
            shared_up.reshape(own_rows, exp_size, shared_part),
        ],
        axis=2,
    ).transpose(1, 0, 2)
    route = ("abxc", "axbc" if seq_size == 4 else "abxc")
    along, across = ("ab", "ab"), ("xc", "xc")
    turned = 16 * (tokens * 3 // 8 // 16)
    (qkv_full, out_full, small_full, grads_all, shared_out, shared_in, gate_all, up_all, down_all) = gather(
        grid,
        [
            jnp.concatenate([w_query, w_key, w_value], axis=1),
            w_out,
            small,
            out_grad.reshape(tokens, width),
            shared_down,
            halves,
            expert_gate,
            expert_up,
            expert_down,
        ],
        [Item(i, route) for i in range(3)]
        + [
            Item(3, along, (turned, tokens - turned)),
            Item(3, ("ba", "ba"), (0, turned)),
            Item(4, across),
            Item(5, across, spread=True),
        ]
        + [Item(i, across, late=10) for i in (6, 7, 8)],
        1,
        "gather_first",
    )
    shared_out = shared_out.reshape(shared_part, width)
    shared_in = shared_in.reshape(width, 2 * shared_part)
    qkv_full = qkv_full.reshape(width, qkv_width)
    out_full = out_full.reshape(query_width, width)
    small_full = small_full.reshape(width, 128)
    gain_one = small_full[:, 0].astype(F32)
    gain_two = small_full[:, 1].astype(F32)
    router_full = small_full[:, 2 : 2 + experts]

    hidden_in = block_input.reshape(tokens, width).astype(F32)
    inverse_one = inverse_rms(hidden_in)
    normed_one = (hidden_in * inverse_one * gain_one).astype(BF)
    qkv = matmul(normed_one, qkv_full).astype(BF)
    (kv_all,) = gather(grid, [qkv[:, query_width:]], [Item(0, across)], 2, "gather_kv")
    kv_all = kv_all.reshape(seq_size, micro, rows, 2 * kv_width)
    qkv = qkv.reshape(micro, rows, qkv_width)
    attended = attend(first, qkv, kv_all).reshape(tokens, query_width)
    hidden_mid = hidden_in + matmul(attended, out_full)
    inverse_two = inverse_rms(hidden_mid)
    normed_two = (hidden_mid * inverse_two * gain_two).astype(BF)

    route_rows = routes.reshape(tokens, TOPK)
    named = route_rows[:, :, None] == jnp.arange(experts, dtype=jnp.int32)
    chosen = jnp.any(named, axis=1)
    logits = matmul(normed_two, router_full)
    masked = jnp.where(chosen, logits, -jnp.inf)
    powers = jnp.exp(masked - jnp.max(masked, axis=-1, keepdims=True))
    gates = powers / jnp.sum(powers, axis=-1, keepdims=True)
    member = chosen.reshape(micro, rows, experts).astype(jnp.int32)
    rank = jnp.cumsum(member, axis=1) - member
    slot = jnp.where(member > 0, rank, -1).astype(F32)

    def by_expert(table):
        return table.reshape(micro, rows, experts).transpose(0, 2, 1).reshape(micro * experts, rows)

    table = jnp.concatenate([by_expert(gates), by_expert(slot)], axis=0)
    inputs_all, _, mixed, back, gate_table, taken, taken_grad, acts, shared_hidden, shared_pre = run_experts(
        grid, micro, slots, normed_two, table, grads_all, gate_all, up_all, down_all, shared_in, shared_out, 3
    )
    flat = inputs_all.reshape(exp_size * tokens, width)
    flat_top = grads_all.reshape(exp_size * tokens, width)
    shared_in_term = left_product(flat, shared_pre.reshape(-1, 2 * shared_part)).astype(BF)
    shared_out_term = left_product(shared_hidden.reshape(-1, shared_part), flat_top).astype(BF)
    hidden_width = expert_gate.shape[2]
    taken = taken.reshape(held, -1, width)
    taken_grad = taken_grad.reshape(held, -1, width)
    acts = acts.reshape(held, -1, 3 * hidden_width)
    shared_in_term = shared_in_term.reshape(exp_size, seq_size, own_rows, 2 * shared_part)
    (
        mixture,
        token_grad,
        gate_grad,
        halves,
        shared_down_grad,
        expert_gate_grad,
        expert_up_grad,
        expert_down_grad,
    ) = return_tokens(
        grid,
        micro,
        mixed,
        back,
        gate_table,
        shared_in_term.transpose(1, 0, 2, 3).reshape(seq_size, exp_size * own_rows, 2 * shared_part),
        shared_out_term.reshape(seq_size, shared_part // seq_size, width),
        taken,
        taken_grad,
        acts,
        4,
    )
    halves = halves.reshape(exp_size, own_rows, 2 * shared_part)

    block_output = (hidden_mid + mixture).astype(BF).reshape(block_input.shape)

    gate_grad = gate_grad.reshape(micro, experts, rows).transpose(0, 2, 1).reshape(tokens, experts)
    logit_grad = gates * (gate_grad - jnp.sum(gates * gate_grad, axis=-1, keepdims=True))
    logit_grad = logit_grad.astype(BF)
    grad_top = out_grad.reshape(tokens, width).astype(F32)
    normed_two_grad = token_grad + right_product(logit_grad, router_full)
    mid_part, norm_two_term = norm_back(normed_two_grad, hidden_mid, inverse_two, gain_two)
    mid_grad = mid_part + grad_top
    attn_grad = mid_grad.astype(BF)
    attended_grad = right_product(attn_grad, out_full).astype(BF)
    query_grad, key_part, value_part = attend_back(
        first, qkv, kv_all, attended_grad.reshape(micro, rows, query_width)
    )
    key_grad, value_grad = scatter(
        grid,
        [
            key_part.reshape(seq_size, tokens, kv_width),
            value_part.reshape(seq_size, tokens, kv_width),
        ],
        [("cx", "cx")] * 2,
        [BF] * 2,
        5,
        "scatter_kv",
    )
    qkv_grad = jnp.concatenate(
        [query_grad.reshape(tokens, query_width), key_grad, value_grad], axis=1
    )
    halves, qkv_grad = lax.optimization_barrier((halves, qkv_grad))
    halves = lax.all_to_all(halves, "exp", split_axis=0, concat_axis=0, tiled=True).astype(F32)
    halves = halves.transpose(1, 0, 2)
    shared_gate_grad = halves[:, :, :shared_part].reshape(own_rows, exp_size * shared_part)
    shared_up_grad = halves[:, :, shared_part:].reshape(own_rows, exp_size * shared_part)
    normed_one_grad = right_product(qkv_grad, qkv_full)
    in_part, norm_one_term = norm_back(normed_one_grad, hidden_in, inverse_one, gain_one)
    input_grad = (in_part + mid_grad).reshape(block_input.shape)
    small_term = jnp.concatenate(
        [norm_one_term[:, None], norm_two_term[:, None], left_product(normed_two, logit_grad)],
        axis=1,
    )
    small_term = jnp.pad(small_term, ((0, 0), (0, 128 - small_term.shape[1])))
    order = ("cxba", "cbxa" if seq_size == 4 else "cxba")
    qkv_share, out_share, small_share = scatter(
        grid,
        [
            left_product(normed_one, qkv_grad).astype(BF).reshape(blocks, own_rows, qkv_width),
            left_product(attended, attn_grad).astype(BF).reshape(blocks, own_rows, width),
            small_term.reshape(blocks, own_rows, 128),
        ],
        [order] * 3,
        [F32] * 3,
        6,
        "scatter_dense",
    )
    return (
        block_output,
        input_grad,
        small_share[:, 0],
        qkv_share[:, :query_width],
        qkv_share[:, query_width : query_width + kv_width],
        qkv_share[:, query_width + kv_width :],
        out_share,
        small_share[:, 1],
        small_share[:, 2 : 2 + experts],
        shared_gate_grad,
        shared_up_grad,
        shared_down_grad,
        expert_gate_grad,
        expert_up_grad,
        expert_down_grad,
    )


def solution(mesh):
    tokens = P(None, "exp", "seq", None)
    vector, matrix = P(("exp", "seq")), P(("exp", "seq"), None)
    stack = P("exp", "seq", None)
    weights = (vector,) + (matrix,) * 4 + (vector,) + (matrix,) * 4 + (stack,) * 3
    return jax.shard_map(
        per_device,
        mesh=mesh,
        in_specs=(tokens,) + weights + (tokens, tokens),
        out_specs=(tokens, tokens) + weights,
        check_vma=False,
    )
```

```python
import functools
import itertools
import math

import jax
import jax.numpy as jnp
from jax import lax
from jax.experimental import pallas as pl
from jax.experimental.pallas import tpu as pltpu
from jax.sharding import PartitionSpec as P

MESH = pl.DeviceIdType.MESH
CANON = "abxc"


class Grid:
    def __init__(self, exp_size, seq_size):
        self.size = {"a": exp_size // 2, "b": 2, "x": seq_size // 2, "c": 2}

    def here(self):
        e = lax.axis_index("exp")
        s = lax.axis_index("seq")
        return {"a": lax.div(e, 2), "b": lax.rem(e, 2), "x": lax.div(s, 2), "c": lax.rem(s, 2)}

    def device(self, pos):
        return (pos["a"] * 2 + pos["b"], pos["x"] * 2 + pos["c"])

    def index(self, pos, dims):
        number = 0
        for d in CANON:
            if d in dims:
                number = number * self.size[d] + pos[d]
        return number

    def count(self, dims):
        return math.prod(self.size[d] for d in dims)

    def offsets(self, d):
        n = self.size[d]
        return (0, 1) if n == 2 else tuple(range(-(n - 1), n))

    def move(self, pos, d, off):
        new = dict(pos)
        if off:
            new[d] = 1 - pos[d] if self.size[d] == 2 else pos[d] + off
        return new

    def valid(self, pos, d, off):
        if off == 0 or self.size[d] == 2:
            return None
        return pos[d] + off >= 0 if off < 0 else pos[d] + off < self.size[d]

    def steps(self, d):
        if self.size[d] == 1:
            return ()
        return (1,) if self.size[d] == 2 else (1, -1)


def both(*conds):
    conds = [c for c in conds if c is not None]
    return functools.reduce(jnp.logical_and, conds) if conds else None


def under(cond, body):
    if cond is None:
        body()
    else:
        pl.when(cond)(body)


def greet(grid, me, dims, total=0):
    bar = pltpu.get_barrier_semaphore()
    for d in dims:
        for step in grid.steps(d):
            ok = grid.valid(me, d, step)

            def signal(d=d, step=step):
                pl.semaphore_signal(
                    bar, inc=1, device_id=grid.device(grid.move(me, d, step)), device_id_type=MESH
                )

            under(ok, signal)
            total = total + (1 if ok is None else ok.astype(jnp.int32))
    pl.semaphore_wait(bar, total)


def remote(src, dst, ssem, rsem, device):
    return pltpu.make_async_remote_copy(
        src_ref=src, dst_ref=dst, send_sem=ssem, recv_sem=rsem, device_id=device, device_id_type=MESH
    )


def gather_plan(grid, orders):
    dims = orders[0]
    events = []
    for combo in itertools.product(*[grid.offsets(d) for d in dims]):
        off = dict(zip(dims, combo))
        sends = []
        for order in orders:
            last = max([k for k, d in enumerate(order) if off[d]], default=-1)
            mine = []
            if last >= 0 and grid.size[order[last]] > 2:
                mine.append((order[last], 1 if off[order[last]] < 0 else -1))
            for d in order[last + 1 :]:
                mine.extend((d, step) for step in grid.steps(d))
            sends.append(mine)
        events.append((sum(abs(v) for v in combo), off, sends))
    events.sort(key=lambda ev: ev[0])
    return events


class Item:
    def __init__(self, array, orders, rows=None, late=0, spread=False, start=0):
        self.array, self.orders, self.rows, self.late, self.spread = array, orders, rows, late, spread
        self.start = start

    def blocks(self, grid):
        return grid.count("abxc" if self.spread else self.orders[0])


def gather_kernel(grid, items, count, *refs):
    srcs, dsts = refs[:count], refs[count : 2 * count]
    ssem, rsem, lsem = refs[2 * count :]
    me = grid.here()
    own = me["a"] * 2 + me["b"]
    exp_size, seq_size = grid.count("ab"), grid.count("xc")
    others = [lax.rem(own + j, exp_size) for j in range(1, exp_size)]
    here = (me["x"] * 2 + me["c"]).astype(jnp.int32)
    wide = any(item.spread for item in items)
    used = "".join(d for d in CANON if any(d in item.orders[0] for item in items))
    if wide:
        greet_wide(grid, me)
    else:
        greet(grid, me, used)
    base, total = [], 0
    for item in items:
        base.append(total)
        total += item.blocks(grid)
    waits, slot, merged = [], 0, []
    for i, item in enumerate(items):
        plan = gather_plan(grid, item.orders)
        for j in range(exp_size if item.spread else 1):
            for hops, off, sends in plan:
                time = hops + item.late * (hops > 0) + item.start + (1.5 if j else 0)
                merged.append((time, i, j, hops, off, sends))
        if item.spread:
            src, dst = srcs[item.array], dsts[item.array]
            mine = own * seq_size + here
            for e in others:
                cp = remote(src.at[e], dst.at[mine], ssem.at[slot], rsem.at[base[i] + mine], (e, here))
                cp.start()
                waits.append((None, cp.wait_send))
                slot += 1
    merged.sort(key=lambda ev: ev[:3])
    for time, i, j, hops, off, sends in merged:
        item = items[i]
        dims = item.orders[0]
        pos, conds = me, []
        for d in dims:
            conds.append(grid.valid(me, d, off[d]))
            pos = grid.move(pos, d, off[d])
        ok = both(*conds)
        idx = grid.index(pos, dims)
        if item.spread:
            idx = (own if j == 0 else others[j - 1]) * seq_size + idx
        sem = rsem.at[base[i] + idx]
        block, src = dsts[item.array].at[idx], srcs[item.array]
        if item.spread:
            src = src.at[own]
        if item.rows is not None:
            block, src = block.at[pl.ds(*item.rows)], src.at[pl.ds(*item.rows)]
        first = hops == 0 and j == 0
        if not first:
            src = block
        plan = []
        for d, step in sorted(set(sends[0]) | set(sends[1])):
            side = None
            if (d, step) not in sends[0]:
                side = me["c"] == 1
            elif (d, step) not in sends[1]:
                side = me["c"] == 0
            cp = remote(src, block, ssem.at[slot], sem, grid.device(grid.move(me, d, step)))
            plan.append((both(grid.valid(me, d, step), side), cp))
            slot += 1

        def arrive(first=first, i=i, src=src, block=block, sem=sem, plan=plan):
            if first:
                pltpu.make_async_copy(src, block, lsem.at[i]).start()
            else:
                to = grid.device(grid.move(me, used[-1], 1))
                remote(block, block, lsem.at[i], sem, to).wait_recv()
            for cond, cp in plan:
                under(cond, cp.start)

        def finish(first=first, i=i, src=src, block=block, plan=plan):
            if first:
                pltpu.make_async_copy(src, block, lsem.at[i]).wait()
            for cond, cp in plan:
                under(cond, cp.wait_send)

        under(ok, arrive)
        waits.append((ok, finish))
    for ok, finish in waits:
        under(ok, finish)


def count_sends(grid, item):
    plan = gather_plan(grid, item.orders)
    sends = sum(len(set(ev[2][0]) | set(ev[2][1])) for ev in plan)
    exp_size = grid.count("ab")
    return sends * exp_size + exp_size - 1 if item.spread else sends


def greet_wide(grid, me):
    bar = pltpu.get_barrier_semaphore()
    own = me["a"] * 2 + me["b"]
    exp_size = grid.count("ab")
    for j in range(1, exp_size):
        to = (lax.rem(own + j, exp_size), me["x"] * 2 + me["c"])
        pl.semaphore_signal(bar, inc=1, device_id=to, device_id_type=MESH)
    greet(grid, me, "xc", exp_size - 1)


def gather(grid, arrays, items, collective_id, name, near=()):
    shapes = {}
    for item in items:
        x = arrays[item.array]
        shapes[item.array] = (item.blocks(grid),) + (x.shape[1:] if item.spread else x.shape)
    return pl.pallas_call(
        functools.partial(gather_kernel, grid, items, len(arrays)),
        out_shape=[jax.ShapeDtypeStruct(shapes[i], x.dtype) for i, x in enumerate(arrays)],
        in_specs=[pl.BlockSpec(memory_space=pltpu.VMEM)] * len(arrays),
        out_specs=[
            pl.BlockSpec(memory_space=pltpu.VMEM if i in near else pl.ANY) for i in range(len(arrays))
        ],
        scratch_shapes=[
            pltpu.SemaphoreType.DMA((sum(count_sends(grid, item) for item in items),)),
            pltpu.SemaphoreType.DMA((sum(item.blocks(grid) for item in items),)),
            pltpu.SemaphoreType.DMA((len(items),)),
        ],
        compiler_params=pltpu.CompilerParams(
            collective_id=collective_id, has_side_effects=True, vmem_limit_bytes=32 << 20
        ),
        name=name,
    )(*arrays)


class Part:
    def __init__(self, orders, blocks, rows, columns, dtype, source, outputs, row=0, ready=None):
        self.orders, self.blocks, self.rows, self.columns = orders, blocks, rows, columns
        self.dtype, self.source, self.outputs, self.row, self.ready = dtype, source, outputs, row, ready
        self.step = min(16, rows)

    def size(self):
        return -(-self.rows // 16) * 16 * self.columns * jnp.dtype(self.dtype).itemsize

    def kept(self, grid):
        half = self.source is not None and grid.size[self.orders[0][0]] == 2
        return self.blocks // 2 if half else self.blocks

    def place(self, grid, pos, order):
        half = self.source is not None and grid.size[order[0]] == 2
        return grid.index(pos, order[1:] if half else order)

    def inbox(self, grid, stage):
        return max(
            (1 if grid.size[o[stage]] == 2 else grid.size[o[stage]] + 1) * grid.count(o[stage + 1 :])
            for o in self.orders
        )


def scatter_plan(grid, part, order):
    lead = order[-1]
    span = grid.size[lead]
    events = []
    for stage, d in enumerate(order):
        rest = order[stage:]
        for combo in itertools.product(*[grid.offsets(r) for r in rest]):
            off = dict(zip(rest, combo))
            time = span - 1 - abs(off[lead]) + stage - (1.5 if d == "c" else 0)
            first = 0 if off[d] else 1
            if order == "ab":
                time = -5 - 0.1 * abs(off["a"]) if stage == 0 else (3.5 if first else -4)
            if part.ready is not None:
                time = part.ready[2 * min(stage, 1) + first]
            elif stage == 0 and grid.size[d] == 2 and off[d]:
                time -= 100
            events.append((time, -stage, first, off))
    events.sort(key=lambda ev: ev[:3])
    return events


class Scatter:
    def __init__(self, grid, parts):
        self.grid, self.parts = grid, parts
        self.base, blocks, sends, slots = [], 0, 0, 0
        for part in parts:
            stages = []
            for stage in range(len(part.orders[0])):
                stages.append(slots)
                slots += part.inbox(grid, stage)
            self.base.append((blocks, sends, stages))
            blocks += part.kept(grid)
            sends += part.blocks
        self.totals = (blocks, sends, slots)

    def scratch(self):
        dma = pltpu.SemaphoreType.DMA
        out = [pltpu.VMEM((p.kept(self.grid), p.rows, p.columns), p.dtype) for p in self.parts]
        for p in self.parts:
            for stage in range(len(p.orders[0])):
                out.append(pltpu.VMEM((p.inbox(self.grid, stage), p.rows, p.columns), p.dtype))
        return out + [dma((n,)) for n in self.totals]

    def bytes(self):
        return sum(
            p.size() * (p.kept(self.grid) + sum(p.inbox(self.grid, k) for k in range(len(p.orders[0]))))
            for p in self.parts
        )

    def bind(self, me, srcs, outs, refs):
        self.me, self.srcs, self.outs = me, srcs, outs
        count = len(self.parts)
        self.accs, refs = refs[:count], refs[count:]
        self.inboxes = []
        for p in self.parts:
            n = len(p.orders[0])
            self.inboxes.append(refs[:n])
            refs = refs[n:]
        self.lsem, self.ssem, self.rsem = refs

    def run(self, fills=()):
        grid, me = self.grid, self.me
        if all(p.orders[0] == p.orders[1] for p in self.parts):
            self.run_side(0, fills)
        else:
            for side in (0, 1):
                pl.when(me["c"] == side)(functools.partial(self.run_side, side, fills))

    def owner(self, order, off):
        pos, conds = self.me, []
        for d in order:
            conds.append(self.grid.valid(self.me, d, off[d]))
            pos = self.grid.move(pos, d, off[d])
        return pos, both(*conds)

    def run_side(self, side, fills):
        grid = self.grid
        todo, self.waits = [], []
        for i, part in enumerate(self.parts):
            order = part.orders[side]
            for time, minus, first, off in scatter_plan(grid, part, order):
                stage = -minus
                todo.append((time, minus, first, functools.partial(self.event, i, order, stage, off)))
                if stage == 0 and part.source is not None:
                    if off[order[0]] == 0 or grid.size[order[0]] > 2:
                        self.fetch(i, order, off)
        for time, fill in fills:
            todo.append((time, -99, 0, fill))
        todo.sort(key=lambda ev: ev[:3])
        for _, _, _, act in todo:
            act()
        for ok, cp in self.waits:
            under(ok, cp.wait_send)

    def load(self, i, pos, order):
        part = self.parts[i]
        idx, at = self.grid.index(pos, order), part.place(self.grid, pos, order)
        return pltpu.make_async_copy(
            self.source(i, idx), self.accs[i].at[at], self.lsem.at[self.base[i][0] + at]
        )

    def source(self, i, idx):
        part = self.parts[i]
        whole = self.srcs[part.source]
        if part.rows == whole.shape[1]:
            return whole.at[idx]
        return whole.at[idx, pl.ds(part.row, part.rows)]

    def fetch(self, i, order, off):
        pos, ok = self.owner(order, off)
        under(ok, self.load(i, pos, order).start)

    def event(self, i, order, stage, off):
        grid, me, part = self.grid, self.me, self.parts[i]
        acc, inbox = self.accs[i], self.inboxes[i][stage]
        _, send_base, inbox_base = self.base[i]
        d = order[stage]
        n = grid.size[d]
        later = order[stage + 1 :]
        pos, ok = self.owner(order[stage:], off)
        idx, at = grid.index(pos, order), part.place(grid, pos, order)
        last = stage == len(order) - 1

        def box(line_slot):
            tail = grid.index(pos, later)
            k = tail if n == 2 else line_slot * grid.count(later) + tail
            return inbox.at[k], self.rsem.at[inbox_base[stage] + k]

        def take(line_slot):
            ref, sem = box(line_slot)
            other = grid.device(grid.move(me, d, 1) if n == 2 else grid.move(me, order[0], 1))
            remote(ref, ref, self.ssem.at[0], sem, other).wait_recv()
            return ref

        def rows(body):
            def step(r, carry):
                body(pl.ds(pl.multiple_of(r * part.step, part.step), part.step))
                return carry

            lax.fori_loop(0, part.rows // part.step, step, 0)

        def add(ref):
            def body(r):
                acc[at, r, :] = (acc[at, r, :].astype(jnp.float32) + ref[r, :].astype(jnp.float32)).astype(
                    acc.dtype
                )

            rows(body)

        def close(refs):
            def body(r):
                total = acc[at, r, :].astype(jnp.float32)
                for ref in refs:
                    total = total + ref[r, :].astype(jnp.float32)
                for out, lead, first, count in part.outputs:
                    target = self.outs[out] if lead is None else self.outs[out].at[lead]
                    to = pl.ds(part.row + r.start, part.step)
                    target[to, :] = total[:, first : first + count].astype(target.dtype)

            rows(body)

        def ready():
            if stage == 0 and part.source is not None:
                self.load(i, pos, order).wait()

        def send(src, step, line_slot):
            ref, sem = box(line_slot)
            to = grid.device(grid.move(me, d, step))
            return remote(src, ref, self.ssem.at[send_base + idx], sem, to)

        if n == 2 and off[d]:
            direct = stage == 0 and part.source is not None
            cp = send(self.source(i, idx) if direct else acc.at[at], 1, 0)
            under(ok, cp.start)
            self.waits.append((ok, cp))
        elif n == 2:

            def merge():
                ready()
                ref = take(0)
                if last:
                    close([ref])
                else:
                    add(ref)

            under(ok, merge)
        elif off[d]:
            back = -1 if off[d] > 0 else 1
            has_back = grid.valid(me, d, back)
            to_slot = pos[d] if back < 0 else jnp.where(pos[d] == me[d] - 1, n, pos[d])
            cp = send(acc.at[at], -back, to_slot)

            def pass_on():
                ready()
                pl.when(has_back)(lambda: add(take(pos[d])))
                cp.start()

            under(ok, pass_on)
            self.waits.append((ok, cp))
        else:

            def collect():
                ready()
                low, high = grid.valid(me, d, -1), grid.valid(me, d, 1)
                if not last:
                    pl.when(low)(lambda: add(take(me[d])))
                    pl.when(high)(lambda: add(take(n)))
                    return
                pl.when(jnp.logical_and(low, high))(lambda: close([take(me[d]), take(n)]))
                pl.when(me[d] == 0)(lambda: close([take(n)]))
                pl.when(me[d] == n - 1)(lambda: close([take(me[d])]))

            under(ok, collect)


def scatter_kernel(grid, plan, count, outs, *refs):
    me = grid.here()
    plan.bind(me, refs[:count], refs[count : count + outs], refs[count + outs :])
    greet(grid, me, "".join(d for d in CANON if any(d in p.orders[0] for p in plan.parts)))
    plan.run()


def scatter(grid, arrays, orders, out_types, collective_id, name):
    parts = [
        Part(o, x.shape[0], x.shape[1], x.shape[2], x.dtype, i, [(i, None, 0, x.shape[2])])
        for i, (x, o) in enumerate(zip(arrays, orders))
    ]
    plan = Scatter(grid, parts)
    outs = sum(4 * p.size() // jnp.dtype(p.dtype).itemsize for p in parts)
    return pl.pallas_call(
        functools.partial(scatter_kernel, grid, plan, len(arrays), len(arrays)),
        out_shape=[jax.ShapeDtypeStruct(x.shape[1:], t) for x, t in zip(arrays, out_types)],
        in_specs=[pl.BlockSpec(memory_space=pl.ANY)] * len(arrays),
        out_specs=[pl.BlockSpec(memory_space=pltpu.VMEM)] * len(arrays),
        scratch_shapes=plan.scratch(),
        compiler_params=pltpu.CompilerParams(
            collective_id=collective_id, has_side_effects=True, vmem_limit_bytes=plan.bytes() + 2 * outs + (4 << 20)
        ),
        name=name,
    )(*arrays)


HEADS = 12
KV_HEADS = 4
HEAD_DIM = 128
TOPK = 6
NORM_EPSILON = 1e-05
GROUP = HEADS // KV_HEADS
BF = jnp.bfloat16
F32 = jnp.float32


def matmul(left, right):
    return jnp.dot(left, right, preferred_element_type=F32)


def left_product(left, right):
    return jnp.einsum("sa,sb->ab", left, right, preferred_element_type=F32)


def right_product(left, right):
    return jnp.einsum("sb,ab->sa", left, right, preferred_element_type=F32)


def inverse_rms(hidden):
    return lax.rsqrt(jnp.mean(hidden * hidden, axis=-1, keepdims=True) + NORM_EPSILON)


def norm_back(grad, hidden, inverse, gain):
    scaled = grad * gain
    inner = jnp.mean(scaled * hidden, axis=-1, keepdims=True)
    gain_grad = jnp.sum(grad * (hidden * inverse), axis=0)
    return inverse * scaled - hidden * (inverse * inverse * inverse) * inner, gain_grad


def silu_parts(pre):
    sigmoid = jax.nn.sigmoid(pre)
    return pre * sigmoid, sigmoid * (1.0 + pre * (1.0 - sigmoid))


def stacked(ref):
    return jnp.concatenate(
        [ref[0, :, g * HEAD_DIM : (g + 1) * HEAD_DIM] for g in range(GROUP)], axis=0
    )


def unstacked(ref, value):
    rows = ref.shape[1]
    for g in range(GROUP):
        ref[0, :, g * HEAD_DIM : (g + 1) * HEAD_DIM] = value[g * rows : (g + 1) * rows].astype(
            ref.dtype
        )


def masked_scores(first, query, key, rows):
    scores = lax.dot_general(
        query, key, (((1,), (1,)), ((), ())), preferred_element_type=F32
    ) * (HEAD_DIM**-0.5)
    place = first + lax.rem(lax.broadcasted_iota(jnp.int32, scores.shape, 0), rows)
    seen = lax.broadcasted_iota(jnp.int32, scores.shape, 1) <= place
    return jnp.where(seen, scores, -1e30)


def attend_kernel(first_ref, query_ref, key_ref, value_ref, out_ref):
    rows = query_ref.shape[1]
    length = key_ref.shape[0] * rows
    query = stacked(query_ref)
    key = key_ref[...].reshape(length, HEAD_DIM)
    value = value_ref[...].reshape(length, HEAD_DIM)
    scores = masked_scores(first_ref[0], query, key, rows)
    weights = jnp.exp(scores - jnp.max(scores, axis=-1, keepdims=True))
    probs = (weights / jnp.sum(weights, axis=-1, keepdims=True)).astype(BF)
    unstacked(out_ref, jnp.dot(probs, value, preferred_element_type=F32))


def attend_back_kernel(
    first_ref, query_ref, key_ref, value_ref, grad_ref, query_out, key_out, value_out
):
    rows = query_ref.shape[1]
    length = key_ref.shape[0] * rows
    scale = HEAD_DIM**-0.5
    query, grad = stacked(query_ref), stacked(grad_ref)
    key = key_ref[...].reshape(length, HEAD_DIM)
    value = value_ref[...].reshape(length, HEAD_DIM)
    scores = masked_scores(first_ref[0], query, key, rows)
    weights = jnp.exp(scores - jnp.max(scores, axis=-1, keepdims=True))
    probs = weights / jnp.sum(weights, axis=-1, keepdims=True)
    prob_grad = lax.dot_general(
        grad, value, (((1,), (1,)), ((), ())), preferred_element_type=F32
    )
    delta = jnp.sum(probs * prob_grad, axis=-1, keepdims=True)
    score_grad = (probs * (prob_grad - delta)).astype(BF)
    unstacked(query_out, jnp.dot(score_grad, key, preferred_element_type=F32) * scale)
    down = (((0,), (0,)), ((), ()))
    key_grad = lax.dot_general(score_grad, query, down, preferred_element_type=F32) * scale
    value_grad = lax.dot_general(probs.astype(BF), grad, down, preferred_element_type=F32)
    key_out[...] = key_grad.astype(BF).reshape(key_out.shape)
    value_out[...] = value_grad.astype(BF).reshape(value_out.shape)


def attention_specs(places, rows):
    query = pl.BlockSpec((1, rows, GROUP * HEAD_DIM), lambda m, h: (m, 0, h))
    key = pl.BlockSpec((places, 1, rows, HEAD_DIM), lambda m, h: (0, m, 0, h))
    value = pl.BlockSpec((places, 1, rows, HEAD_DIM), lambda m, h: (0, m, 0, KV_HEADS + h))
    return pl.BlockSpec(memory_space=pltpu.SMEM), query, key, value


def attend(first, qkv, kv_all):
    micro, rows, _ = qkv.shape
    scalar, query, key, value = attention_specs(kv_all.shape[0], rows)
    return pl.pallas_call(
        attend_kernel,
        grid=(micro, KV_HEADS),
        out_shape=jax.ShapeDtypeStruct((micro, rows, HEADS * HEAD_DIM), BF),
        in_specs=[scalar, query, key, value],
        out_specs=query,
        compiler_params=pltpu.CompilerParams(vmem_limit_bytes=40 << 20),
        name="attend",
    )(first, qkv, kv_all, kv_all)


def attend_back(first, qkv, kv_all, grad):
    micro, rows, _ = qkv.shape
    scalar, query, key, value = attention_specs(kv_all.shape[0], rows)
    kv_out = jax.ShapeDtypeStruct((kv_all.shape[0], micro, rows, KV_HEADS * HEAD_DIM), BF)
    return pl.pallas_call(
        attend_back_kernel,
        grid=(micro, KV_HEADS),
        out_shape=[jax.ShapeDtypeStruct((micro, rows, HEADS * HEAD_DIM), BF), kv_out, kv_out],
        in_specs=[scalar, query, key, value, query],
        out_specs=[query, key, key],
        compiler_params=pltpu.CompilerParams(vmem_limit_bytes=56 << 20),
        name="attend_back",
    )(first, qkv, kv_all, kv_all, grad)


def nearest(n, place, k):
    value = jnp.int32(0)
    for i in range(n):
        for j, t in enumerate(sorted(range(n), key=lambda t: (abs(t - i), t))):
            if t:
                value = jnp.where(jnp.logical_and(place == i, k == j), t, value)
    return value


TILE = 1536


def tiles(total, body, size=TILE):
    def step(t, carry):
        body(pl.ds(pl.multiple_of(t * size, size), size))
        return carry

    lax.fori_loop(0, total // size, step, 0)


def dot_tn(left, right):
    return lax.dot_general(left, right, (((0,), (0,)), ((), ())), preferred_element_type=F32)


def dot_nt(left, right):
    return lax.dot_general(left, right, (((1,), (1,)), ((), ())), preferred_element_type=F32)


def expert_kernel(grid, micro, slots, *refs):
    (x_ref, table_ref, top_ref, gate_ref, up_ref, down_ref, in_ref, out_ref) = refs[:8]
    (x_all, table_all, mixed_ref, back_ref, gates_ref, taken_ref, grad_ref, acts_ref, shid_ref, spre_ref) = refs[8:18]
    (w_in, w_down, s_in, s_out, x_buf, d_buf, t_buf, mixed_out, back_out, taken, grad, acts, shid, spre, picked, turned, top_rows, scaled, rows_back) = refs[18:37]
    (ssem, rsem, osem, wsem, lsem, dsem, msem, esem, ssem2) = refs[37:]
    me = grid.here()
    line, place = grid.size["a"], me["a"]
    held, hidden_width, width = w_down.shape
    rows = table_ref.shape[1]
    tokens = micro * rows
    unit_tokens = 2 * tokens
    half_slots = micro * slots
    unit_slots = 2 * half_slots
    shared_part = s_out.shape[0]
    experts = table_ref.shape[0] // (2 * micro)
    first_held = (me["a"] * 2 + me["b"]) * held
    greet(grid, me, "ab")

    moves = [(in_ref, s_in), (out_ref, s_out)]
    for s in range(gate_ref.shape[0]):
        for e in range(held):
            at = pl.ds(s * gate_ref.shape[2], gate_ref.shape[2])
            moves.append((gate_ref.at[s, e], w_in.at[e, at, pl.ds(0, hidden_width)]))
            moves.append((up_ref.at[s, e], w_in.at[e, at, pl.ds(hidden_width, hidden_width)]))
            at = pl.ds(s * down_ref.shape[2], down_ref.shape[2])
            moves.append((down_ref.at[s, e], w_down.at[e, at]))
    fetches = [pltpu.make_async_copy(src, dst, wsem.at[i]) for i, (src, dst) in enumerate(moves)]
    own = me["a"] * 2 + me["b"]
    pairs = ((x_ref, x_all), (table_ref, table_all))
    keeps = [pltpu.make_async_copy(src, dst.at[own], osem.at[i]) for i, (src, dst) in enumerate(pairs)]

    def sends(a, mine=False):
        idx = a * 2 + me["b"]
        made = []
        for i, (src, dst) in enumerate(pairs):
            block = dst.at[idx]
            src = src if mine else block
            for j, (d, step) in enumerate((("a", 1), ("a", -1), ("b", 1))):
                cond = None
                if d == "a":
                    ahead = a <= place if step > 0 else a >= place
                    cond = jnp.logical_and(ahead, grid.valid(me, d, step))
                to = grid.device(grid.move(me, d, step))
                made.append((cond, remote(src, block, ssem.at[i, a, j], rsem.at[i, idx], to)))
        return made

    def arrived(idx):
        for i, (_, dst) in enumerate(pairs):
            block = dst.at[idx]
            to = grid.device(grid.move(me, "b", 1))
            remote(block, block, osem.at[i], rsem.at[i, idx], to).wait_recv()

    for cond, cp in sends(place, True):
        under(cond, cp.start)
    for cp in fetches + keeps:
        cp.start()

    def top_copy(k):
        a = nearest(line, place, k)
        at = lax.rem(k, 2)
        return pltpu.make_async_copy(top_ref.at[pl.ds(a * 2, 2)], d_buf.at[at], dsem.at[at])

    top_copy(0).start()
    gates_ref[...] = jnp.zeros_like(gates_ref)
    for cp in fetches:
        cp.wait()

    def out_copies(a):
        at = pl.ds(a * 2, 2)
        return (
            pltpu.make_async_copy(mixed_out, mixed_ref.at[at], msem.at[0]),
            pltpu.make_async_copy(back_out, back_ref.at[at], msem.at[1]),
            pltpu.make_async_copy(shid, shid_ref.at[a], msem.at[2]),
            pltpu.make_async_copy(spre, spre_ref.at[a], msem.at[3]),
        )

    def row_copies(e, k):
        return (
            pltpu.make_async_copy(taken.at[e], taken_ref.at[e, k], esem.at[e, 0]),
            pltpu.make_async_copy(grad.at[e], grad_ref.at[e, k], esem.at[e, 1]),
            pltpu.make_async_copy(acts.at[e], acts_ref.at[e, k], esem.at[e, 2]),
        )

    def unit(k, carry):
        a = nearest(line, place, k)
        for step in (1, -1):
            far = place - step * (k + 1)
            ok = far >= 0 if step > 0 else far < line

            def relay(far=far):
                arrived(far * 2 + me["b"])
                for cond, cp in sends(far):
                    under(cond, cp.start)

            pl.when(ok)(relay)
        pl.when(k + 1 < line)(lambda: top_copy(k + 1).start())
        arrived(a * 2 + 1 - me["b"])

        def fetch(near, far):
            copies = []
            for j, (b, sources) in enumerate(((me["b"], near), (1 - me["b"], far))):
                for i, (source, buf) in enumerate(zip(sources, (x_buf, t_buf))):
                    copies.append(pltpu.make_async_copy(source, buf.at[b], lsem.at[2 * j + i]))
            for cp in copies:
                cp.start()
            for cp in copies:
                cp.wait()

        other = a * 2 + 1 - me["b"]
        kept = a * 2 + me["b"]
        far = (x_all.at[other], table_all.at[other])
        pl.when(k == 0)(lambda: fetch((x_ref, table_ref), far))
        pl.when(k > 0)(lambda: fetch((x_all.at[kept], table_all.at[kept]), far))
        top_copy(k).wait()

        def leave():
            for cp in out_copies(a):
                cp.wait()

        pl.when(k > 0)(leave)
        x = x_buf.reshape(unit_tokens, width)
        top = d_buf.at[lax.rem(k, 2)].reshape(unit_tokens, width)

        def shared_rows(at):
            pre = jnp.dot(x[at, :], s_in[...], preferred_element_type=F32)
            silu, slope = silu_parts(pre[:, :shared_part])
            pre_up = pre[:, shared_part:]
            shid[at, :] = (silu * pre_up).astype(BF)
            mid_grad = dot_nt(top[at, :], s_out[...])
            spre[at, :shared_part] = (mid_grad * pre_up * slope).astype(BF)
            spre[at, shared_part:] = (mid_grad * silu).astype(BF)

        tiles(unit_tokens, shared_rows, 256)

        def expert(e, carry):
            def settle():
                for cp in row_copies(e, k):
                    cp.wait()

            pl.when(k > 0)(settle)
            gains = []
            for b in range(2):
                slot, gate = [], []
                for m in range(micro):
                    row = m * experts + first_held + e
                    one = t_buf[b, pl.ds(micro * experts + row, 1), :]
                    slot.append(jnp.where(one >= 0, one + m * slots, -1.0))
                    gate.append(t_buf[b, pl.ds(row, 1), :])
                slot = jnp.concatenate(slot, axis=1).astype(jnp.int32)
                named = lax.broadcasted_iota(jnp.int32, (half_slots, tokens), 0) == slot
                ones = named.astype(F32)
                picked[e, b] = ones.astype(BF)
                turned[e, b] = ones.T.astype(BF)
                gains.append(
                    jnp.sum(ones * jnp.concatenate(gate, axis=1), axis=1, keepdims=True)
                )
            gain = jnp.concatenate(gains, axis=0)

            def pick_rows(at):
                for b in range(2):
                    own = pl.ds(b * half_slots, half_slots)
                    of = pl.ds(b * tokens, tokens)
                    pick = picked[e, b]
                    taken[e, own, at] = jnp.dot(pick, x[of, at], preferred_element_type=F32).astype(BF)
                    got = jnp.dot(pick, top[of, at], preferred_element_type=F32)
                    top_rows[own, at] = got.astype(BF)
                    grad[e, own, at] = (gains[b] * got).astype(BF)

            tiles(width, pick_rows)
            pre = jnp.dot(taken[e], w_in[e], preferred_element_type=F32)
            hidden_grad = dot_nt(grad[e], w_down[e])
            silu, slope = silu_parts(pre[:, :hidden_width])
            pre_up = pre[:, hidden_width:]
            acts[e, :, :hidden_width] = (silu * pre_up).astype(BF)
            acts[e, :, hidden_width : 2 * hidden_width] = (hidden_grad * pre_up * slope).astype(BF)
            acts[e, :, 2 * hidden_width :] = (hidden_grad * silu).astype(BF)

            def leave_rows(t, gate_grad):
                at = pl.ds(pl.multiple_of(t * TILE, TILE), TILE)
                hidden = acts[e, :, :hidden_width]
                result = jnp.dot(hidden, w_down[e, :, at], preferred_element_type=F32)
                result = result.astype(BF).astype(F32)
                scaled[e, :, at] = (gain * result).astype(BF)
                product = top_rows[:, at].astype(F32) * result
                for c in range(0, TILE, 128):
                    gate_grad = gate_grad + product[:, c : c + 128]
                rows_back[e, :, at] = dot_nt(acts[e, :, hidden_width:], w_in[e, at, :]).astype(BF)
                return gate_grad

            gate_grad = lax.fori_loop(
                0, width // TILE, leave_rows, jnp.zeros((unit_slots, 128), F32)
            )
            gate_grad = jnp.sum(gate_grad, axis=1, keepdims=True)
            for b in range(2):
                spread = jnp.sum(
                    picked[e, b].astype(F32) * gate_grad[b * half_slots : (b + 1) * half_slots],
                    axis=0,
                    keepdims=True,
                )
                for m in range(micro):
                    row = m * experts + first_held + e
                    gates_ref[a * 2 + b, pl.ds(row, 1), :] = spread[:, m * rows : (m + 1) * rows]
            for cp in row_copies(e, k):
                cp.start()
            return carry

        lax.fori_loop(0, held, expert, 0)

        def combine(at):
            for b in range(2):
                own = pl.ds(b * half_slots, half_slots)
                of = pl.ds(b * tokens, tokens)
                mixed = jnp.dot(shid[of, :], s_out[:, at], preferred_element_type=F32)
                back = dot_nt(spre[of, :], s_in[at, :])
                for e in range(held):
                    turn = turned[e, b]
                    mixed += jnp.dot(turn, scaled[e, own, at], preferred_element_type=F32)
                    back += jnp.dot(turn, rows_back[e, own, at], preferred_element_type=F32)
                mixed_out[b, :, at] = mixed.astype(BF)
                back_out[b, :, at] = back.astype(BF)

        tiles(width, combine)
        for cp in out_copies(a):
            cp.start()
        return carry

    lax.fori_loop(0, line, unit, 0)
    for cp in out_copies(0):
        cp.wait()
    for e in range(held):
        for cp in row_copies(e, 0):
            cp.wait()
    for cp in keeps:
        cp.wait()
    for a in range(line):
        for cond, cp in sends(a):
            under(cond, cp.wait_send)


def run_experts(grid, micro, slots, x, table, tops, w_gate, w_up, w_down, s_in, s_out, collective_id):
    line = grid.size["a"]
    blocks = 2 * line
    tokens, width = x.shape
    seq, held, _, hidden_width = w_gate.shape
    unit_tokens, unit_slots = 2 * tokens, 2 * micro * slots
    shared_part = s_out.shape[0]
    any_spec, vmem = pl.BlockSpec(memory_space=pl.ANY), pl.BlockSpec(memory_space=pltpu.VMEM)
    shape = jax.ShapeDtypeStruct
    dma = pltpu.SemaphoreType.DMA
    return pl.pallas_call(
        functools.partial(expert_kernel, grid, micro, slots),
        out_shape=[
            shape((blocks, tokens, width), BF),
            shape((blocks,) + table.shape, F32),
            shape((blocks, tokens, width), BF),
            shape((blocks, tokens, width), BF),
            shape((blocks, table.shape[0] // 2, table.shape[1]), F32),
            shape((held, line, unit_slots, width), BF),
            shape((held, line, unit_slots, width), BF),
            shape((held, line, unit_slots, 3 * hidden_width), BF),
            shape((line, unit_tokens, shared_part), BF),
            shape((line, unit_tokens, 2 * shared_part), BF),
        ],
        in_specs=[vmem] * 2 + [pl.BlockSpec(memory_space=pltpu.HBM)] * 6,
        out_specs=[any_spec] * 4 + [vmem] + [any_spec] * 5,
        scratch_shapes=[
            pltpu.VMEM((held, width, 2 * hidden_width), BF),
            pltpu.VMEM((held, hidden_width, width), BF),
            pltpu.VMEM(s_in.shape, BF),
            pltpu.VMEM(s_out.shape, BF),
            pltpu.VMEM((2, tokens, width), BF),
            pltpu.VMEM((2, 2, tokens, width), BF),
            pltpu.VMEM((2,) + table.shape, F32),
            pltpu.VMEM((2, tokens, width), BF),
            pltpu.VMEM((2, tokens, width), BF),
            pltpu.VMEM((held, unit_slots, width), BF),
            pltpu.VMEM((held, unit_slots, width), BF),
            pltpu.VMEM((held, unit_slots, 3 * hidden_width), BF),
            pltpu.VMEM((unit_tokens, shared_part), BF),
            pltpu.VMEM((unit_tokens, 2 * shared_part), BF),
            pltpu.VMEM((held, 2, micro * slots, tokens), BF),
            pltpu.VMEM((held, 2, tokens, micro * slots), BF),
            pltpu.VMEM((unit_slots, width), BF),
            pltpu.VMEM((held, unit_slots, width), BF),
            pltpu.VMEM((held, unit_slots, width), BF),
            dma((2, line, 3)),
            dma((2, blocks)),
            dma((2,)),
            dma((3 * held * seq + 2,)),
            dma((4,)),
            dma((2,)),
            dma((4,)),
            dma((held, 3)),
            dma((1,)),
        ],
        compiler_params=pltpu.CompilerParams(
            collective_id=collective_id, has_side_effects=True, vmem_limit_bytes=56 << 20
        ),
        name="experts",
    )(x, table, tops, w_gate, w_up, w_down, s_in, s_out)


def return_kernel(grid, plan, micro, *refs):
    ins, outs, refs = refs[:8], refs[8:16], refs[16:]
    taken_ref, grad_ref, acts_ref = ins[5:]
    taken, grad, acts, fsem = refs[:4]
    me = grid.here()
    plan.bind(me, ins[:5], outs, refs[4:])
    held = taken_ref.shape[0]
    hidden_width = acts.shape[1] // 3

    def loads(e):
        return [
            pltpu.make_async_copy(src.at[e], dst, fsem.at[j])
            for j, (src, dst) in enumerate(((taken_ref, taken), (acts_ref, acts), (grad_ref, grad)))
        ]

    for cp in loads(0):
        cp.start()
    greet(grid, me, "abxc")

    def product(left, first, right, total, acc):
        block = acc.shape[1]
        chunk = math.lcm(block, 128)

        def step(t, carry):
            at = pl.ds(pl.multiple_of(first + t * chunk, 128), chunk)
            value = dot_tn(left[:, at], right).astype(BF)
            for q in range(chunk // block):
                acc[t * (chunk // block) + q] = value[q * block : (q + 1) * block]
            return carry

        lax.fori_loop(0, total // chunk, step, 0)

    def fill(e):
        for cp in loads(e):
            cp.wait()
        product(taken, 0, acts[:, hidden_width:], taken.shape[1], plan.accs[9 + 2 * e])
        product(acts, 0, grad[...], hidden_width, plan.accs[10 + 2 * e])
        if e + 1 < held:
            for cp in loads(e + 1):
                cp.start()

    plan.run([(0.04 + 1.05 * e, functools.partial(fill, e)) for e in range(held)])


def return_tokens(grid, micro, mixed, back, gates, shared_in, shared_out, taken, grad, acts, collective_id):
    held, _, width = taken.shape
    hidden_width = acts.shape[2] // 3
    seq = grid.size["x"] * 2
    rows = mixed.shape[1]
    cuts = [0] + [16 * (rows * n // 8 // 16) for n in (1, 3, 5)] + [rows]
    parts = []
    for k in (1, 2, 3, 0):
        for i, x in enumerate((mixed, back)):
            way = ("ba", "ba") if k else ("ab", "ab")
            size, whole = cuts[k + 1] - cuts[k], [(i, None, 0, x.shape[2])]
            parts.append(Part(way, x.shape[0], size, x.shape[2], BF, i, whole, row=cuts[k]))
    parts.append(Part(("ba", "ba"), *gates.shape, F32, 2, [(2, None, 0, gates.shape[2])]))
    for e in range(held):
        ready = (0.041 + 1.05 * e, 0.06 + 1.05 * e, 0.07 + 1.05 * e, 2.6 + 2 * e)
        rows = width // seq
        ways = [(5, e, 0, hidden_width), (6, e, hidden_width, hidden_width)]
        parts.append(Part(("cx", "cx"), seq, rows, 2 * hidden_width, BF, None, ways, ready=ready))
        rows = hidden_width // seq
        parts.append(Part(("cx", "cx"), seq, rows, width, BF, None, [(7, e, 0, width)], ready=ready))
    for i, x in enumerate((shared_in, shared_out)):
        parts.append(
            Part(("cx", "cx"), seq, x.shape[1], x.shape[2], BF, 3 + i, [(3 + i, None, 0, x.shape[2])])
        )
    plan = Scatter(grid, parts)
    shape = jax.ShapeDtypeStruct
    dma = pltpu.SemaphoreType.DMA
    return pl.pallas_call(
        functools.partial(return_kernel, grid, plan, micro),
        out_shape=[
            shape(mixed.shape[1:], F32),
            shape(back.shape[1:], F32),
            shape(gates.shape[1:], F32),
            shape(shared_in.shape[1:], BF),
            shape(shared_out.shape[1:], F32),
            shape((held, width // seq, hidden_width), F32),
            shape((held, width // seq, hidden_width), F32),
            shape((held, hidden_width // seq, width), F32),
        ],
        in_specs=[pl.BlockSpec(memory_space=pl.ANY)] * 8,
        out_specs=[pl.BlockSpec(memory_space=pltpu.VMEM)] * 8,
        scratch_shapes=[
            pltpu.VMEM(taken.shape[1:], BF),
            pltpu.VMEM(grad.shape[1:], BF),
            pltpu.VMEM(acts.shape[1:], BF),
            dma((3,)),
        ]
        + plan.scratch(),
        compiler_params=pltpu.CompilerParams(
            collective_id=collective_id, has_side_effects=True, vmem_limit_bytes=62 << 20
        ),
        name="return_tokens",
    )(mixed, back, gates, shared_in, shared_out, taken, grad, acts)


def per_device(
    block_input,
    norm_attn,
    w_query,
    w_key,
    w_value,
    w_out,
    norm_ffn,
    w_router,
    shared_gate,
    shared_up,
    shared_down,
    expert_gate,
    expert_up,
    expert_down,
    routes,
    out_grad,
):
    micro, _, rows, width = block_input.shape
    tokens = micro * rows
    experts = w_router.shape[1]
    held = expert_gate.shape[0]
    exp_size, seq_size = lax.axis_size("exp"), lax.axis_size("seq")
    blocks = exp_size * seq_size
    grid = Grid(exp_size, seq_size)
    slots = min(rows, 8 * ((3 * rows * TOPK // (2 * experts) + 7) // 8))
    query_width = HEADS * HEAD_DIM
    kv_width = KV_HEADS * HEAD_DIM
    qkv_width = query_width + 2 * kv_width
    own_rows = w_query.shape[0]
    shared_part = shared_gate.shape[1] // exp_size
    first = (lax.axis_index("seq") * rows).astype(jnp.int32).reshape(1)

    small = jnp.concatenate([norm_attn[:, None], norm_ffn[:, None], w_router], axis=1)
    small = jnp.pad(small, ((0, 0), (0, 128 - small.shape[1])))
    halves = jnp.concatenate(
        [
            shared_gate.reshape(own_rows, exp_size, shared_part),
            shared_up.reshape(own_rows, exp_size, shared_part),
        ],
        axis=2,
    ).transpose(1, 0, 2)
    route = ("abxc", "axbc" if seq_size == 4 else "abxc")
    along, across = ("ab", "ab"), ("xc", "xc")
    turned = 16 * (tokens * 3 // 8 // 16)
    (qkv_full, out_full, small_full, grads_all, shared_out, shared_in, gate_all, up_all, down_all) = gather(
        grid,
        [
            jnp.concatenate([w_query, w_key, w_value], axis=1),
            w_out,
            small,
            out_grad.reshape(tokens, width),
            shared_down,
            halves,
            expert_gate,
            expert_up,
            expert_down,
        ],
        [Item(i, route) for i in range(3)]
        + [
            Item(3, along, (turned, tokens - turned)),
            Item(3, ("ba", "ba"), (0, turned)),
            Item(4, across),
            Item(5, across, spread=True),
        ]
        + [Item(i, across, late=10 - start, start=start) for i, start in ((6, 0), (7, 1.2), (8, 2.2))],
        1,
        "gather_first",
    )
    shared_out = shared_out.reshape(shared_part, width)
    shared_in = shared_in.reshape(width, 2 * shared_part)
    qkv_full = qkv_full.reshape(width, qkv_width)
    out_full = out_full.reshape(query_width, width)
    small_full = small_full.reshape(width, 128)
    gain_one = small_full[:, 0].astype(F32)
    gain_two = small_full[:, 1].astype(F32)
    router_full = small_full[:, 2 : 2 + experts]

    hidden_in = block_input.reshape(tokens, width).astype(F32)
    inverse_one = inverse_rms(hidden_in)
    normed_one = (hidden_in * inverse_one * gain_one).astype(BF)
    qkv = matmul(normed_one, qkv_full).astype(BF)
    (kv_all,) = gather(grid, [qkv[:, query_width:]], [Item(0, across)], 2, "gather_kv")
    kv_all = kv_all.reshape(seq_size, micro, rows, 2 * kv_width)
    qkv = qkv.reshape(micro, rows, qkv_width)
    attended = attend(first, qkv, kv_all).reshape(tokens, query_width)
    hidden_mid = hidden_in + matmul(attended, out_full)
    inverse_two = inverse_rms(hidden_mid)
    normed_two = (hidden_mid * inverse_two * gain_two).astype(BF)

    route_rows = routes.reshape(tokens, TOPK)
    named = route_rows[:, :, None] == jnp.arange(experts, dtype=jnp.int32)
    chosen = jnp.any(named, axis=1)
    logits = matmul(normed_two, router_full)
    masked = jnp.where(chosen, logits, -jnp.inf)
    powers = jnp.exp(masked - jnp.max(masked, axis=-1, keepdims=True))
    gates = powers / jnp.sum(powers, axis=-1, keepdims=True)
    member = chosen.reshape(micro, rows, experts).astype(jnp.int32)
    rank = jnp.cumsum(member, axis=1) - member
    slot = jnp.where(member > 0, rank, -1).astype(F32)

    def by_expert(table):
        return table.reshape(micro, rows, experts).transpose(0, 2, 1).reshape(micro * experts, rows)

    table = jnp.concatenate([by_expert(gates), by_expert(slot)], axis=0)
    inputs_all, _, mixed, back, gate_table, taken, taken_grad, acts, shared_hidden, shared_pre = run_experts(
        grid, micro, slots, normed_two, table, grads_all, gate_all, up_all, down_all, shared_in, shared_out, 3
    )
    flat = inputs_all.reshape(exp_size * tokens, width)
    flat_top = grads_all.reshape(exp_size * tokens, width)
    shared_in_term = left_product(flat, shared_pre.reshape(-1, 2 * shared_part)).astype(BF)
    shared_out_term = left_product(shared_hidden.reshape(-1, shared_part), flat_top).astype(BF)
    hidden_width = expert_gate.shape[2]
    taken = taken.reshape(held, -1, width)
    taken_grad = taken_grad.reshape(held, -1, width)
    acts = acts.reshape(held, -1, 3 * hidden_width)
    shared_in_term = shared_in_term.reshape(exp_size, seq_size, own_rows, 2 * shared_part)
    (
        mixture,
        token_grad,
        gate_grad,
        halves,
        shared_down_grad,
        expert_gate_grad,
        expert_up_grad,
        expert_down_grad,
    ) = return_tokens(
        grid,
        micro,
        mixed,
        back,
        gate_table,
        shared_in_term.transpose(1, 0, 2, 3).reshape(seq_size, exp_size * own_rows, 2 * shared_part),
        shared_out_term.reshape(seq_size, shared_part // seq_size, width),
        taken,
        taken_grad,
        acts,
        4,
    )
    halves = halves.reshape(exp_size, own_rows, 2 * shared_part)

    block_output = (hidden_mid + mixture).astype(BF).reshape(block_input.shape)

    gate_grad = gate_grad.reshape(micro, experts, rows).transpose(0, 2, 1).reshape(tokens, experts)
    logit_grad = gates * (gate_grad - jnp.sum(gates * gate_grad, axis=-1, keepdims=True))
    logit_grad = logit_grad.astype(BF)
    grad_top = out_grad.reshape(tokens, width).astype(F32)
    normed_two_grad = token_grad + right_product(logit_grad, router_full)
    mid_part, norm_two_term = norm_back(normed_two_grad, hidden_mid, inverse_two, gain_two)
    mid_grad = mid_part + grad_top
    attn_grad = mid_grad.astype(BF)
    attended_grad = right_product(attn_grad, out_full).astype(BF)
    query_grad, key_part, value_part = attend_back(
        first, qkv, kv_all, attended_grad.reshape(micro, rows, query_width)
    )
    key_grad, value_grad = scatter(
        grid,
        [
            key_part.reshape(seq_size, tokens, kv_width),
            value_part.reshape(seq_size, tokens, kv_width),
        ],
        [("cx", "cx")] * 2,
        [BF] * 2,
        5,
        "scatter_kv",
    )
    qkv_grad = jnp.concatenate(
        [query_grad.reshape(tokens, query_width), key_grad, value_grad], axis=1
    )
    halves, qkv_grad = lax.optimization_barrier((halves, qkv_grad))
    halves = lax.all_to_all(halves, "exp", split_axis=0, concat_axis=0, tiled=True).astype(F32)
    halves = halves.transpose(1, 0, 2)
    shared_gate_grad = halves[:, :, :shared_part].reshape(own_rows, exp_size * shared_part)
    shared_up_grad = halves[:, :, shared_part:].reshape(own_rows, exp_size * shared_part)
    normed_one_grad = right_product(qkv_grad, qkv_full)
    in_part, norm_one_term = norm_back(normed_one_grad, hidden_in, inverse_one, gain_one)
    input_grad = (in_part + mid_grad).reshape(block_input.shape)
    small_term = jnp.concatenate(
        [norm_one_term[:, None], norm_two_term[:, None], left_product(normed_two, logit_grad)],
        axis=1,
    )
    small_term = jnp.pad(small_term, ((0, 0), (0, 128 - small_term.shape[1])))
    order = ("cxba", "cbxa" if seq_size == 4 else "cxba")
    qkv_share, out_share, small_share = scatter(
        grid,
        [
            left_product(normed_one, qkv_grad).astype(BF).reshape(blocks, own_rows, qkv_width),
            left_product(attended, attn_grad).astype(BF).reshape(blocks, own_rows, width),
            small_term.reshape(blocks, own_rows, 128),
        ],
        [order] * 3,
        [F32] * 3,
        6,
        "scatter_dense",
    )
    return (
        block_output,
        input_grad,
        small_share[:, 0],
        qkv_share[:, :query_width],
        qkv_share[:, query_width : query_width + kv_width],
        qkv_share[:, query_width + kv_width :],
        out_share,
        small_share[:, 1],
        small_share[:, 2 : 2 + experts],
        shared_gate_grad,
        shared_up_grad,
        shared_down_grad,
        expert_gate_grad,
        expert_up_grad,
        expert_down_grad,
    )


def solution(mesh):
    tokens = P(None, "exp", "seq", None)
    vector, matrix = P(("exp", "seq")), P(("exp", "seq"), None)
    stack = P("exp", "seq", None)
    weights = (vector,) + (matrix,) * 4 + (vector,) + (matrix,) * 4 + (stack,) * 3
    return jax.shard_map(
        per_device,
        mesh=mesh,
        in_specs=(tokens,) + weights + (tokens, tokens),
        out_specs=(tokens, tokens) + weights,
        check_vma=False,
    )
```
